32 devices in a mesh: dp: 4 (over x, core), seq: 8 (over z, y).
Axes of the slice: x: 2, y: 2, z: 4, core: 2. Of those that a mesh axis runs over, the one named last changes fastest.
Arguments:
- tokens: bfloat16 [24, 2048, 512], P('dp', 'seq'), may hold values from -6 to 6
- document_starts: int32 [24, 16], P('dp'), may hold values from 0 to 2047, as said below
- attention_in: bfloat16 [512, 1536], replicated, may hold values from -0.375 to 0.375
- attention_out: bfloat16 [512, 512], replicated, may hold values from -1 to 1
- feedforward_in: bfloat16 [512, 1536], replicated, may hold values from -0.25 to 0.25
- feedforward_out: bfloat16 [768, 512], replicated, may hold values from -0.21875 to 0.21875
- gain_first: float32 [512], replicated, may hold values from 0.1 to 1.9
- gain_second: float32 [512], replicated, may hold values from 0.1 to 1.9
- result_grad: bfloat16 [24, 2048, 512], P('dp', 'seq'), may hold values from -6 to 6
Outputs:
- activations: bfloat16 [24, 2048, 512], P('dp', 'seq')
- grad_tokens: float32 [24, 2048, 512], P('dp', 'seq')
- grad_attention_in: float32 [512, 1536], replicated
- grad_attention_out: float32 [512, 512], replicated
- grad_feedforward_in: float32 [512, 1536], replicated
- grad_feedforward_out: float32 [768, 512], replicated
- grad_gain_first: float32 [512], replicated
- grad_gain_second: float32 [512], replicated
The draws below stay inside these ranges and needn't reach their ends.
Inputs may be any that keep to these rules, and one draw needn't show every extreme that they name: `document_starts`: in each row the 16 document starts rise strictly from 0.
All inputs are finite; a program needn't handle non-finite values.
Results may differ from the reference program's by a relative error of at most 0.014.
The reference program's roundings to bfloat16 on the way count: a program that leaves them out, or rounds other values in their place, can miss the bound.
Values may be sent and summed in bfloat16 or wider, within the bound.
No kernel may reach another device: no remote copies, remote signals or barrier semaphores. Data moves between devices by JAX's collectives and lax.ppermute only.
A program may use at most 192 MiB of HBM per device.

```python
import jax
import jax.numpy as jnp
from jax import lax

D = 512
HEADS = 8
HEAD_DIM = 64
FF = 768
HALF_WIN = 64
TOK_DEV = 256
MICRO = 6
NDOC = 16
SEQ_LEN = 2048
ROWS = 24


def draw_document_starts(key, part):
    key = jax.random.fold_in(key, 7)
    pick_key = jax.random.fold_in(key, 1)
    cut_key = jax.random.fold_in(key, 2)
    row_ids = jnp.arange(ROWS, dtype=jnp.int32)
    chosen = jax.random.randint(pick_key, (ROWS // MICRO,), 0, MICRO)
    spanning = row_ids % MICRO == chosen[row_ids // MICRO]
    half_len = TOK_DEV // 2
    front_count = NDOC // 2
    back_count = NDOC - 1 - front_count

    def one_row(row_key):
        key_spread = jax.random.fold_in(row_key, 1)
        key_front = jax.random.fold_in(row_key, 2)
        key_back = jax.random.fold_in(row_key, 3)
        spread_cuts = jnp.sort(jax.random.permutation(key_spread, SEQ_LEN - 1)[:NDOC - 1] + 1)
        front_cuts = jax.random.permutation(key_front, half_len)[:front_count] + 1
        back_offsets = jnp.concatenate([jnp.zeros((1,), jnp.int32), jax.random.permutation(key_back, half_len - 1)[:back_count - 1].astype(jnp.int32) + 1])
        back_cuts = SEQ_LEN - 1 - back_offsets
        edge_cuts = jnp.sort(jnp.concatenate([front_cuts.astype(jnp.int32), back_cuts.astype(jnp.int32)]))
        return (spread_cuts.astype(jnp.int32), edge_cuts)
    spread_all, edge_all = jax.vmap(one_row)(jax.random.split(cut_key, ROWS))
    cuts = jnp.where(spanning[:, None], edge_all, spread_all)
    return jnp.concatenate([jnp.zeros((ROWS, 1), jnp.int32), cuts.astype(jnp.int32)], axis=1)


def level_of(rng, extent, shards, low, top_value):
    loudness, own = 1.0, jax.random.fold_in(rng, 6)
    for axis_at, blocks in shards:
        heights = jnp.exp(jax.random.uniform(jax.random.fold_in(own, axis_at), (blocks,), jnp.float32, low / len(shards), top_value / len(shards)))
        loudness = loudness * jnp.repeat(heights, extent[axis_at] // blocks).reshape([-1 if axis == axis_at else 1 for axis in range(len(extent))])
    return loudness


def gaussian(own_key, dims, deviation, most, shards=(), kind=jnp.bfloat16):
    array = jax.random.normal(own_key, dims, jnp.float32) * deviation
    if len(shards) > 0:
        array = level_of(own_key, dims, shards, -0.22, 0.18) * array
    return jnp.clip(array, min=-most, max=most).astype(kind)


def setup_inputs(seed: int = 0) -> dict:
    keys = jax.random.split(jax.random.key(seed), 10)
    tokens = gaussian(keys[0], (ROWS, SEQ_LEN, D), 1.0, 6.0, ((0, 4), (1, 8)))
    document_starts = draw_document_starts(jax.random.fold_in(keys[9], 71), 0)
    attention_in = gaussian(keys[2], (D, 3 * D), (D // 2) ** -0.5, 0.375)
    attention_out = gaussian(keys[3], (D, D), (D // 16) ** -0.5, 1.0)
    feedforward_in = gaussian(keys[4], (D, 2 * FF), D ** -0.5, 0.25)
    feedforward_out = gaussian(keys[5], (FF, D), FF ** -0.5, 0.21875)
    gain_first = jnp.clip(1.0 + 0.18 * jax.random.normal(keys[6], (D,), jnp.float32), 0.1, 1.9)
    gain_second = jnp.clip(1.0 + 0.18 * jax.random.normal(keys[7], (D,), jnp.float32), 0.1, 1.9)
    result_grad = gaussian(keys[8], (ROWS, SEQ_LEN, D), 1.0, 6.0, ((0, 4), (1, 8)))
    return dict(tokens=tokens, document_starts=document_starts, attention_in=attention_in, attention_out=attention_out, feedforward_in=feedforward_in, feedforward_out=feedforward_out, gain_first=gain_first, gain_second=gain_second, result_grad=result_grad)


EPSILON = 1e-05
ROTARY_BASE = 10000.0
PRECISE = lax.Precision.HIGHEST

@jax.custom_vjp
def low(v):
    return lax.optimization_barrier(v.astype(jnp.bfloat16)).astype(jnp.float32)

@jax.custom_vjp
def low_back(v):
    return v

def low_keep(v):
    return (low(v), None)

def low_pass(kept, grad):
    return (grad,)

def back_keep(v):
    return (v, None)

def back_low(kept, grad):
    return (low(grad),)
low.defvjp(low_keep, low_pass)
low_back.defvjp(back_keep, back_low)

def norm_rows(values, scaling):
    center = lax.optimization_barrier(jnp.mean(values, axis=-1, keepdims=True))
    shifted = values - center
    spread = lax.optimization_barrier(jnp.mean(shifted * shifted, axis=-1, keepdims=True))
    return shifted * lax.rsqrt(spread + EPSILON) * scaling

def rotary_tables(positions):
    inverse = ROTARY_BASE ** (-(jnp.arange(0, HEAD_DIM, 2).astype(jnp.float32) / HEAD_DIM))
    angles = positions.astype(jnp.float32)[:, None] * inverse[None, :]
    angles = jnp.concatenate([angles, angles], axis=-1)
    return (jnp.cos(angles), jnp.sin(angles))

def rotate(values, cosine, sines):
    middle_col = values.shape[-1] // 2
    turned = jnp.concatenate([-values[..., middle_col:], values[..., :middle_col]], axis=-1)
    return values * cosine[:, None, :] + turned * sines[:, None, :]

def row_forward(row_tokens, row_starts, weight_one, weight_two, weight_three, weight_four, gain_one, gain_two):
    positions = jnp.arange(SEQ_LEN, dtype=jnp.int32)
    row_docs = lax.optimization_barrier(jnp.sum((row_starts[None, :] <= positions[:, None]).astype(jnp.int32), axis=1)) - 1
    normed_one = low(norm_rows(row_tokens, gain_one))
    projected = low_back(jnp.dot(normed_one, weight_one, precision=PRECISE))
    cosine, sines = rotary_tables(positions)
    queries = low(rotate(projected[:, :D].reshape(SEQ_LEN, HEADS, HEAD_DIM), cosine, sines))
    rotated_keys = low(rotate(projected[:, D:2 * D].reshape(SEQ_LEN, HEADS, HEAD_DIM), cosine, sines))
    values = low(projected[:, 2 * D:].reshape(SEQ_LEN, HEADS, HEAD_DIM))
    pad_widths = ((HALF_WIN, HALF_WIN), (0, 0), (0, 0))
    wide_keys = jnp.pad(rotated_keys, pad_widths)
    wide_values = jnp.pad(values, pad_widths)
    wide_docs = jnp.pad(row_docs, HALF_WIN, constant_values=-1)
    block_rows = 512 if SEQ_LEN % 512 == 0 else SEQ_LEN
    span_rows = block_rows + 2 * HALF_WIN
    distance = jnp.arange(block_rows)[:, None] + HALF_WIN - jnp.arange(span_rows)[None, :]
    near_mask = jnp.abs(distance) <= HALF_WIN
    score_scale = HEAD_DIM ** (-0.5)

    def attend(block_index):
        first_row = (block_index * block_rows).astype(jnp.int32)
        block_queries = lax.dynamic_slice_in_dim(queries, first_row, block_rows, 0)
        block_keys = lax.dynamic_slice_in_dim(wide_keys, first_row, span_rows, 0)
        block_values = lax.dynamic_slice_in_dim(wide_values, first_row, span_rows, 0)
        query_docs = lax.dynamic_slice_in_dim(row_docs, first_row, block_rows, 0)
        key_docs = lax.dynamic_slice_in_dim(wide_docs, first_row, span_rows, 0)
        allowed = near_mask & (query_docs[:, None] == key_docs[None, :])
        scores = low_back(jnp.einsum('qhd,khd->hqk', block_queries, block_keys, precision=PRECISE) * score_scale)
        scores = jnp.where(allowed[None], scores, -jnp.inf)
        row_max = lax.optimization_barrier(jnp.max(scores, axis=-1, keepdims=True))
        weights = jnp.exp(scores - row_max)
        probabilities = low(weights / lax.optimization_barrier(jnp.sum(weights, axis=-1, keepdims=True)))
        return jnp.einsum('hqk,khd->qhd', probabilities, block_values, precision=PRECISE)
    attended = lax.map(jax.checkpoint(attend), jnp.arange(SEQ_LEN // block_rows, dtype=jnp.int32))
    attended = low(low_back(attended.reshape(SEQ_LEN, D)))
    middle = row_tokens + low_back(jnp.dot(attended, weight_two, precision=PRECISE))
    normed_two = low(norm_rows(middle, gain_two))
    gate_up = low_back(jnp.dot(normed_two, weight_three, precision=PRECISE))
    mixed = low(jax.nn.gelu(gate_up[:, :FF], approximate=False) * gate_up[:, FF:])
    return middle + jnp.dot(mixed, weight_four, precision=PRECISE)

def reference(tokens, document_starts, attention_in, attention_out, feedforward_in, feedforward_out, gain_first, gain_second, result_grad):

    def forward(token_values, weight_one, weight_two, weight_three, weight_four, gain_one, gain_two):

        def one_row(row_pair):
            return row_forward(row_pair[0], row_pair[1], weight_one, weight_two, weight_three, weight_four, gain_one, gain_two)
        return lax.map(jax.checkpoint(one_row), (token_values, document_starts))
    result, pullback = jax.vjp(forward, tokens.astype(jnp.float32), attention_in.astype(jnp.float32), attention_out.astype(jnp.float32), feedforward_in.astype(jnp.float32), feedforward_out.astype(jnp.float32), gain_first.astype(jnp.float32), gain_second.astype(jnp.float32))
    gradients = pullback(result_grad.astype(jnp.float32))
    return (result.astype(jnp.bfloat16), gradients[0], gradients[1], gradients[2], gradients[3], gradients[4], gradients[5], gradients[6])
```

```python
import functools

import jax
import jax.numpy as jnp
from jax import lax
from jax.experimental import pallas as pl
from jax.experimental.pallas import tpu as pltpu
from jax.sharding import PartitionSpec as P

HEADS = 8
HEAD_DIM = 64
HALF_WIN = 64
EPSILON = 1e-05
ROTARY_BASE = 10000.0
SCALE = HEAD_DIM**-0.5
BLOCKS = 32
GROUP = 4
WIDE = GROUP * HEAD_DIM
VMEM = 56 * 1024 * 1024

F32 = jnp.float32
BF16 = jnp.bfloat16


def dot(a, b, contract):
    return lax.dot_general(a, b, ((contract[:1], contract[1:]), ((), ())), preferred_element_type=F32)


def nn(a, b):
    return dot(a, b, (1, 0))


def nt(a, b):
    return dot(a, b, (1, 1))


def tn(a, b):
    return dot(a, b, (0, 0))


def normalize(values):
    shifted = values - jnp.mean(values, axis=-1, keepdims=True)
    inverse = lax.rsqrt(jnp.mean(shifted * shifted, axis=-1, keepdims=True) + EPSILON)
    return shifted * inverse, inverse


def norm_back(scaled_grad, unit, inverse):
    return (
        scaled_grad
        - jnp.mean(scaled_grad, axis=-1, keepdims=True)
        - unit * jnp.mean(scaled_grad * unit, axis=-1, keepdims=True)
    ) * inverse


def half_swap(values):
    lane = lax.broadcasted_iota(jnp.int32, values.shape, 1)
    return jnp.where(lane % HEAD_DIM < HEAD_DIM // 2, pltpu.roll(values, 96, 1), pltpu.roll(values, 32, 1))


def rotate(values, cosine, sines):
    parts = [values[:, c : c + 128] for c in range(0, values.shape[1], 128)]
    return jnp.concatenate([p * cosine + half_swap(p) * sines for p in parts], axis=1)


def rotate_back(values, cosine, sines):
    parts = [values[:, c : c + 128] for c in range(0, values.shape[1], 128)]
    return jnp.concatenate([p * cosine - half_swap(p) * sines for p in parts], axis=1)


def doc_ids(starts_ref, row, positions):
    total = jnp.zeros(positions.shape, jnp.int32)
    for j in range(starts_ref.shape[1]):
        total += (positions >= starts_ref[row, j]).astype(jnp.int32)
    return total


def mask_bias(starts_ref, row, first_query, queries, first_key, keys, row_len, turned):
    q_dim, shape = (1, (keys, queries)) if turned else (0, (queries, keys))
    q_shape = (1, queries) if turned else (queries, 1)
    k_shape = (keys, 1) if turned else (1, keys)
    q_pos = first_query + lax.broadcasted_iota(jnp.int32, q_shape, q_dim)
    k_pos = first_key + lax.broadcasted_iota(jnp.int32, k_shape, 1 - q_dim)
    q_doc = doc_ids(starts_ref, row, q_pos)
    k_doc = jnp.where(k_pos < row_len, doc_ids(starts_ref, row, k_pos), -1)
    distance = (
        lax.broadcasted_iota(jnp.int32, shape, q_dim)
        - lax.broadcasted_iota(jnp.int32, shape, 1 - q_dim)
        + (first_query - first_key)
    )
    allowed = (jnp.abs(distance) <= HALF_WIN) & (q_doc == k_doc)
    return jnp.where(allowed, 0.0, -jnp.inf)


def by_head(values):
    head = lax.broadcasted_iota(jnp.int32, values.shape, 1) // HEAD_DIM
    zero = jnp.zeros_like(values)
    return jnp.concatenate([jnp.where(head == h, values, zero) for h in range(GROUP)], axis=0)


def pick_heads(stacked, count):
    head = lax.broadcasted_iota(jnp.int32, (count, stacked.shape[1]), 1) // HEAD_DIM
    out = stacked[:count]
    for h in range(1, GROUP):
        out = jnp.where(head == h, stacked[h * count : (h + 1) * count], out)
    return out


def attend(queries, keys, values, bias):
    count = queries.shape[0]
    outs = []
    for c in range(0, queries.shape[1], WIDE):
        scores = nt(by_head(queries[:, c : c + WIDE]), keys[:, c : c + WIDE])
        probs = []
        for h in range(GROUP):
            part = scores[h * count : (h + 1) * count] + bias
            part = jnp.exp(part - jnp.max(part, axis=-1, keepdims=True))
            probs.append((part * (1.0 / jnp.sum(part, axis=-1, keepdims=True))).astype(BF16))
        outs.append(pick_heads(nn(jnp.concatenate(probs, axis=0), values[:, c : c + WIDE]), count))
    return jnp.concatenate(outs, axis=1).astype(BF16)


def gelu_parts(gate):
    bell = jnp.exp(-0.5 * gate * gate)
    t = 1.0 / (1.0 + (0.3275911 * 0.7071067811865476) * jnp.abs(gate))
    tail = t * (
        0.5 * 0.254829592
        + t * (0.5 * -0.284496736 + t * (0.5 * 1.421413741 + t * (0.5 * -1.453152027 + t * (0.5 * 1.061405429))))
    )
    tail = tail * bell
    return jnp.where(gate < 0, tail, 1.0 - tail), gate * bell * 0.3989422804014327


def dense_chain(inputs, attended, top, out_ref, up_ref, down_ref, gain_two, sums):
    sum_up, sum_down, sum_out = sums
    hidden = down_ref.shape[0]
    middle = inputs + nn(attended, out_ref[...])
    unit, inverse = normalize(middle)
    normed = (unit * gain_two).astype(BF16)
    result = middle
    grad_normed = None
    for c in range(0, hidden, 256):
        gate = nn(normed, up_ref[:, c : c + 256])
        lift = nn(normed, up_ref[:, hidden + c : hidden + c + 256])
        grad_mixed = nt(top, down_ref[c : c + 256])
        phi, slope = gelu_parts(gate)
        active = gate * phi
        mixed = (active * lift).astype(BF16)
        grad_gate = (grad_mixed * lift * (phi + slope)).astype(BF16)
        grad_lift = (grad_mixed * active).astype(BF16)
        result = result + nn(mixed, down_ref[c : c + 256])
        part = nt(grad_gate, up_ref[:, c : c + 256]) + nt(grad_lift, up_ref[:, hidden + c : hidden + c + 256])
        grad_normed = part if grad_normed is None else grad_normed + part
        sum_down[c : c + 256] += tn(mixed, top)
        sum_up[:, c : c + 256] += tn(normed, grad_gate)
        sum_up[:, hidden + c : hidden + c + 256] += tn(normed, grad_lift)
    grad_middle = top.astype(F32) + norm_back(grad_normed * gain_two, unit, inverse)
    branch = grad_middle.astype(BF16)
    sum_out[...] += tn(attended, branch)
    return result.astype(BF16), grad_middle, nt(branch, out_ref[...]).astype(BF16)


def first_kernel(
    own_len,
    place_ref,
    starts_ref,
    tokens_ref,
    top_ref,
    in_ref,
    out_ref,
    up_ref,
    down_ref,
    gains_ref,
    cos_ref,
    sin_ref,
    normed_ref,
    queries_ref,
    keys_ref,
    values_ref,
    result_ref,
    grad_middle_ref,
    grad_attended_ref,
    sum_up,
    sum_down,
    sum_out,
):
    step = pl.program_id(0)
    pair, _, width = tokens_ref.shape
    lo, hi = HALF_WIN, own_len - HALF_WIN

    @pl.when(step == 0)
    def _():
        for ref in (sum_up, sum_down, sum_out):
            ref[...] = jnp.zeros_like(ref)

    cosine, sines = cos_ref[...], sin_ref[...]
    attended, inputs, tops = [], [], []
    for r in range(pair):
        row_inputs = tokens_ref[r].astype(F32)
        unit, _ = normalize(row_inputs)
        normed = (unit * gains_ref[0:1]).astype(BF16)
        normed_ref[r] = normed
        queries = (rotate(nn(normed, in_ref[:, :width]), cosine, sines) * SCALE).astype(BF16)
        keys = rotate(nn(normed, in_ref[:, width : 2 * width]), cosine, sines).astype(BF16)
        values = nn(normed, in_ref[:, 2 * width :]).astype(BF16)
        queries_ref[r] = queries
        keys_ref[r] = keys
        values_ref[r] = values
        bias = mask_bias(
            starts_ref, step * pair + r, place_ref[0] + lo, hi - lo, place_ref[0], own_len, place_ref[1], False
        )
        attended.append(attend(queries[lo:hi], keys, values, bias))
        inputs.append(row_inputs[lo:hi])
        tops.append(top_ref[r, lo:hi])
    result, grad_middle, grad_attended = dense_chain(
        jnp.concatenate(inputs, axis=0),
        jnp.concatenate(attended, axis=0),
        jnp.concatenate(tops, axis=0),
        out_ref,
        up_ref,
        down_ref,
        gains_ref[1:2],
        (sum_up, sum_down, sum_out),
    )
    shape = (pair, hi - lo, width)
    result_ref[...] = result.reshape(shape)
    grad_middle_ref[...] = grad_middle.reshape(shape)
    grad_attended_ref[...] = grad_attended.reshape(shape)


def second_kernel(
    own_len,
    place_ref,
    starts_ref,
    tokens_ref,
    low_ref,
    high_ref,
    top_ref,
    queries_ref,
    keys_ref,
    values_ref,
    in_ref,
    out_ref,
    up_ref,
    down_ref,
    gains_ref,
    cos_ref,
    sin_ref,
    begun_up,
    begun_down,
    begun_out,
    normed_ref,
    halo_keys_ref,
    halo_values_ref,
    result_ref,
    grad_middle_ref,
    grad_attended_ref,
    keep_ref,
    send_ref,
    sum_up,
    sum_down,
    sum_out,
):
    step = pl.program_id(0)
    pair, _, width = tokens_ref.shape
    win = HALF_WIN
    hidden = down_ref.shape[0]

    @pl.when(step == 0)
    def _():
        sum_up[...] = begun_up[...]
        sum_down[...] = begun_down[...]
        sum_out[...] = begun_out[...]

    cosine, sines = cos_ref[...], sin_ref[...]
    attended, inputs, tops = [], [], []
    for r in range(pair):
        unit, _ = normalize(jnp.concatenate([low_ref[r], high_ref[r]], axis=0).astype(F32))
        normed = (unit * gains_ref[0:1]).astype(BF16)
        keys = rotate(nn(normed, in_ref[:, width : 2 * width]), cosine, sines).astype(BF16)
        values = nn(normed, in_ref[:, 2 * width :]).astype(BF16)
        for side in range(2):
            part = slice(side * win, (side + 1) * win)
            normed_ref[r, side] = normed[part]
            halo_keys_ref[r, side] = keys[part]
            halo_values_ref[r, side] = values[part]
        for side in range(2):
            own = slice(0, win) if side == 0 else slice(own_len - win, own_len)
            first_query = place_ref[0] + own.start
            if side == 0:
                wide_keys = jnp.concatenate([keys[:win], keys_ref[r, : 2 * win]], axis=0)
                wide_values = jnp.concatenate([values[:win], values_ref[r, : 2 * win]], axis=0)
            else:
                wide_keys = jnp.concatenate([keys_ref[r, own_len - 2 * win :], keys[win:]], axis=0)
                wide_values = jnp.concatenate([values_ref[r, own_len - 2 * win :], values[win:]], axis=0)
            bias = mask_bias(
                starts_ref, step * pair + r, first_query, win, first_query - win, 3 * win, place_ref[1], False
            )
            attended.append(attend(queries_ref[r, own], wide_keys, wide_values, bias))
            inputs.append(tokens_ref[r, own].astype(F32))
            tops.append(top_ref[r, own])
    result, grad_middle, grad_attended = dense_chain(
        jnp.concatenate(inputs, axis=0),
        jnp.concatenate(attended, axis=0),
        jnp.concatenate(tops, axis=0),
        out_ref,
        up_ref,
        down_ref,
        gains_ref[1:2],
        (sum_up, sum_down, sum_out),
    )
    shape = (pair, 2, win, width)
    result_ref[...] = result.reshape(shape)
    grad_middle_ref[...] = grad_middle.reshape(shape)
    grad_attended_ref[...] = grad_attended.reshape(shape)

    @pl.when(step == pl.num_programs(0) - 1)
    def _():
        rows = width // BLOCKS
        for ref, base in ((keep_ref, 0), (send_ref, BLOCKS // 2)):

            @pl.loop(0, BLOCKS // 2)
            def _(i):
                block = place_ref[2] ^ (i + base)
                own_rows = pl.ds(pl.multiple_of(block * rows, rows), rows)
                for c in range(up_ref.shape[1] // width):
                    ref[i, c * rows : (c + 1) * rows] = sum_up[own_rows, c * width : (c + 1) * width].astype(BF16)
                at = up_ref.shape[1] // width * rows
                ref[i, at : at + rows] = sum_out[own_rows, :].astype(BF16)
                down_rows = hidden // BLOCKS
                ref[i, at + rows :] = sum_down[
                    pl.ds(pl.multiple_of(block * down_rows, down_rows), down_rows), :
                ].astype(BF16)


def third_kernel(
    own_len,
    place_ref,
    starts_ref,
    queries_ref,
    keys_ref,
    values_ref,
    halo_keys_ref,
    halo_values_ref,
    normed_ref,
    halo_normed_ref,
    mid_grad_ref,
    out_grad_ref,
    in_ref,
    cos_ref,
    sin_ref,
    own_ref,
    to_low_ref,
    to_high_ref,
    keep_ref,
    send_ref,
    sum_in,
):
    row = pl.program_id(0)
    width = queries_ref.shape[2]
    win = HALF_WIN
    count = own_len // 2
    span = count + 2 * win

    @pl.when(row == 0)
    def _():
        sum_in[...] = jnp.zeros_like(sum_in)

    keys = jnp.concatenate([halo_keys_ref[0, 0], keys_ref[0], halo_keys_ref[0, 1]], axis=0)
    values = jnp.concatenate([halo_values_ref[0, 0], values_ref[0], halo_values_ref[0, 1]], axis=0)
    normed = jnp.concatenate([halo_normed_ref[0, 0], normed_ref[0], halo_normed_ref[0, 1]], axis=0)
    grads = jnp.concatenate([out_grad_ref[0, 0], mid_grad_ref[0], out_grad_ref[0, 1]], axis=0)
    queries = queries_ref[0]
    biases = [
        mask_bias(
            starts_ref, row, place_ref[0] + b * count, count, place_ref[0] + b * count - win, span, place_ref[1], True
        )
        for b in range(2)
    ]
    cosine, sines = cos_ref[...], sin_ref[...]
    own = slice(win, win + own_len)
    grad_normed = jnp.zeros((own_len + 2 * win, width), F32)
    grad_own = jnp.zeros((own_len, width), F32)
    for c in range(0, width, WIDE):
        grad_keys, grad_values, grad_queries = [], [], []
        for b in range(2):
            k4 = keys[b * count : b * count + span, c : c + WIDE]
            v4 = values[b * count : b * count + span, c : c + WIDE]
            q4 = by_head(queries[b * count : (b + 1) * count, c : c + WIDE])
            g4 = by_head(grads[b * count : (b + 1) * count, c : c + WIDE])
            scores = nt(k4, q4)
            grad_probs = nt(v4, g4)
            lows, grad_scores = [], []
            for h in range(GROUP):
                cols = slice(h * count, (h + 1) * count)
                part = scores[:, cols] + biases[b]
                part = jnp.exp(part - jnp.max(part, axis=0, keepdims=True))
                part = part * (1.0 / jnp.sum(part, axis=0, keepdims=True))
                grad_part = grad_probs[:, cols]
                inner = jnp.sum(part * grad_part, axis=0, keepdims=True)
                lows.append(part.astype(BF16))
                grad_scores.append((part * (grad_part - inner)).astype(BF16))
            low = jnp.concatenate(lows, axis=1)
            grad_score = jnp.concatenate(grad_scores, axis=1)
            grad_values.append(nn(low, g4))
            grad_keys.append(nn(grad_score, q4))
            grad_queries.append(pick_heads(tn(grad_score, k4), count))

        def merge(parts):
            return jnp.concatenate(
                [parts[0][:count], parts[0][count:] + parts[1][: span - count], parts[1][span - count :]], axis=0
            )

        for part, at in ((merge(grad_keys), width), (merge(grad_values), 2 * width)):
            if at == width:
                part = rotate_back(part, cosine, sines)
            part = part.astype(BF16)
            sum_in[:, at + c : at + c + WIDE] += tn(normed, part)
            grad_normed = grad_normed + nt(part, in_ref[:, at + c : at + c + WIDE])
        part = jnp.concatenate(grad_queries, axis=0) * SCALE
        part = rotate_back(part, cosine[own], sines[own]).astype(BF16)
        sum_in[:, c : c + WIDE] += tn(normed[own], part)
        grad_own = grad_own + nt(part, in_ref[:, c : c + WIDE])
    own_ref[0] = grad_normed[own] + grad_own
    to_low_ref[0] = grad_normed[:win].astype(BF16)
    to_high_ref[0] = grad_normed[win + own_len :].astype(BF16)

    @pl.when(row == pl.num_programs(0) - 1)
    def _():
        rows = width // BLOCKS
        for ref, base in ((keep_ref, 0), (send_ref, BLOCKS // 2)):

            @pl.loop(0, BLOCKS // 2)
            def _(i):
                own_rows = pl.ds(pl.multiple_of((place_ref[2] ^ (i + base)) * rows, rows), rows)
                for c in range(in_ref.shape[1] // width):
                    ref[i, c * rows : (c + 1) * rows] = sum_in[own_rows, c * width : (c + 1) * width].astype(BF16)


def fourth_kernel(
    own_len,
    tokens_ref,
    own_ref,
    from_low_ref,
    from_high_ref,
    mid_grad_ref,
    out_grad_ref,
    gains_ref,
    mid_result_ref,
    out_result_ref,
    grad_ref,
    result_ref,
):
    win = HALF_WIN
    unit, inverse = normalize(tokens_ref[0].astype(F32))
    grads = jnp.concatenate(
        [
            own_ref[0, :win] + from_low_ref[0].astype(F32),
            own_ref[0, win : own_len - win],
            own_ref[0, own_len - win :] + from_high_ref[0].astype(F32),
        ],
        axis=0,
    )
    middle = jnp.concatenate([out_grad_ref[0, 0], mid_grad_ref[0], out_grad_ref[0, 1]], axis=0)
    grad_ref[0] = middle + norm_back(grads * gains_ref[0:1], unit, inverse)
    result_ref[0] = jnp.concatenate([out_result_ref[0, 0], mid_result_ref[0], out_result_ref[0, 1]], axis=0)


def place_kernel(place_ref, own_ref, other_ref, *out_refs):
    half = BLOCKS // 2
    for ref, base in ((own_ref, 0), (other_ref, half)):

        @pl.loop(0, half)
        def _(i):
            block = place_ref[2] ^ (i + base)
            at = 0
            for out in out_refs:
                rows = out.shape[0] // BLOCKS
                for c in range(0, out.shape[1], ref.shape[2]):
                    out[pl.ds(pl.multiple_of(block * rows, rows), rows), c : c + ref.shape[2]] = ref[
                        i, at : at + rows
                    ].astype(F32)
                    at += rows


def shift_route(size, distance):
    return [(i, i + distance) for i in range(size) if 0 <= i + distance < size]


def swap_route(flip):
    dp, seq = lax.axis_size("dp"), lax.axis_size("seq")

    def partner(i):
        d, s = divmod(i, seq)
        core, x, y, z, rest = flip
        return (d ^ (core + 2 * x)) * seq + (s ^ (y + 2 * z + 8 * rest))

    return [(i, partner(i)) for i in range(dp * seq)]


def swap(values, core=0, x=0, y=0, z=0, rest=0):
    return lax.ppermute(values, ("dp", "seq"), swap_route((core, x, y, z, rest)))


def add_all(*parts):
    return sum(p.astype(F32) for p in parts).astype(BF16)


def total_over_devices(keep, send):
    own = add_all(keep, swap(send, core=1))
    own = own.reshape((4, 4) + own.shape[1:])
    own = add_all(own[0], *[swap(own[k], x=k >> 1, y=k & 1) for k in (1, 2, 3)])
    own = add_all(own[0], *[swap(own[k], z=k) for k in (1, 2, 3)])
    rest = 1
    while 8 * rest < lax.axis_size("seq"):
        own = add_all(own, swap(own, rest=rest))
        rest *= 2
    own = jnp.stack([own] + [swap(own, z=k) for k in (1, 2, 3)])
    own = jnp.concatenate([own] + [swap(own, x=k >> 1, y=k & 1) for k in (1, 2, 3)])
    return own, swap(own, core=1)


def whole(array):
    return pl.BlockSpec(array.shape, lambda i: (0,) * array.ndim)


def rows_of(array, pair):
    return pl.BlockSpec((pair,) + array.shape[1:], lambda i: (i,) + (0,) * (array.ndim - 1))


SMEM = pl.BlockSpec(memory_space=pltpu.SMEM)


def params():
    return pltpu.CompilerParams(vmem_limit_bytes=VMEM)


def cost(flops, moved, special=0):
    return pl.CostEstimate(flops=int(flops), bytes_accessed=int(moved), transcendentals=int(special))


def shards(
    tokens,
    document_starts,
    attention_in,
    attention_out,
    feedforward_in,
    feedforward_out,
    gain_first,
    gain_second,
    result_grad,
):
    rows, own_len, width = tokens.shape
    hidden = feedforward_out.shape[0]
    win = HALF_WIN
    seq = lax.axis_size("seq")
    s, d = lax.axis_index("seq"), lax.axis_index("dp")
    start = s * own_len
    block = (d % 2) * 16 + (d // 2) * 8 + (s % 2) * 4 + (s // 2) % 4
    place = jnp.stack([start, jnp.int32(own_len * seq), block]).astype(jnp.int32)
    gains = jnp.stack([gain_first, gain_second])
    inverse = ROTARY_BASE ** (-(jnp.arange(0, HEAD_DIM, 2).astype(F32) / HEAD_DIM))
    positions = start - win + jnp.arange(own_len + 2 * win, dtype=jnp.int32)
    angles = positions.astype(F32)[:, None] * inverse[None, :]
    cosine, sines = jnp.cos(angles), jnp.sin(angles)
    cosine = jnp.concatenate([cosine] * 4, axis=1)
    sines = jnp.concatenate([-sines, sines] * 2, axis=1)
    own_cos, own_sin = cosine[win : win + own_len], sines[win : win + own_len]
    halo_cos = jnp.concatenate([cosine[:win], cosine[win + own_len :]])
    halo_sin = jnp.concatenate([sines[:win], sines[win + own_len :]])

    up_route, down_route = shift_route(seq, 1), shift_route(seq, -1)
    low_tokens = lax.ppermute(tokens[:, own_len - win :], "seq", up_route)
    high_tokens = lax.ppermute(tokens[:, :win], "seq", down_route)

    def shape(*dims, kind=BF16):
        return jax.ShapeDtypeStruct(dims, kind)

    weights = (attention_in, attention_out, feedforward_in, feedforward_out)
    pair = 2
    mid = own_len - 2 * win
    sums = [shape(*w.shape, kind=F32) for w in (feedforward_in, feedforward_out, attention_out)]
    outs = [shape(rows, own_len, width)] * 4 + [
        shape(rows, mid, width),
        shape(rows, mid, width, kind=F32),
        shape(rows, mid, width),
    ]
    small = (gains, own_cos, own_sin)
    normed, queries, keys, values, mid_result, mid_grad, mid_attended, sum_up, sum_down, sum_out = pl.pallas_call(
        functools.partial(first_kernel, own_len),
        grid=(rows // pair,),
        in_specs=[SMEM, SMEM, rows_of(tokens, pair), rows_of(tokens, pair)] + [whole(a) for a in weights + small],
        out_specs=[rows_of(o, pair) for o in outs] + [whole(o) for o in sums],
        out_shape=outs + sums,
        compiler_params=params(),
        cost_estimate=cost(16e9, 30e6),
        name="first",
    )(place, document_starts, tokens, result_grad, *weights, *small)

    outs = [shape(rows, 2, win, width)] * 4 + [
        shape(rows, 2, win, width, kind=F32),
        shape(rows, 2, win, width),
    ]
    piece = (2 * feedforward_in.shape[1] + 2 * width + 2 * hidden) // (2 * BLOCKS)
    piece = (feedforward_in.shape[1] // width * width + width + hidden) // BLOCKS
    blocks = [shape(BLOCKS // 2, piece, width)] * 2
    small = (gains, halo_cos, halo_sin)
    begun = (sum_up, sum_down, sum_out)
    by_row = (tokens, low_tokens, high_tokens, result_grad, queries, keys, values)
    halo_normed, halo_keys, halo_values, out_result, out_grad, out_attended, keep_one, send_one = pl.pallas_call(
        functools.partial(second_kernel, own_len),
        grid=(rows // pair,),
        in_specs=[SMEM, SMEM]
        + [rows_of(a, pair) for a in by_row]
        + [whole(a) for a in weights + small + begun],
        out_specs=[rows_of(o, pair) for o in outs] + [whole(o) for o in blocks],
        out_shape=outs + blocks,
        scratch_shapes=[pltpu.VMEM(o.shape, F32) for o in sums],
        compiler_params=params(),
        cost_estimate=cost(16e9, 30e6),
        name="second",
    )(place, document_starts, *by_row, *weights, *small, *begun)

    outs = [shape(rows, own_len, width, kind=F32), shape(rows, win, width), shape(rows, win, width)]
    piece = attention_in.shape[1] // width * width // BLOCKS
    blocks = [shape(BLOCKS // 2, piece, width)] * 2
    by_row = (queries, keys, values, halo_keys, halo_values, normed, halo_normed, mid_attended, out_attended)
    small = (attention_in, cosine, sines)
    own_grad, to_low, to_high, keep_two, send_two = pl.pallas_call(
        functools.partial(third_kernel, own_len),
        grid=(rows,),
        in_specs=[SMEM, SMEM] + [rows_of(a, 1) for a in by_row] + [whole(a) for a in small],
        out_specs=[rows_of(o, 1) for o in outs] + [whole(o) for o in blocks],
        out_shape=outs + blocks,
        scratch_shapes=[pltpu.VMEM(attention_in.shape, F32)],
        compiler_params=params(),
        cost_estimate=cost(20e9, 30e6),
        name="third",
    )(place, document_starts, *by_row, *small)

    total_one = total_over_devices(keep_one, send_one)
    total_two = total_over_devices(keep_two, send_two)
    from_high = lax.ppermute(to_low, "seq", down_route)
    from_low = lax.ppermute(to_high, "seq", up_route)

    outs = [shape(rows, own_len, width, kind=F32), shape(rows, own_len, width)]
    by_row = (tokens, own_grad, from_low, from_high, mid_grad, out_grad)
    results = (mid_result, out_result)
    grad_tokens, activations = pl.pallas_call(
        functools.partial(fourth_kernel, own_len),
        grid=(rows,),
        in_specs=[rows_of(a, 1) for a in by_row] + [whole(gains)] + [rows_of(a, 1) for a in results],
        out_specs=[rows_of(o, 1) for o in outs],
        out_shape=outs,
        compiler_params=params(),
        cost_estimate=cost(1e7, 15e6),
        name="fourth",
    )(*by_row, gains, *results)

    def placed(parts, *weights):
        return pl.pallas_call(
            place_kernel,
            grid=(1,),
            in_specs=[SMEM] + [whole(a) for a in parts],
            out_specs=[whole(w) for w in weights],
            out_shape=[shape(*w.shape, kind=F32) for w in weights],
            compiler_params=params(),
            cost_estimate=cost(1e6, 8e6),
            name="place",
        )(place, *parts)

    grad_up, grad_out, grad_down = placed(total_one, feedforward_in, attention_out, feedforward_out)
    (grad_in,) = placed(total_two, attention_in)
    grad_gain_one = jnp.sum(grad_in * attention_in.astype(F32), axis=1) / gain_first
    grad_gain_two = jnp.sum(grad_up * feedforward_in.astype(F32), axis=1) / gain_second
    return activations, grad_tokens, grad_in, grad_out, grad_up, grad_down, grad_gain_one, grad_gain_two


def solution(mesh):
    token, rest = P("dp", "seq", None), P()
    return jax.shard_map(
        shards,
        mesh=mesh,
        in_specs=(token, P("dp", None)) + (rest,) * 6 + (token,),
        out_specs=(token, token) + (rest,) * 6,
        check_vma=False,
    )
```

```python
import functools

import jax
import jax.numpy as jnp
import numpy as np
from jax import lax
from jax.experimental import pallas as pl
from jax.experimental.pallas import tpu as pltpu
from jax.sharding import PartitionSpec as P

HEADS = 8
HEAD_DIM = 64
HALF = HEAD_DIM // 2
HALF_WIN = 64
EPSILON = 1e-05
ROTARY_BASE = 10000.0
SCALE = HEAD_DIM**-0.5
BLOCKS = 32
GROUP = 4
WIDE = GROUP * HEAD_DIM
LANES = 128
MB = 1024 * 1024

F32 = jnp.float32
BF16 = jnp.bfloat16


def dot(a, b, contract):
    return lax.dot_general(a, b, ((contract[:1], contract[1:]), ((), ())), preferred_element_type=F32)


def nn(a, b):
    return dot(a, b, (1, 0))


def nt(a, b):
    return dot(a, b, (1, 1))


def tn(a, b):
    return dot(a, b, (0, 0))


def iota(shape, dim):
    return lax.broadcasted_iota(jnp.int32, shape, dim)


def flat(values):
    return values.reshape(-1, values.shape[-1])


def normalize(values):
    shifted = values - jnp.mean(values, axis=-1, keepdims=True)
    inverse = lax.rsqrt(jnp.mean(shifted * shifted, axis=-1, keepdims=True) + EPSILON)
    return shifted * inverse, inverse


def norm_back(scaled_grad, unit, inverse):
    return (
        scaled_grad
        - jnp.mean(scaled_grad, axis=-1, keepdims=True)
        - unit * jnp.mean(scaled_grad * unit, axis=-1, keepdims=True)
    ) * inverse


def halves_first():
    old, new = iota((WIDE, WIDE), 0), iota((WIDE, WIDE), 1)
    moved = (old % HEAD_DIM) // HALF * LANES + old // HEAD_DIM * HALF + old % HALF
    return (moved == new).astype(BF16)


def head_of(shape, halved):
    lane = iota(shape, 1)
    return lane % LANES // HALF if halved else lane // HEAD_DIM


def by_head(values, halved):
    head = head_of(values.shape, halved)
    zero = jnp.zeros_like(values)
    return jnp.concatenate([jnp.where(head == h, values, zero) for h in range(GROUP)], axis=0)


def pick_heads(stacked, halved):
    count = stacked.shape[0] // GROUP
    head = head_of((count, stacked.shape[1]), halved)
    out = stacked[:count]
    for h in range(1, GROUP):
        out = jnp.where(head == h, stacked[h * count : (h + 1) * count], out)
    return out


def turn(values, cosine, sines):
    first, second = values[:, :LANES], values[:, LANES:]
    return jnp.concatenate([first * cosine - second * sines, second * cosine + first * sines], axis=1)


def turn_back(values, cosine, sines):
    first, second = values[:, :LANES], values[:, LANES:]
    return jnp.concatenate([first * cosine + second * sines, second * cosine - first * sines], axis=1)


def project_kernel(
    tokens_ref,
    starts_ref,
    in_ref,
    gain_ref,
    base_ref,
    table_ref,
    normed_ref,
    queries_ref,
    keys_ref,
    values_ref,
    weight_ref,
    angles_ref,
    bounds_ref,
):
    rows, own_len, width = tokens_ref.shape
    win = HALF_WIN
    place = lax.axis_index("seq")
    start = place * own_len
    row_len = own_len * lax.axis_size("seq")

    base_cos, base_sin = base_ref[place, 0:1], base_ref[place, 1:2]
    angles_ref[0] = base_cos * table_ref[0] - base_sin * table_ref[1]
    angles_ref[1] = base_sin * table_ref[0] + base_cos * table_ref[1]

    lane = iota((rows, own_len - 2 * win + 4 * win), 1)
    mid = own_len - 2 * win
    pos = start + jnp.where(
        lane < mid, lane + win, jnp.where(lane < mid + 2 * win, lane % win, own_len - win + lane % win)
    )
    first, last = jnp.maximum(pos - win, 0), jnp.minimum(pos + win, row_len - 1)
    for j in range(starts_ref.shape[1]):
        cut = starts_ref[:, j : j + 1]
        first = jnp.maximum(first, jnp.where(cut <= pos, cut, 0))
        last = jnp.minimum(last, jnp.where(cut > pos, cut - 1, row_len))
    for r in range(rows):
        bounds_ref[r, 0:1] = first[r : r + 1]
        bounds_ref[r, 1:2] = last[r : r + 1]

    order = halves_first()
    for c in range(0, 2 * width, WIDE):
        weight_ref[:, c : c + WIDE] = nn(in_ref[:, c : c + WIDE], order).astype(BF16)
    weight_ref[:, 2 * width :] = in_ref[:, 2 * width :]

    pair = 2
    cosine, sines = angles_ref[0, win : win + own_len], angles_ref[1, win : win + own_len]
    cosine, sines = jnp.concatenate([cosine] * pair), jnp.concatenate([sines] * pair)

    @pl.loop(0, rows // pair)
    def _(i):
        at = pl.ds(i * pair, pair)
        unit, _ = normalize(flat(tokens_ref[at]).astype(F32))
        normed = (unit * gain_ref[...]).astype(BF16)
        normed_ref[at] = normed.reshape(pair, own_len, width)
        for c in range(0, width, WIDE):
            part = turn(nn(normed, weight_ref[:, c : c + WIDE]), cosine * SCALE, sines * SCALE)
            queries_ref[at, :, c : c + WIDE] = part.astype(BF16).reshape(pair, own_len, WIDE)
            part = turn(nn(normed, weight_ref[:, width + c : width + c + WIDE]), cosine, sines)
            keys_ref[at, :, c : c + WIDE] = part.astype(BF16).reshape(pair, own_len, WIDE)
        values_ref[at] = nn(normed, weight_ref[:, 2 * width :]).astype(BF16).reshape(pair, own_len, width)


def halo_kernel(low_ref, high_ref, weight_ref, gain_ref, angles_ref, normed_ref, keys_ref, values_ref):
    rows, win, width = low_ref.shape
    pair = 3
    span = angles_ref.shape[1]
    cosine = jnp.concatenate([angles_ref[0, :win], angles_ref[0, span - win :]] * pair)
    sines = jnp.concatenate([angles_ref[1, :win], angles_ref[1, span - win :]] * pair)

    @pl.loop(0, rows // pair)
    def _(i):
        at = pl.ds(i * pair, pair)
        unit, _ = normalize(flat(jnp.concatenate([low_ref[at], high_ref[at]], axis=1)).astype(F32))
        normed = (unit * gain_ref[...]).astype(BF16)
        normed_ref[at] = normed.reshape(pair, 2 * win, width)
        for c in range(0, width, WIDE):
            part = turn(nn(normed, weight_ref[:, width + c : width + c + WIDE]), cosine, sines)
            keys_ref[at, :, c : c + WIDE] = part.astype(BF16).reshape(pair, 2 * win, WIDE)
        values_ref[at] = nn(normed, weight_ref[:, 2 * width :]).astype(BF16).reshape(pair, 2 * win, width)


def bias_of(bounds_ref, row, lanes, first_key, keys):
    key = first_key + iota((keys, LANES), 0)
    first, last = bounds_ref[row, 0:1, lanes], bounds_ref[row, 1:2, lanes]
    return jnp.where((key >= first) & (key <= last), 0.0, -jnp.inf)


def probabilities(scores, bias):
    parts = []
    for c in range(0, scores.shape[1], LANES):
        part = scores[:, c : c + LANES] + bias
        part = jnp.exp(part - jnp.max(part, axis=0, keepdims=True))
        parts.append(part * (1.0 / jnp.sum(part, axis=0, keepdims=True)))
    return jnp.concatenate(parts, axis=1)


def attend_mid_kernel(queries_ref, keys_ref, values_ref, bounds_ref, attended_ref, probs_ref):
    rows, own_len, width = queries_ref.shape
    win = HALF_WIN
    mid = own_len - 2 * win
    start = lax.axis_index("seq") * own_len
    pair = 2

    @pl.loop(0, rows // pair)
    def _(i):
        for r in range(pair):
            row = i * pair + r
            bias = bias_of(bounds_ref, row, slice(0, mid), start, own_len)
            for g in range(width // WIDE):
                cols = slice(g * WIDE, (g + 1) * WIDE)
                probs = probabilities(
                    nt(keys_ref[row, :, cols], by_head(queries_ref[row, win : win + mid, cols], True)), bias
                )
                probs_ref[row, g] = probs
                out = tn(probs.astype(BF16), values_ref[row, :, cols])
                attended_ref[row, :, cols] = pick_heads(out, False).astype(BF16)


def wide_side(own, halo, side):
    win = HALF_WIN
    if side == 0:
        return jnp.concatenate([halo[:win], own[: 2 * win]], axis=0)
    return jnp.concatenate([own[own.shape[0] - 2 * win :], halo[win:]], axis=0)


def attend_out_kernel(
    queries_ref, keys_ref, values_ref, halo_keys_ref, halo_values_ref, bounds_ref, attended_ref, probs_ref
):
    rows, own_len, width = queries_ref.shape
    win = HALF_WIN
    mid = own_len - 2 * win
    start = lax.axis_index("seq") * own_len
    pair = 2

    @pl.loop(0, rows // pair)
    def _(i):
        for r in range(pair):
            row = i * pair + r
            for side in range(2):
                own = slice(0, win) if side == 0 else slice(own_len - win, own_len)
                lanes = slice(mid + side * LANES, mid + (side + 1) * LANES)
                bias = bias_of(bounds_ref, row, lanes, start + own.start - win, 3 * win)
                for g in range(width // WIDE):
                    cols = slice(g * WIDE, (g + 1) * WIDE)
                    keys = wide_side(keys_ref[row, :, cols], halo_keys_ref[row, :, cols], side)
                    values = wide_side(values_ref[row, :, cols], halo_values_ref[row, :, cols], side)
                    probs = probabilities(nt(keys, by_head(queries_ref[row, own, cols], True)), bias)
                    probs_ref[row, side, g] = probs
                    out = tn(probs.astype(BF16), values)
                    attended_ref[row, side * win : (side + 1) * win, cols] = pick_heads(out, False).astype(BF16)


def gelu_parts(gate):
    bell = jnp.exp(-0.5 * gate * gate)
    t = 1.0 / (1.0 + (0.3275911 * 0.7071067811865476) * jnp.abs(gate))
    tail = t * (
        0.5 * 0.254829592
        + t * (0.5 * -0.284496736 + t * (0.5 * 1.421413741 + t * (0.5 * -1.453152027 + t * (0.5 * 1.061405429))))
    )
    tail = tail * bell
    return jnp.where(gate < 0, tail, 1.0 - tail), gate * bell * 0.3989422804014327


def part_of(ref, at, outer):
    own_len, win = ref.shape[1], HALF_WIN
    if outer:
        return flat(jnp.concatenate([ref[at, :win], ref[at, own_len - win :]], axis=1))
    return flat(ref[at, win : own_len - win])


def dense_kernel(
    outer,
    tokens_ref,
    top_ref,
    attended_ref,
    out_ref,
    up_ref,
    down_ref,
    gain_ref,
    middle_ref,
    normed_ref,
    mixed_ref,
    grad_up_ref,
    grad_middle_ref,
    branch_ref,
    grad_attended_ref,
):
    rows, count, width = attended_ref.shape
    hidden = down_ref.shape[0]
    pair = 3

    @pl.loop(0, rows // pair)
    def _(i):
        at = pl.ds(i * pair, pair)

        def put(ref, values, cols=slice(None)):
            ref[at, :, cols] = values.reshape(pair, count, -1)

        top = part_of(top_ref, at, outer)
        middle = part_of(tokens_ref, at, outer).astype(F32) + nn(flat(attended_ref[at]), out_ref[...])
        put(middle_ref, middle)
        unit, inverse = normalize(middle)
        normed = (unit * gain_ref[...]).astype(BF16)
        put(normed_ref, normed)
        for c in range(0, hidden, 256):
            gate = nn(normed, up_ref[:, c : c + 256])
            lift = nn(normed, up_ref[:, hidden + c : hidden + c + 256])
            grad_mixed = nt(top, down_ref[c : c + 256])
            phi, slope = gelu_parts(gate)
            active = gate * phi
            put(mixed_ref, (active * lift).astype(BF16), slice(c, c + 256))
            put(grad_up_ref, (grad_mixed * lift * (phi + slope)).astype(BF16), slice(c, c + 256))
            put(grad_up_ref, (grad_mixed * active).astype(BF16), slice(hidden + c, hidden + c + 256))
        grad_normed = nt(flat(grad_up_ref[at]), up_ref[...])
        grad_middle = top.astype(F32) + norm_back(grad_normed * gain_ref[...], unit, inverse)
        put(grad_middle_ref, grad_middle)
        branch = grad_middle.astype(BF16)
        put(branch_ref, branch)
        put(grad_attended_ref, nt(branch, out_ref[...]).astype(BF16))


def both(mid_ref, out_ref, cols=slice(None)):
    return jnp.concatenate([flat(mid_ref[:, :, cols]), flat(out_ref[:, :, cols])], axis=0)


def store_blocks(keep_ref, send_ref, store):
    seq, dp = lax.axis_index("seq"), lax.axis_index("dp")
    place = (dp % 2) * 16 + (dp // 2) * 8 + (seq % 2) * 4 + (seq // 2) % 4
    for ref, base in ((keep_ref, 0), (send_ref, BLOCKS // 2)):

        @pl.loop(0, BLOCKS // 2)
        def _(i):
            store(ref, i, place ^ (i + base))


def weights_kernel(
    top_ref,
    mid_normed_ref,
    out_normed_ref,
    mid_grad_up_ref,
    out_grad_up_ref,
    mid_mixed_ref,
    out_mixed_ref,
    mid_attended_ref,
    out_attended_ref,
    mid_branch_ref,
    out_branch_ref,
    keep_ref,
    send_ref,
    up_sum,
    out_sum,
    down_sum,
):
    width = top_ref.shape[2]
    everything = slice(0, top_ref.shape[0])
    normed = both(mid_normed_ref, out_normed_ref)
    for c in range(0, up_sum.shape[1], 256):
        cols = slice(c, c + 256)
        up_sum[:, cols] = tn(normed, both(mid_grad_up_ref, out_grad_up_ref, cols)).astype(BF16)
    top = jnp.concatenate([part_of(top_ref, everything, False), part_of(top_ref, everything, True)], axis=0)
    for c in range(0, down_sum.shape[0], 256):
        down_sum[c : c + 256] = tn(both(mid_mixed_ref, out_mixed_ref, slice(c, c + 256)), top)
    out_sum[...] = tn(both(mid_attended_ref, out_attended_ref), both(mid_branch_ref, out_branch_ref)).astype(BF16)
    rows, down_rows = width // BLOCKS, down_sum.shape[0] // BLOCKS

    def store(ref, i, block):
        own = pl.ds(pl.multiple_of(block * rows, rows), rows)
        at = 0
        for c in range(0, up_sum.shape[1], width):
            ref[i, at : at + rows] = up_sum[own, c : c + width]
            at += rows
        ref[i, at : at + rows] = out_sum[own, :]
        at += rows
        ref[i, at:] = down_sum[pl.ds(pl.multiple_of(block * down_rows, down_rows), down_rows), :].astype(BF16)

    store_blocks(keep_ref, send_ref, store)


def attend_back_kernel(
    group,
    queries_ref,
    keys_ref,
    values_ref,
    halo_keys_ref,
    halo_values_ref,
    mid_grad_ref,
    out_grad_ref,
    mid_probs_ref,
    out_probs_ref,
    angles_ref,
    own_ref,
    halo_ref,
):
    rows, own_len, _ = queries_ref.shape
    win = HALF_WIN
    mid = own_len - 2 * win
    cols = slice(group * WIDE, (group + 1) * WIDE)
    cosine, sines = angles_ref[0], angles_ref[1]
    own_cos, own_sin = cosine[win : win + own_len], sines[win : win + own_len]
    halo_cos = jnp.concatenate([cosine[:win], cosine[win + own_len :]])
    halo_sin = jnp.concatenate([sines[:win], sines[win + own_len :]])
    pair = 2

    def unit(queries, keys, values, grads, probs):
        q4, g4 = by_head(queries, True), by_head(grads, False)
        grad_probs = nt(values, g4)
        lows, grad_scores = [], []
        for c in range(0, probs.shape[1], LANES):
            part, grad_part = probs[:, c : c + LANES], grad_probs[:, c : c + LANES]
            inner = jnp.sum(part * grad_part, axis=0, keepdims=True)
            lows.append(part.astype(BF16))
            grad_scores.append((part * (grad_part - inner)).astype(BF16))
        grad_scores = jnp.concatenate(grad_scores, axis=1)
        return (
            pick_heads(tn(grad_scores, keys), True),
            nn(grad_scores, q4),
            nn(jnp.concatenate(lows, axis=1), g4),
        )

    @pl.loop(0, rows // pair)
    def _(i):
        for r in range(pair):
            row = i * pair + r
            queries, keys, values = queries_ref[row, :, cols], keys_ref[row, :, cols], values_ref[row, :, cols]
            halo_keys, halo_values = halo_keys_ref[row, :, cols], halo_values_ref[row, :, cols]
            grads = out_grad_ref[row, :, cols]
            middle = unit(queries[win : win + mid], keys, values, mid_grad_ref[row, :, cols], mid_probs_ref[row, group])
            sides = [
                unit(
                    queries[:win] if side == 0 else queries[own_len - win :],
                    wide_side(keys, halo_keys, side),
                    wide_side(values, halo_values, side),
                    grads[side * win : (side + 1) * win],
                    out_probs_ref[row, side, group],
                )
                for side in range(2)
            ]
            low, high = sides
            own = [jnp.concatenate([low[0], middle[0], high[0]], axis=0) * SCALE]
            halo = []
            for k in (1, 2):
                own.append(middle[k] + jnp.concatenate([low[k][win:], high[k][: 2 * win]], axis=0))
                halo.append(jnp.concatenate([low[k][:win], high[k][2 * win :]], axis=0))
            own_ref[row, :, :WIDE] = turn_back(own[0], own_cos, own_sin).astype(BF16)
            own_ref[row, :, WIDE : 2 * WIDE] = turn_back(own[1], own_cos, own_sin).astype(BF16)
            own_ref[row, :, 2 * WIDE :] = own[2].astype(BF16)
            halo_ref[row, :, :WIDE] = turn_back(halo[0], halo_cos, halo_sin).astype(BF16)
            halo_ref[row, :, WIDE:] = halo[1].astype(BF16)


def weight_in_kernel(normed_ref, halo_normed_ref, *refs):
    *grads, keep_ref, send_ref, total = refs
    width = normed_ref.shape[2]
    normed, halo_normed = flat(normed_ref[...]), flat(halo_normed_ref[...])
    normed_all = jnp.concatenate([normed, halo_normed], axis=0)
    order = halves_first()
    for g in range(len(grads) // 2):
        own, halo = grads[2 * g : 2 * g + 2]
        for k in range(3):
            part = flat(own[:, :, k * WIDE : (k + 1) * WIDE])
            if k == 0:
                part = tn(normed, part)
            else:
                part = tn(normed_all, jnp.concatenate([part, flat(halo[:, :, (k - 1) * WIDE : k * WIDE])], axis=0))
            part = part.astype(BF16)
            if k < 2:
                part = nt(part, order).astype(BF16)
            total[:, k * width + g * WIDE : k * width + (g + 1) * WIDE] = part
    rows = width // BLOCKS

    def store(ref, i, block):
        own = pl.ds(pl.multiple_of(block * rows, rows), rows)
        for k in range(3):
            ref[i, k * rows : (k + 1) * rows] = total[own, k * width : (k + 1) * width]

    store_blocks(keep_ref, send_ref, store)


def grad_halo_kernel(weight_ref, *refs):
    *grads, low_ref, high_ref = refs
    rows, win, width = low_ref.shape
    total = None
    for g, ref in enumerate(grads):
        weight = jnp.concatenate(
            [weight_ref[:, k * width + g * WIDE : k * width + (g + 1) * WIDE] for k in (1, 2)], axis=1
        )
        part = nt(flat(ref[...]), weight)
        total = part if total is None else total + part
    total = total.astype(BF16).reshape(rows, 2 * win, width)
    low_ref[...] = total[:, :win]
    high_ref[...] = total[:, win:]


def grad_own_kernel(weight_ref, *refs):
    *grads, out_ref = refs
    rows, own_len, width = out_ref.shape
    pair = 2
    groups = len(grads)

    @pl.loop(0, rows // pair)
    def _(i):
        at = pl.ds(i * pair, pair)
        grad = jnp.concatenate([flat(ref[at]) for ref in grads], axis=1)
        weight = jnp.concatenate(
            [
                weight_ref[:, k * width + g * WIDE : k * width + (g + 1) * WIDE]
                for g in range(groups)
                for k in range(3)
            ],
            axis=1,
        )
        out_ref[at] = nt(grad, weight).reshape(pair, own_len, width)


def result_kernel(mid_middle_ref, out_middle_ref, mid_mixed_ref, out_mixed_ref, down_ref, result_ref):
    own_len, win = result_ref.shape[1], HALF_WIN
    pair = 3

    @pl.loop(0, result_ref.shape[0] // pair)
    def _(i):
        at = pl.ds(i * pair, pair)

        def result(middle_ref, mixed_ref):
            total = flat(middle_ref[at]) + nn(flat(mixed_ref[at]), down_ref[...])
            return total.astype(BF16).reshape(middle_ref[at].shape)

        result_ref[at, win : own_len - win] = result(mid_middle_ref, mid_mixed_ref)
        outer = result(out_middle_ref, out_mixed_ref)
        result_ref[at, :win] = outer[:, :win]
        result_ref[at, own_len - win :] = outer[:, win:]


def finish_kernel(
    tokens_ref, own_ref, from_low_ref, from_high_ref, mid_grad_ref, out_grad_ref, gain_ref, grad_ref
):
    own_len, win = tokens_ref.shape[1], HALF_WIN

    @pl.loop(0, tokens_ref.shape[0])
    def _(row):
        unit, inverse = normalize(tokens_ref[row].astype(F32))
        own = own_ref[row]
        grads = jnp.concatenate(
            [
                own[:win] + from_low_ref[row].astype(F32),
                own[win : own_len - win],
                own[own_len - win :] + from_high_ref[row].astype(F32),
            ],
            axis=0,
        )
        outer = out_grad_ref[row]
        middle = jnp.concatenate([outer[:win], mid_grad_ref[row], outer[win:]], axis=0)
        grad_ref[row] = middle + norm_back(grads * gain_ref[...], unit, inverse)


def place_kernel(own_ref, other_ref, *out_refs):
    def store(ref, i, block):
        at = 0
        for out in out_refs:
            rows = out.shape[0] // BLOCKS
            for c in range(0, out.shape[1], ref.shape[2]):
                out[pl.ds(pl.multiple_of(block * rows, rows), rows), c : c + ref.shape[2]] = ref[
                    i, at : at + rows
                ].astype(F32)
                at += rows

    store_blocks(own_ref, other_ref, store)


def shift_route(size, distance):
    return [(i, i + distance) for i in range(size) if 0 <= i + distance < size]


def swap_route(core, x, y, z, rest):
    dp, seq = lax.axis_size("dp"), lax.axis_size("seq")

    def partner(i):
        d, s = divmod(i, seq)
        return (d ^ (core + 2 * x)) * seq + (s ^ (y + 2 * z + 8 * rest))

    return [(i, partner(i)) for i in range(dp * seq)]


def swap(values, core=0, x=0, y=0, z=0, rest=0):
    return lax.ppermute(values, ("dp", "seq"), swap_route(core, x, y, z, rest))


def add_all(*parts):
    return sum(p.astype(F32) for p in parts).astype(BF16)


def total_over_devices(keep, send):
    own = add_all(keep, swap(send, core=1))
    own = own.reshape((4, 4) + own.shape[1:])
    own = add_all(own[0], *[swap(own[k], x=k >> 1, y=k & 1) for k in (1, 2, 3)])
    own = add_all(own[0], *[swap(own[k], z=k) for k in (1, 2, 3)])
    rest = 1
    while 8 * rest < lax.axis_size("seq"):
        own = add_all(own, swap(own, rest=rest))
        rest *= 2
    own = jnp.stack([own] + [swap(own, z=k) for k in (1, 2, 3)])
    own = jnp.concatenate([own] + [swap(own, x=k >> 1, y=k & 1) for k in (1, 2, 3)])
    return own, swap(own, core=1)


def shape(*dims, kind=BF16):
    return jax.ShapeDtypeStruct(dims, kind)


def call(name, kernel, outs, *args, grant=16, flops=1e9, scratch=()):
    spec = pl.BlockSpec(memory_space=pltpu.VMEM)
    moved = sum(int(np.prod(a.shape)) * a.dtype.itemsize for a in (*args, *outs))
    return pl.pallas_call(
        kernel,
        out_shape=outs,
        in_specs=[spec] * len(args),
        out_specs=[spec] * len(outs),
        scratch_shapes=scratch,
        compiler_params=pltpu.CompilerParams(vmem_limit_bytes=grant * MB),
        cost_estimate=pl.CostEstimate(flops=int(flops), bytes_accessed=moved, transcendentals=0),
        name=name,
    )(*args)


def angle_tables(own_len, pieces):
    inverse = ROTARY_BASE ** (-(np.arange(0, HEAD_DIM, 2) / HEAD_DIM))
    inverse = np.tile(inverse, LANES // HALF)
    base = np.arange(pieces)[:, None] * own_len * inverse
    local = (np.arange(own_len + 2 * HALF_WIN) - HALF_WIN)[:, None] * inverse
    return [jnp.asarray(np.stack([np.cos(a), np.sin(a)], axis=d), F32) for a, d in ((base, 1), (local, 0))]


def shards(
    tokens,
    document_starts,
    attention_in,
    attention_out,
    feedforward_in,
    feedforward_out,
    gain_first,
    gain_second,
    result_grad,
):
    rows, own_len, width = tokens.shape
    hidden = feedforward_out.shape[0]
    win = HALF_WIN
    mid = own_len - 2 * win
    seq = lax.axis_size("seq")
    groups = width // WIDE
    gain_one, gain_two = gain_first[None], gain_second[None]

    up_route, down_route = shift_route(seq, 1), shift_route(seq, -1)
    low_tokens = lax.ppermute(tokens[:, own_len - win :], "seq", up_route)
    high_tokens = lax.ppermute(tokens[:, :win], "seq", down_route)

    row_shape = shape(rows, own_len, width)
    normed, queries, keys, values, weight, angles, bounds = call(
        "project",
        project_kernel,
        [row_shape] * 4
        + [
            shape(*attention_in.shape),
            shape(2, own_len + 2 * win, LANES, kind=F32),
            shape(rows, 2, mid + 4 * win, kind=jnp.int32),
        ],
        tokens,
        document_starts,
        attention_in,
        gain_one,
        *angle_tables(own_len, seq),
        flops=3e9,
    )
    mid_attended, mid_probs = call(
        "attend_mid",
        attend_mid_kernel,
        [shape(rows, mid, width), shape(rows, groups, own_len, GROUP * mid, kind=F32)],
        queries,
        keys,
        values,
        bounds,
        flops=2e9,
    )

    def dense(name, outer, attended):
        count = attended.shape[1]
        return call(
            name,
            functools.partial(dense_kernel, outer),
            [
                shape(rows, count, width, kind=F32),
                shape(rows, count, width),
                shape(rows, count, hidden),
                shape(rows, count, 2 * hidden),
                shape(rows, count, width, kind=F32),
                shape(rows, count, width),
                shape(rows, count, width),
            ],
            tokens,
            result_grad,
            attended,
            attention_out,
            feedforward_in,
            feedforward_out,
            gain_two,
            flops=5e9,
        )

    mid_middle, mid_normed, mid_mixed, mid_grad_up, mid_grad, mid_branch, mid_grad_attended = dense(
        "dense_mid", False, mid_attended
    )

    halo_normed, halo_keys, halo_values = call(
        "halo",
        halo_kernel,
        [shape(rows, 2 * win, width)] * 3,
        low_tokens,
        high_tokens,
        weight,
        gain_one,
        angles,
        flops=1e9,
    )
    out_attended, out_probs = call(
        "attend_out",
        attend_out_kernel,
        [shape(rows, 2 * win, width), shape(rows, 2, groups, 3 * win, GROUP * win, kind=F32)],
        queries,
        keys,
        values,
        halo_keys,
        halo_values,
        bounds,
        flops=2e9,
    )
    out_middle, out_normed, out_mixed, out_grad_up, out_grad, out_branch, out_grad_attended = dense(
        "dense_out", True, out_attended
    )

    piece = (feedforward_in.shape[1] // width * width + width + hidden) // BLOCKS
    keep_one, send_one = call(
        "weights",
        weights_kernel,
        [shape(BLOCKS // 2, piece, width)] * 2,
        result_grad,
        mid_normed,
        out_normed,
        mid_grad_up,
        out_grad_up,
        mid_mixed,
        out_mixed,
        mid_attended,
        out_attended,
        mid_branch,
        out_branch,
        flops=5e9,
        scratch=[
            pltpu.VMEM(feedforward_in.shape, BF16),
            pltpu.VMEM(attention_out.shape, BF16),
            pltpu.VMEM(feedforward_out.shape, F32),
        ],
    )

    own_grads, halo_grads = [], []
    for g in range(groups):
        own_part, halo_part = call(
            "attend_back_%d" % g,
            functools.partial(attend_back_kernel, g),
            [shape(rows, own_len, 3 * WIDE), shape(rows, 2 * win, 2 * WIDE)],
            queries,
            keys,
            values,
            halo_keys,
            halo_values,
            mid_grad_attended,
            out_grad_attended,
            mid_probs,
            out_probs,
            angles,
            flops=4e9,
        )
        own_grads.append(own_part)
        halo_grads.append(halo_part)
    keep_two, send_two = call(
        "weight_in",
        weight_in_kernel,
        [shape(BLOCKS // 2, attention_in.shape[1] // BLOCKS, width)] * 2,
        normed,
        halo_normed,
        *[a for pair in zip(own_grads, halo_grads) for a in pair],
        flops=4e9,
        scratch=[pltpu.VMEM(attention_in.shape, BF16)],
    )
    to_low, to_high = call(
        "grad_halo", grad_halo_kernel, [shape(rows, win, width)] * 2, weight, *halo_grads, flops=1e9
    )
    (own_grad,) = call(
        "grad_own", grad_own_kernel, [shape(rows, own_len, width, kind=F32)], weight, *own_grads, flops=2e9
    )

    total_one = total_over_devices(keep_one, send_one)
    total_two = total_over_devices(keep_two, send_two)
    from_high = lax.ppermute(to_low, "seq", down_route)
    from_low = lax.ppermute(to_high, "seq", up_route)

    (activations,) = call(
        "result", result_kernel, [row_shape], mid_middle, out_middle, mid_mixed, out_mixed, feedforward_out, flops=2e9
    )
    (grad_tokens,) = call(
        "finish",
        finish_kernel,
        [shape(rows, own_len, width, kind=F32)],
        tokens,
        own_grad,
        from_low,
        from_high,
        mid_grad,
        out_grad,
        gain_one,
        flops=1e8,
    )

    def placed(parts, *weights):
        return call("place", place_kernel, [shape(*w.shape, kind=F32) for w in weights], *parts, flops=1e6)

    grad_up, grad_out, grad_down = placed(total_one, feedforward_in, attention_out, feedforward_out)
    (grad_in,) = placed(total_two, attention_in)
    grad_gain_one = jnp.sum(grad_in * attention_in.astype(F32), axis=1) / gain_first
    grad_gain_two = jnp.sum(grad_up * feedforward_in.astype(F32), axis=1) / gain_second
    return activations, grad_tokens, grad_in, grad_out, grad_up, grad_down, grad_gain_one, grad_gain_two


def solution(mesh):
    token, rest = P("dp", "seq", None), P()
    return jax.shard_map(
        shards,
        mesh=mesh,
        in_specs=(token, P("dp", None)) + (rest,) * 6 + (token,),
        out_specs=(token, token) + (rest,) * 6,
        check_vma=False,
    )
```

```python
import functools

import jax
import jax.numpy as jnp
import numpy as np
from jax import lax
from jax.experimental import pallas as pl
from jax.experimental.pallas import tpu as pltpu
from jax.sharding import PartitionSpec as P

HEADS = 8
HEAD_DIM = 64
HALF = HEAD_DIM // 2
HALF_WIN = 64
EPSILON = 1e-05
ROTARY_BASE = 10000.0
SCALE = HEAD_DIM**-0.5
BLOCKS = 32
GROUP = 4
WIDE = GROUP * HEAD_DIM
LANES = 128
MB = 1024 * 1024

F32 = jnp.float32
BF16 = jnp.bfloat16


def dot(a, b, contract):
    return lax.dot_general(a, b, ((contract[:1], contract[1:]), ((), ())), preferred_element_type=F32)


def nn(a, b):
    return dot(a, b, (1, 0))


def nt(a, b):
    return dot(a, b, (1, 1))


def tn(a, b):
    return dot(a, b, (0, 0))


def iota(shape, dim):
    return lax.broadcasted_iota(jnp.int32, shape, dim)


def flat(values):
    return values.reshape(-1, values.shape[-1])


def normalize(values):
    shifted = values - jnp.mean(values, axis=-1, keepdims=True)
    inverse = lax.rsqrt(jnp.mean(shifted * shifted, axis=-1, keepdims=True) + EPSILON)
    return shifted * inverse, inverse


def norm_back(scaled_grad, unit, inverse):
    return (
        scaled_grad
        - jnp.mean(scaled_grad, axis=-1, keepdims=True)
        - unit * jnp.mean(scaled_grad * unit, axis=-1, keepdims=True)
    ) * inverse


def halves_first():
    old, new = iota((WIDE, WIDE), 0), iota((WIDE, WIDE), 1)
    moved = (old % HEAD_DIM) // HALF * LANES + old // HEAD_DIM * HALF + old % HALF
    return (moved == new).astype(BF16)


def head_of(shape, halved):
    lane = iota(shape, 1)
    return lane % LANES // HALF if halved else lane // HEAD_DIM


def by_head(values, halved):
    head = head_of(values.shape, halved)
    zero = jnp.zeros_like(values)
    return jnp.concatenate([jnp.where(head == h, values, zero) for h in range(GROUP)], axis=0)


def pick_heads(stacked, halved):
    count = stacked.shape[0] // GROUP
    head = head_of((count, stacked.shape[1]), halved)
    out = stacked[:count]
    for h in range(1, GROUP):
        out = jnp.where(head == h, stacked[h * count : (h + 1) * count], out)
    return out


def turn(values, cosine, sines):
    first, second = values[:, :LANES], values[:, LANES:]
    return jnp.concatenate([first * cosine - second * sines, second * cosine + first * sines], axis=1)


def turn_back(values, cosine, sines):
    first, second = values[:, :LANES], values[:, LANES:]
    return jnp.concatenate([first * cosine + second * sines, second * cosine - first * sines], axis=1)


def load_kernel(count, *refs):
    sources, outs, sems = refs[:count], refs[count:-1], refs[-1]
    own_len, win = sources[0].shape[1], HALF_WIN
    odd = lax.axis_index("seq") % 2
    copies = []
    for k, out in enumerate(outs):
        source = sources[0] if k >= count else sources[k]
        if k >= count:
            high = odd == 0 if k == count else odd == 1
            at = pl.multiple_of(jnp.where(high, own_len - win, 0), win)
            source = source.at[:, pl.ds(at, win)]
        copies.append(pltpu.make_async_copy(source, out, sems.at[k]))
    for copy in copies:
        copy.start()
    for copy in copies:
        copy.wait()


def by_side(inner, other):
    odd = lax.axis_index("seq") % 2 == 1
    return jnp.where(odd, inner, other), jnp.where(odd, other, inner)


def project_kernel(
    tokens_ref,
    starts_ref,
    in_ref,
    gain_ref,
    base_ref,
    table_ref,
    normed_ref,
    queries_ref,
    keys_ref,
    values_ref,
    weight_ref,
    angles_ref,
    bounds_ref,
):
    rows, own_len, width = tokens_ref.shape
    win = HALF_WIN
    place = lax.axis_index("seq")
    start = place * own_len
    row_len = own_len * lax.axis_size("seq")

    base_cos, base_sin = base_ref[place, 0:1], base_ref[place, 1:2]
    angles_ref[0] = base_cos * table_ref[0] - base_sin * table_ref[1]
    angles_ref[1] = base_sin * table_ref[0] + base_cos * table_ref[1]

    lane = iota((rows, own_len - 2 * win + 4 * win), 1)
    mid = own_len - 2 * win
    pos = start + jnp.where(
        lane < mid, lane + win, jnp.where(lane < mid + 2 * win, lane % win, own_len - win + lane % win)
    )
    first, last = jnp.maximum(pos - win, 0), jnp.minimum(pos + win, row_len - 1)
    for j in range(starts_ref.shape[1]):
        cut = starts_ref[:, j : j + 1]
        first = jnp.maximum(first, jnp.where(cut <= pos, cut, 0))
        last = jnp.minimum(last, jnp.where(cut > pos, cut - 1, row_len))
    for r in range(rows):
        bounds_ref[r, 0:1] = first[r : r + 1]
        bounds_ref[r, 1:2] = last[r : r + 1]

    order = halves_first()
    for c in range(0, 2 * width, WIDE):
        weight_ref[:, c : c + WIDE] = nn(in_ref[:, c : c + WIDE], order).astype(BF16)
    weight_ref[:, 2 * width :] = in_ref[:, 2 * width :]

    pair = 2
    cosine, sines = angles_ref[0, win : win + own_len], angles_ref[1, win : win + own_len]
    cosine, sines = jnp.concatenate([cosine] * pair), jnp.concatenate([sines] * pair)

    @pl.loop(0, rows // pair)
    def _(i):
        at = pl.ds(i * pair, pair)
        unit, _ = normalize(flat(tokens_ref[at]).astype(F32))
        normed = (unit * gain_ref[...]).astype(BF16)
        normed_ref[at] = normed.reshape(pair, own_len, width)
        for c in range(0, width, WIDE):
            part = turn(nn(normed, weight_ref[:, c : c + WIDE]), cosine * SCALE, sines * SCALE)
            queries_ref[at, :, c : c + WIDE] = part.astype(BF16).reshape(pair, own_len, WIDE)
            part = turn(nn(normed, weight_ref[:, width + c : width + c + WIDE]), cosine, sines)
            keys_ref[at, :, c : c + WIDE] = part.astype(BF16).reshape(pair, own_len, WIDE)
        values_ref[at] = nn(normed, weight_ref[:, 2 * width :]).astype(BF16).reshape(pair, own_len, width)


def halo_kernel(inner_ref, other_ref, weight_ref, gain_ref, angles_ref, normed_ref, keys_ref, values_ref):
    rows, win, width = inner_ref.shape
    pair = 3
    span = angles_ref.shape[1]
    cosine = jnp.concatenate([angles_ref[0, :win], angles_ref[0, span - win :]] * pair)
    sines = jnp.concatenate([angles_ref[1, :win], angles_ref[1, span - win :]] * pair)

    @pl.loop(0, rows // pair)
    def _(i):
        at = pl.ds(i * pair, pair)
        sides = by_side(inner_ref[at], other_ref[at])
        unit, _ = normalize(flat(jnp.concatenate(sides, axis=1)).astype(F32))
        normed = (unit * gain_ref[...]).astype(BF16)
        normed_ref[at] = normed.reshape(pair, 2 * win, width)
        for c in range(0, width, WIDE):
            part = turn(nn(normed, weight_ref[:, width + c : width + c + WIDE]), cosine, sines)
            keys_ref[at, :, c : c + WIDE] = part.astype(BF16).reshape(pair, 2 * win, WIDE)
        values_ref[at] = nn(normed, weight_ref[:, 2 * width :]).astype(BF16).reshape(pair, 2 * win, width)


def bias_of(bounds_ref, row, lanes, first_key, keys):
    key = first_key + iota((keys, LANES), 0)
    first, last = bounds_ref[row, 0:1, lanes], bounds_ref[row, 1:2, lanes]
    return jnp.where((key >= first) & (key <= last), 0.0, -jnp.inf)


def probabilities(scores, bias):
    parts = []
    for c in range(0, scores.shape[1], LANES):
        part = scores[:, c : c + LANES] + bias
        part = jnp.exp(part - jnp.max(part, axis=0, keepdims=True))
        parts.append(part * (1.0 / jnp.sum(part, axis=0, keepdims=True)))
    return jnp.concatenate(parts, axis=1)


def attend_mid_kernel(queries_ref, keys_ref, values_ref, bounds_ref, attended_ref, probs_ref):
    rows, own_len, width = queries_ref.shape
    win = HALF_WIN
    mid = own_len - 2 * win
    start = lax.axis_index("seq") * own_len
    pair = 2

    @pl.loop(0, rows // pair)
    def _(i):
        for r in range(pair):
            row = i * pair + r
            bias = bias_of(bounds_ref, row, slice(0, mid), start, own_len)
            for g in range(width // WIDE):
                cols = slice(g * WIDE, (g + 1) * WIDE)
                probs = probabilities(
                    nt(keys_ref[row, :, cols], by_head(queries_ref[row, win : win + mid, cols], True)), bias
                )
                probs_ref[row, g] = probs
                out = tn(probs.astype(BF16), values_ref[row, :, cols])
                attended_ref[row, :, cols] = pick_heads(out, False).astype(BF16)


def wide_side(own, halo, side):
    win = HALF_WIN
    if side == 0:
        return jnp.concatenate([halo[:win], own[: 2 * win]], axis=0)
    return jnp.concatenate([own[own.shape[0] - 2 * win :], halo[win:]], axis=0)


def attend_out_kernel(
    queries_ref, keys_ref, values_ref, halo_keys_ref, halo_values_ref, bounds_ref, attended_ref, probs_ref
):
    rows, own_len, width = queries_ref.shape
    win = HALF_WIN
    mid = own_len - 2 * win
    start = lax.axis_index("seq") * own_len
    pair = 2

    @pl.loop(0, rows // pair)
    def _(i):
        for r in range(pair):
            row = i * pair + r
            for side in range(2):
                own = slice(0, win) if side == 0 else slice(own_len - win, own_len)
                lanes = slice(mid + side * LANES, mid + (side + 1) * LANES)
                bias = bias_of(bounds_ref, row, lanes, start + own.start - win, 3 * win)
                for g in range(width // WIDE):
                    cols = slice(g * WIDE, (g + 1) * WIDE)
                    keys = wide_side(keys_ref[row, :, cols], halo_keys_ref[row, :, cols], side)
                    values = wide_side(values_ref[row, :, cols], halo_values_ref[row, :, cols], side)
                    probs = probabilities(nt(keys, by_head(queries_ref[row, own, cols], True)), bias)
                    probs_ref[row, side, g] = probs
                    out = tn(probs.astype(BF16), values)
                    attended_ref[row, side * win : (side + 1) * win, cols] = pick_heads(out, False).astype(BF16)


def gelu_parts(gate):
    bell = jnp.exp(-0.5 * gate * gate)
    t = 1.0 / (1.0 + (0.3275911 * 0.7071067811865476) * jnp.abs(gate))
    tail = t * (
        0.5 * 0.254829592
        + t * (0.5 * -0.284496736 + t * (0.5 * 1.421413741 + t * (0.5 * -1.453152027 + t * (0.5 * 1.061405429))))
    )
    tail = tail * bell
    return jnp.where(gate < 0, tail, 1.0 - tail), gate * bell * 0.3989422804014327


def part_of(ref, at, outer):
    own_len, win = ref.shape[1], HALF_WIN
    if outer:
        return flat(jnp.concatenate([ref[at, :win], ref[at, own_len - win :]], axis=1))
    return flat(ref[at, win : own_len - win])


def dense_kernel(
    outer,
    tokens_ref,
    top_ref,
    attended_ref,
    out_ref,
    up_ref,
    down_ref,
    gain_ref,
    middle_ref,
    normed_ref,
    mixed_ref,
    grad_up_ref,
    grad_middle_ref,
    branch_ref,
    grad_attended_ref,
):
    rows, count, width = attended_ref.shape
    hidden = down_ref.shape[0]
    pair = 3

    @pl.loop(0, rows // pair)
    def _(i):
        at = pl.ds(i * pair, pair)

        def put(ref, values, cols=slice(None)):
            ref[at, :, cols] = values.reshape(pair, count, -1)

        top = part_of(top_ref, at, outer)
        middle = part_of(tokens_ref, at, outer).astype(F32) + nn(flat(attended_ref[at]), out_ref[...])
        put(middle_ref, middle)
        unit, inverse = normalize(middle)
        normed = (unit * gain_ref[...]).astype(BF16)
        put(normed_ref, normed)
        for c in range(0, hidden, 256):
            gate = nn(normed, up_ref[:, c : c + 256])
            lift = nn(normed, up_ref[:, hidden + c : hidden + c + 256])
            grad_mixed = nt(top, down_ref[c : c + 256])
            phi, slope = gelu_parts(gate)
            active = gate * phi
            put(mixed_ref, (active * lift).astype(BF16), slice(c, c + 256))
            put(grad_up_ref, (grad_mixed * lift * (phi + slope)).astype(BF16), slice(c, c + 256))
            put(grad_up_ref, (grad_mixed * active).astype(BF16), slice(hidden + c, hidden + c + 256))
        grad_normed = nt(flat(grad_up_ref[at]), up_ref[...])
        grad_middle = top.astype(F32) + norm_back(grad_normed * gain_ref[...], unit, inverse)
        put(grad_middle_ref, grad_middle)
        branch = grad_middle.astype(BF16)
        put(branch_ref, branch)
        put(grad_attended_ref, nt(branch, out_ref[...]).astype(BF16))


def both(mid_ref, out_ref, cols=slice(None)):
    return jnp.concatenate([flat(mid_ref[:, :, cols]), flat(out_ref[:, :, cols])], axis=0)


def store_blocks(keep_ref, send_ref, store):
    seq, dp = lax.axis_index("seq"), lax.axis_index("dp")
    place = (dp % 2) * 16 + (dp // 2) * 8 + (seq % 2) * 4 + (seq // 2) % 4
    for ref, base in ((keep_ref, 0), (send_ref, BLOCKS // 2)):

        @pl.loop(0, BLOCKS // 2)
        def _(i):
            store(ref, i, place ^ (i + base))


def weights_kernel(
    top_ref,
    mid_normed_ref,
    out_normed_ref,
    mid_grad_up_ref,
    out_grad_up_ref,
    mid_mixed_ref,
    out_mixed_ref,
    mid_attended_ref,
    out_attended_ref,
    mid_branch_ref,
    out_branch_ref,
    keep_ref,
    send_ref,
    up_sum,
    out_sum,
    down_sum,
):
    width = top_ref.shape[2]
    everything = slice(0, top_ref.shape[0])
    normed = both(mid_normed_ref, out_normed_ref)
    for c in range(0, up_sum.shape[1], 256):
        cols = slice(c, c + 256)
        up_sum[:, cols] = tn(normed, both(mid_grad_up_ref, out_grad_up_ref, cols)).astype(BF16)
    top = jnp.concatenate([part_of(top_ref, everything, False), part_of(top_ref, everything, True)], axis=0)
    for c in range(0, down_sum.shape[0], 256):
        down_sum[c : c + 256] = tn(both(mid_mixed_ref, out_mixed_ref, slice(c, c + 256)), top)
    out_sum[...] = tn(both(mid_attended_ref, out_attended_ref), both(mid_branch_ref, out_branch_ref)).astype(BF16)
    rows, down_rows = width // BLOCKS, down_sum.shape[0] // BLOCKS

    def store(ref, i, block):
        own = pl.ds(pl.multiple_of(block * rows, rows), rows)
        at = 0
        for c in range(0, up_sum.shape[1], width):
            ref[i, at : at + rows] = up_sum[own, c : c + width]
            at += rows
        ref[i, at : at + rows] = out_sum[own, :]
        at += rows
        ref[i, at:] = down_sum[pl.ds(pl.multiple_of(block * down_rows, down_rows), down_rows), :].astype(BF16)

    store_blocks(keep_ref, send_ref, store)


def attend_back_kernel(
    group,
    queries_ref,
    keys_ref,
    values_ref,
    halo_keys_ref,
    halo_values_ref,
    mid_grad_ref,
    out_grad_ref,
    mid_probs_ref,
    out_probs_ref,
    angles_ref,
    own_ref,
    halo_ref,
):
    rows, own_len, _ = queries_ref.shape
    win = HALF_WIN
    mid = own_len - 2 * win
    cols = slice(group * WIDE, (group + 1) * WIDE)
    cosine, sines = angles_ref[0], angles_ref[1]
    own_cos, own_sin = cosine[win : win + own_len], sines[win : win + own_len]
    halo_cos = jnp.concatenate([cosine[:win], cosine[win + own_len :]])
    halo_sin = jnp.concatenate([sines[:win], sines[win + own_len :]])
    pair = 2

    def unit(queries, keys, values, grads, probs):
        q4, g4 = by_head(queries, True), by_head(grads, False)
        grad_probs = nt(values, g4)
        lows, grad_scores = [], []
        for c in range(0, probs.shape[1], LANES):
            part, grad_part = probs[:, c : c + LANES], grad_probs[:, c : c + LANES]
            inner = jnp.sum(part * grad_part, axis=0, keepdims=True)
            lows.append(part.astype(BF16))
            grad_scores.append((part * (grad_part - inner)).astype(BF16))
        grad_scores = jnp.concatenate(grad_scores, axis=1)
        return (
            pick_heads(tn(grad_scores, keys), True),
            nn(grad_scores, q4),
            nn(jnp.concatenate(lows, axis=1), g4),
        )

    @pl.loop(0, rows // pair)
    def _(i):
        for r in range(pair):
            row = i * pair + r
            queries, keys, values = queries_ref[row, :, cols], keys_ref[row, :, cols], values_ref[row, :, cols]
            halo_keys, halo_values = halo_keys_ref[row, :, cols], halo_values_ref[row, :, cols]
            grads = out_grad_ref[row, :, cols]
            middle = unit(queries[win : win + mid], keys, values, mid_grad_ref[row, :, cols], mid_probs_ref[row, group])
            sides = [
                unit(
                    queries[:win] if side == 0 else queries[own_len - win :],
                    wide_side(keys, halo_keys, side),
                    wide_side(values, halo_values, side),
                    grads[side * win : (side + 1) * win],
                    out_probs_ref[row, side, group],
                )
                for side in range(2)
            ]
            low, high = sides
            own = [jnp.concatenate([low[0], middle[0], high[0]], axis=0) * SCALE]
            halo = []
            for k in (1, 2):
                own.append(middle[k] + jnp.concatenate([low[k][win:], high[k][: 2 * win]], axis=0))
                halo.append(jnp.concatenate([low[k][:win], high[k][2 * win :]], axis=0))
            own_ref[row, :, :WIDE] = turn_back(own[0], own_cos, own_sin).astype(BF16)
            own_ref[row, :, WIDE : 2 * WIDE] = turn_back(own[1], own_cos, own_sin).astype(BF16)
            own_ref[row, :, 2 * WIDE :] = own[2].astype(BF16)
            halo_ref[row, :, :WIDE] = turn_back(halo[0], halo_cos, halo_sin).astype(BF16)
            halo_ref[row, :, WIDE:] = halo[1].astype(BF16)


def weight_in_kernel(normed_ref, halo_normed_ref, *refs):
    *grads, total = refs
    width = normed_ref.shape[2]
    normed, halo_normed = flat(normed_ref[...]), flat(halo_normed_ref[...])
    normed_all = jnp.concatenate([normed, halo_normed], axis=0)
    order = halves_first()
    for g in range(len(grads) // 2):
        own, halo = grads[2 * g : 2 * g + 2]
        for k in range(3):
            part = flat(own[:, :, k * WIDE : (k + 1) * WIDE])
            if k == 0:
                part = tn(normed, part)
            else:
                part = tn(normed_all, jnp.concatenate([part, flat(halo[:, :, (k - 1) * WIDE : k * WIDE])], axis=0))
            part = part.astype(BF16)
            if k < 2:
                part = nt(part, order).astype(BF16)
            total[:, k * width + g * WIDE : k * width + (g + 1) * WIDE] = part


def split_kernel(weight_ref, *refs):
    *halos, total, inner_ref, other_ref, keep_ref, send_ref = refs
    grad_halo_kernel(weight_ref, *halos, inner_ref, other_ref)
    rows, width = total.shape[0] // BLOCKS, total.shape[0]

    def store(ref, i, block):
        own = pl.ds(pl.multiple_of(block * rows, rows), rows)
        for k in range(3):
            ref[i, k * rows : (k + 1) * rows] = total[own, k * width : (k + 1) * width]

    store_blocks(keep_ref, send_ref, store)


def grad_halo_kernel(weight_ref, *refs):
    *grads, inner_ref, other_ref = refs
    rows, win, width = inner_ref.shape
    total = None
    for g, ref in enumerate(grads):
        weight = jnp.concatenate(
            [weight_ref[:, k * width + g * WIDE : k * width + (g + 1) * WIDE] for k in (1, 2)], axis=1
        )
        part = nt(flat(ref[...]), weight)
        total = part if total is None else total + part
    total = total.astype(BF16).reshape(rows, 2 * win, width)
    inner_ref[...], other_ref[...] = by_side(total[:, :win], total[:, win:])


def backward_kernel(*refs):
    shared, (normed_ref, halo_normed_ref), (*grads, total) = refs[:10], refs[10:12], refs[12:]
    for group in range(len(grads) // 2):
        attend_back_kernel(group, *shared, *grads[2 * group : 2 * group + 2])
    weight_in_kernel(normed_ref, halo_normed_ref, *grads, total)


def grad_own_kernel(weight_ref, *refs):
    *grads, out_ref = refs
    rows, own_len, width = out_ref.shape
    pair = 2
    groups = len(grads)

    @pl.loop(0, rows // pair)
    def _(i):
        at = pl.ds(i * pair, pair)
        grad = jnp.concatenate([flat(ref[at]) for ref in grads], axis=1)
        weight = jnp.concatenate(
            [
                weight_ref[:, k * width + g * WIDE : k * width + (g + 1) * WIDE]
                for g in range(groups)
                for k in range(3)
            ],
            axis=1,
        )
        out_ref[at] = nt(grad, weight).reshape(pair, own_len, width)


def result_kernel(mid_middle_ref, out_middle_ref, mid_mixed_ref, out_mixed_ref, down_ref, result_ref):
    own_len, win = result_ref.shape[1], HALF_WIN
    pair = 3

    @pl.loop(0, result_ref.shape[0] // pair)
    def _(i):
        at = pl.ds(i * pair, pair)

        def result(middle_ref, mixed_ref):
            total = flat(middle_ref[at]) + nn(flat(mixed_ref[at]), down_ref[...])
            return total.astype(BF16).reshape(middle_ref[at].shape)

        result_ref[at, win : own_len - win] = result(mid_middle_ref, mid_mixed_ref)
        outer = result(out_middle_ref, out_mixed_ref)
        result_ref[at, :win] = outer[:, :win]
        result_ref[at, own_len - win :] = outer[:, win:]


def finish_kernel(
    tokens_ref, own_ref, inner_ref, other_ref, mid_grad_ref, out_grad_ref, gain_ref, grad_ref
):
    own_len, win = tokens_ref.shape[1], HALF_WIN

    @pl.loop(0, tokens_ref.shape[0])
    def _(row):
        unit, inverse = normalize(tokens_ref[row].astype(F32))
        own = own_ref[row]
        low, high = by_side(inner_ref[row].astype(F32), other_ref[row].astype(F32))
        grads = jnp.concatenate(
            [own[:win] + low, own[win : own_len - win], own[own_len - win :] + high],
            axis=0,
        )
        outer = out_grad_ref[row]
        middle = jnp.concatenate([outer[:win], mid_grad_ref[row], outer[win:]], axis=0)
        grad_ref[row] = middle + norm_back(grads * gain_ref[...], unit, inverse)


def place_kernel(own_ref, other_ref, weight_ref, gain_ref, *out_refs):
    *out_refs, gain_grad_ref = out_refs

    def store(ref, i, block):
        at = 0
        for out in out_refs:
            rows = out.shape[0] // BLOCKS
            for c in range(0, out.shape[1], ref.shape[2]):
                out[pl.ds(pl.multiple_of(block * rows, rows), rows), c : c + ref.shape[2]] = ref[
                    i, at : at + rows
                ].astype(F32)
                at += rows

    store_blocks(own_ref, other_ref, store)
    total = None
    for c in range(0, weight_ref.shape[1], LANES):
        part = out_refs[0][:, c : c + LANES] * weight_ref[:, c : c + LANES].astype(F32)
        total = part if total is None else total + part
    gain_grad_ref[...] = jnp.sum(total.T, axis=0, keepdims=True) / gain_ref[...]


def add_kernel(count, *refs):
    parts, outs = refs[:count], refs[count:]
    if len(outs) == 1:
        outs[0][...] = sum(p[...].astype(F32) for p in parts).astype(BF16)
        return
    size = parts[0].shape[0] // len(outs)
    for k, out in enumerate(outs):
        at = slice(k * size, (k + 1) * size) if len(out.shape) == len(parts[0].shape) else k
        out[...] = sum(p[at].astype(F32) for p in parts).astype(BF16)


def join_kernel(*refs):
    *parts, out = refs
    if len(out.shape) > len(parts[0].shape):
        for k, part in enumerate(parts):
            out[k] = part[...]
    else:
        size = parts[0].shape[0]
        for k, part in enumerate(parts):
            out[k * size : (k + 1) * size] = part[...]


def to_neighbours(inner, other):
    size = lax.axis_size("seq")
    pairs = [(i, i ^ 1) for i in range(size)]
    between = [p for i in range(1, size - 1, 2) for p in ((i, i + 1), (i + 1, i))]
    return lax.ppermute(inner, "seq", pairs), lax.ppermute(other, "seq", between)


def swap_route(core, x, y, z, rest):
    dp, seq = lax.axis_size("dp"), lax.axis_size("seq")

    def partner(i):
        d, s = divmod(i, seq)
        return (d ^ (core + 2 * x)) * seq + (s ^ (y + 2 * z + 8 * rest))

    return [(i, partner(i)) for i in range(dp * seq)]


def swap(values, core=0, x=0, y=0, z=0, rest=0):
    return lax.ppermute(values, ("dp", "seq"), swap_route(core, x, y, z, rest))


def shape(*dims, kind=BF16):
    return jax.ShapeDtypeStruct(dims, kind)


def call(name, kernel, outs, *args, after=(), grant=6, flops=1e9, scratch=()):
    spec = pl.BlockSpec(memory_space=pltpu.VMEM)
    moved = sum(int(np.prod(a.shape)) * a.dtype.itemsize for a in (*args, *outs))

    def body(*refs):
        return kernel(*refs[len(after) :])

    return pl.pallas_call(
        body,
        out_shape=outs,
        in_specs=[pl.BlockSpec(memory_space=pl.ANY)] * len(after) + [spec] * len(args),
        out_specs=[spec] * len(outs),
        scratch_shapes=scratch,
        compiler_params=pltpu.CompilerParams(vmem_limit_bytes=grant * MB),
        cost_estimate=pl.CostEstimate(flops=int(flops), bytes_accessed=moved, transcendentals=0),
        name=name,
    )(*after, *args)


def add_up(parts, outs, after=()):
    return call("add", functools.partial(add_kernel, len(parts)), outs, *parts, after=after, grant=4, flops=1e6)


def join(parts, stacked, after=()):
    size = parts[0].shape
    out = shape(len(parts), *size) if stacked else shape(len(parts) * size[0], *size[1:])
    return call("join", join_kernel, [out], *parts, after=after, grant=4, flops=1e6)[0]


def swap_plane(parts):
    return [swap(parts[k], x=k >> 1, y=k & 1) for k in (1, 2, 3)]


def swap_line(parts):
    return [swap(parts[k], z=k) for k in (1, 2, 3)]


def swap_rest(own):
    rest = 1
    while 8 * rest < lax.axis_size("seq"):
        (own,) = add_up([own, swap(own, rest=rest)], [shape(*own.shape)])
        rest *= 2
    return own


def angle_tables(own_len, pieces):
    inverse = ROTARY_BASE ** (-(np.arange(0, HEAD_DIM, 2) / HEAD_DIM))
    inverse = np.tile(inverse, LANES // HALF)
    base = np.arange(pieces)[:, None] * own_len * inverse
    local = (np.arange(own_len + 2 * HALF_WIN) - HALF_WIN)[:, None] * inverse
    return [jnp.asarray(np.stack([np.cos(a), np.sin(a)], axis=d), F32) for a, d in ((base, 1), (local, 0))]


def shards(
    tokens,
    document_starts,
    attention_in,
    attention_out,
    feedforward_in,
    feedforward_out,
    gain_first,
    gain_second,
    result_grad,
):
    rows, own_len, width = tokens.shape
    hidden = feedforward_out.shape[0]
    win = HALF_WIN
    mid = own_len - 2 * win
    seq = lax.axis_size("seq")
    groups = width // WIDE
    gain_one, gain_two = gain_first[None], gain_second[None]

    loaded = [tokens, document_starts, attention_in, gain_one, *angle_tables(own_len, seq)]
    outs = [pltpu.VMEM(a.shape, a.dtype) for a in loaded] + [pltpu.VMEM((rows, win, width), BF16)] * 2
    tokens, document_starts, attention_in, gain_one, *tables, inner_tokens, other_tokens = pl.pallas_call(
        functools.partial(load_kernel, len(loaded)),
        out_shape=outs,
        in_specs=[pl.BlockSpec(memory_space=pltpu.HBM)] * len(loaded),
        out_specs=[pl.BlockSpec(memory_space=pltpu.VMEM)] * len(outs),
        scratch_shapes=[pltpu.SemaphoreType.DMA((len(outs),))],
        compiler_params=pltpu.CompilerParams(vmem_limit_bytes=MB),
        name="load",
    )(*[pltpu.with_memory_space_constraint(a, pltpu.HBM) for a in loaded])
    inner_halo, other_halo = to_neighbours(inner_tokens, other_tokens)

    row_shape = shape(rows, own_len, width)
    normed, queries, keys, values, weight, angles, bounds = call(
        "project",
        project_kernel,
        [row_shape] * 4
        + [
            shape(*attention_in.shape),
            shape(2, own_len + 2 * win, LANES, kind=F32),
            shape(rows, 2, mid + 4 * win, kind=jnp.int32),
        ],
        tokens,
        document_starts,
        attention_in,
        gain_one,
        *tables,
        flops=3e9,
    )
    mid_attended, mid_probs = call(
        "attend_mid",
        attend_mid_kernel,
        [shape(rows, mid, width), shape(rows, groups, own_len, GROUP * mid, kind=F32)],
        queries,
        keys,
        values,
        bounds,
        flops=2e9,
    )

    def dense(name, outer, attended):
        count = attended.shape[1]
        return call(
            name,
            functools.partial(dense_kernel, outer),
            [
                shape(rows, count, width, kind=F32),
                shape(rows, count, width),
                shape(rows, count, hidden),
                shape(rows, count, 2 * hidden),
                shape(rows, count, width, kind=F32),
                shape(rows, count, width),
                shape(rows, count, width),
            ],
            tokens,
            result_grad,
            attended,
            attention_out,
            feedforward_in,
            feedforward_out,
            gain_two,
            flops=5e9,
        )

    mid_middle, mid_normed, mid_mixed, mid_grad_up, mid_grad, mid_branch, mid_grad_attended = dense(
        "dense_mid", False, mid_attended
    )

    halo_normed, halo_keys, halo_values = call(
        "halo",
        halo_kernel,
        [shape(rows, 2 * win, width)] * 3,
        inner_halo,
        other_halo,
        weight,
        gain_one,
        angles,
        flops=1e9,
    )
    out_attended, out_probs = call(
        "attend_out",
        attend_out_kernel,
        [shape(rows, 2 * win, width), shape(rows, 2, groups, 3 * win, GROUP * win, kind=F32)],
        queries,
        keys,
        values,
        halo_keys,
        halo_values,
        bounds,
        flops=2e9,
    )
    out_middle, out_normed, out_mixed, out_grad_up, out_grad, out_branch, out_grad_attended = dense(
        "dense_out", True, out_attended
    )

    piece = (feedforward_in.shape[1] // width * width + width + hidden) // BLOCKS
    keep_one, send_one = call(
        "weights",
        weights_kernel,
        [shape(BLOCKS // 2, piece, width)] * 2,
        result_grad,
        mid_normed,
        out_normed,
        mid_grad_up,
        out_grad_up,
        mid_mixed,
        out_mixed,
        mid_attended,
        out_attended,
        mid_branch,
        out_branch,
        flops=5e9,
        scratch=[
            pltpu.VMEM(feedforward_in.shape, BF16),
            pltpu.VMEM(attention_out.shape, BF16),
            pltpu.VMEM(feedforward_out.shape, F32),
        ],
    )

    def cut(blocks, parts, stacked=False):
        if stacked:
            return [shape(*blocks.shape[1:])] * parts
        return [shape(blocks.shape[0] // parts, *blocks.shape[1:])] * parts

    (activations,) = call(
        "result",
        result_kernel,
        [row_shape],
        mid_middle,
        out_middle,
        mid_mixed,
        out_mixed,
        feedforward_out,
        flops=2e9,
        after=[keep_one],
    )
    chip_one = add_up([keep_one, swap(send_one, core=1)], cut(keep_one, 4), after=[activations])
    from_plane = swap_plane(chip_one)
    grad_shapes = [shape(rows, own_len, 3 * WIDE), shape(rows, 2 * win, 2 * WIDE)] * groups
    *grads, total_in = call(
        "backward",
        backward_kernel,
        [shape(rows, own_len, 3 * WIDE), shape(rows, 2 * win, 2 * WIDE)] * groups + [shape(*attention_in.shape)],
        queries,
        keys,
        values,
        halo_keys,
        halo_values,
        mid_grad_attended,
        out_grad_attended,
        mid_probs,
        out_probs,
        angles,
        normed,
        halo_normed,
        flops=16e9,
        after=[chip_one[0]],
    )
    plane_one = add_up([chip_one[0], *from_plane], cut(chip_one[0], 4, True), after=[total_in])
    from_line = swap_line(plane_one)
    inner_grad, other_grad, keep_two, send_two = call(
        "split",
        split_kernel,
        [shape(rows, win, width)] * 2 + [shape(BLOCKS // 2, attention_in.shape[1] // BLOCKS, width)] * 2,
        weight,
        *grads[1::2],
        total_in,
        flops=1e9,
        after=[plane_one[0]],
    )
    from_core_two = swap(send_two, core=1)
    inner_grad, other_grad = to_neighbours(inner_grad, other_grad)
    (own_grad,) = call(
        "grad_own",
        grad_own_kernel,
        [shape(rows, own_len, width, kind=F32)],
        weight,
        *grads[::2],
        flops=2e9,
        after=[keep_two],
    )
    chip_two = add_up([keep_two, from_core_two], cut(keep_two, 4), after=[own_grad])
    from_plane = swap_plane(chip_two)
    (line_one,) = add_up([plane_one[0], *from_line], cut(plane_one[0], 1), after=[chip_two[0]])
    line_one = swap_rest(line_one)
    plane_two = add_up([chip_two[0], *from_plane], cut(chip_two[0], 4, True))
    line_one = join([line_one, *swap_line([line_one] * 4)], True, after=[plane_two[0], inner_grad, other_grad])
    from_line = swap_line(plane_two)
    from_plane = swap_plane([line_one] * 4)
    (grad_tokens,) = call(
        "finish",
        finish_kernel,
        [shape(rows, own_len, width, kind=F32)],
        tokens,
        own_grad,
        inner_grad,
        other_grad,
        mid_grad,
        out_grad,
        gain_one,
        flops=1e8,
        after=[line_one],
    )
    (line_two,) = add_up([plane_two[0], *from_line], cut(plane_two[0], 1))
    line_two = swap_rest(line_two)
    line_two = join([line_two, *swap_line([line_two] * 4)], True)
    from_plane_two = swap_plane([line_two] * 4)
    whole_one = join([line_one, *from_plane], False, after=[line_two, grad_tokens])

    def placed(parts, gain, *weights):
        outs = [shape(*w.shape, kind=F32) for w in weights] + [shape(1, width, kind=F32)]
        return call("place", place_kernel, outs, *parts, weights[0], gain, flops=1e6)

    grad_up, grad_out, grad_down, grad_gain_two = placed(
        (whole_one, swap(whole_one, core=1)), gain_two, feedforward_in, attention_out, feedforward_out
    )
    whole_two = join([line_two, *from_plane_two], False, after=[grad_gain_two])
    grad_in, grad_gain_one = placed((whole_two, swap(whole_two, core=1)), gain_one, attention_in)
    return activations, grad_tokens, grad_in, grad_out, grad_up, grad_down, grad_gain_one[0], grad_gain_two[0]


def solution(mesh):
    token, rest = P("dp", "seq", None), P()
    return jax.shard_map(
        shards,
        mesh=mesh,
        in_specs=(token, P("dp", None)) + (rest,) * 6 + (token,),
        out_specs=(token, token) + (rest,) * 6,
        check_vma=False,
    )
```

```python
import functools

import jax
import jax.numpy as jnp
import numpy as np
from jax import lax
from jax.experimental import pallas as pl
from jax.experimental.pallas import tpu as pltpu
from jax.sharding import PartitionSpec as P

HEADS = 8
HEAD_DIM = 64
HALF = HEAD_DIM // 2
HALF_WIN = 64
EPSILON = 1e-05
ROTARY_BASE = 10000.0
SCALE = HEAD_DIM**-0.5
BLOCKS = 32
GROUP = 4
WIDE = GROUP * HEAD_DIM
LANES = 128
MB = 1024 * 1024

F32 = jnp.float32
BF16 = jnp.bfloat16


def dot(a, b, contract):
    return lax.dot_general(a, b, ((contract[:1], contract[1:]), ((), ())), preferred_element_type=F32)


def nn(a, b):
    return dot(a, b, (1, 0))


def nt(a, b):
    return dot(a, b, (1, 1))


def tn(a, b):
    return dot(a, b, (0, 0))


def iota(shape, dim):
    return lax.broadcasted_iota(jnp.int32, shape, dim)


def flat(values):
    return values.reshape(-1, values.shape[-1])


def normalize(values):
    shifted = values - jnp.mean(values, axis=-1, keepdims=True)
    inverse = lax.rsqrt(jnp.mean(shifted * shifted, axis=-1, keepdims=True) + EPSILON)
    return shifted * inverse, inverse


def norm_back(scaled_grad, unit, inverse):
    return (
        scaled_grad
        - jnp.mean(scaled_grad, axis=-1, keepdims=True)
        - unit * jnp.mean(scaled_grad * unit, axis=-1, keepdims=True)
    ) * inverse


def halves_first():
    old, new = iota((WIDE, WIDE), 0), iota((WIDE, WIDE), 1)
    moved = (old % HEAD_DIM) // HALF * LANES + old // HEAD_DIM * HALF + old % HALF
    return (moved == new).astype(BF16)


def head_of(shape, halved):
    lane = iota(shape, 1)
    return lane % LANES // HALF if halved else lane // HEAD_DIM


def by_head(values, halved):
    head = head_of(values.shape, halved)
    zero = jnp.zeros_like(values)
    return jnp.concatenate([jnp.where(head == h, values, zero) for h in range(GROUP)], axis=0)


def pick_heads(stacked, halved):
    count = stacked.shape[0] // GROUP
    head = head_of((count, stacked.shape[1]), halved)
    out = stacked[:count]
    for h in range(1, GROUP):
        out = jnp.where(head == h, stacked[h * count : (h + 1) * count], out)
    return out


def turn(values, cosine, sines):
    first, second = values[:, :LANES], values[:, LANES:]
    return jnp.concatenate([first * cosine - second * sines, second * cosine + first * sines], axis=1)


def turn_back(values, cosine, sines):
    first, second = values[:, :LANES], values[:, LANES:]
    return jnp.concatenate([first * cosine + second * sines, second * cosine - first * sines], axis=1)


def load_kernel(count, *refs):
    sources, outs, sems = refs[:count], refs[count:-1], refs[-1]
    own_len, win = sources[0].shape[1], HALF_WIN
    odd = lax.axis_index("seq") % 2
    copies = []
    for k, out in enumerate(outs):
        source = sources[0] if k >= count else sources[k]
        if k >= count:
            high = odd == 0 if k == count else odd == 1
            at = pl.multiple_of(jnp.where(high, own_len - win, 0), win)
            source = source.at[:, pl.ds(at, win)]
        copies.append(pltpu.make_async_copy(source, out, sems.at[k]))
    for copy in copies:
        copy.start()
    for copy in copies:
        copy.wait()


def by_side(inner, other):
    odd = lax.axis_index("seq") % 2 == 1
    return jnp.where(odd, inner, other), jnp.where(odd, other, inner)


def project_kernel(
    tokens_ref,
    starts_ref,
    in_ref,
    gain_ref,
    base_ref,
    table_ref,
    normed_ref,
    queries_ref,
    keys_ref,
    values_ref,
    weight_ref,
    angles_ref,
    bounds_ref,
):
    rows, own_len, width = tokens_ref.shape
    win = HALF_WIN
    place = lax.axis_index("seq")
    start = place * own_len
    row_len = own_len * lax.axis_size("seq")

    base_cos, base_sin = base_ref[place, 0:1], base_ref[place, 1:2]
    angles_ref[0] = base_cos * table_ref[0] - base_sin * table_ref[1]
    angles_ref[1] = base_sin * table_ref[0] + base_cos * table_ref[1]

    lane = iota((rows, own_len - 2 * win + 4 * win), 1)
    mid = own_len - 2 * win
    pos = start + jnp.where(
        lane < mid, lane + win, jnp.where(lane < mid + 2 * win, lane % win, own_len - win + lane % win)
    )
    first, last = jnp.maximum(pos - win, 0), jnp.minimum(pos + win, row_len - 1)
    for j in range(starts_ref.shape[1]):
        cut = starts_ref[:, j : j + 1]
        first = jnp.maximum(first, jnp.where(cut <= pos, cut, 0))
        last = jnp.minimum(last, jnp.where(cut > pos, cut - 1, row_len))
    for r in range(rows):
        bounds_ref[r, 0:1] = first[r : r + 1]
        bounds_ref[r, 1:2] = last[r : r + 1]

    order = halves_first()
    for c in range(0, 2 * width, WIDE):
        weight_ref[:, c : c + WIDE] = nn(in_ref[:, c : c + WIDE], order).astype(BF16)
    weight_ref[:, 2 * width :] = in_ref[:, 2 * width :]

    pair = 2
    cosine, sines = angles_ref[0, win : win + own_len], angles_ref[1, win : win + own_len]
    cosine, sines = jnp.concatenate([cosine] * pair), jnp.concatenate([sines] * pair)

    @pl.loop(0, rows // pair)
    def _(i):
        at = pl.ds(i * pair, pair)
        unit, _ = normalize(flat(tokens_ref[at]).astype(F32))
        normed = (unit * gain_ref[...]).astype(BF16)
        normed_ref[at] = normed.reshape(pair, own_len, width)
        for c in range(0, width, WIDE):
            part = turn(nn(normed, weight_ref[:, c : c + WIDE]), cosine * SCALE, sines * SCALE)
            queries_ref[at, :, c : c + WIDE] = part.astype(BF16).reshape(pair, own_len, WIDE)
            part = turn(nn(normed, weight_ref[:, width + c : width + c + WIDE]), cosine, sines)
            keys_ref[at, :, c : c + WIDE] = part.astype(BF16).reshape(pair, own_len, WIDE)
        values_ref[at] = nn(normed, weight_ref[:, 2 * width :]).astype(BF16).reshape(pair, own_len, width)


def halo_kernel(inner_ref, other_ref, weight_ref, gain_ref, angles_ref, normed_ref, keys_ref, values_ref):
    rows, win, width = inner_ref.shape
    pair = 3
    span = angles_ref.shape[1]
    cosine = jnp.concatenate([angles_ref[0, :win], angles_ref[0, span - win :]] * pair)
    sines = jnp.concatenate([angles_ref[1, :win], angles_ref[1, span - win :]] * pair)

    @pl.loop(0, rows // pair)
    def _(i):
        at = pl.ds(i * pair, pair)
        sides = by_side(inner_ref[at], other_ref[at])
        unit, _ = normalize(flat(jnp.concatenate(sides, axis=1)).astype(F32))
        normed = (unit * gain_ref[...]).astype(BF16)
        normed_ref[at] = normed.reshape(pair, 2 * win, width)
        for c in range(0, width, WIDE):
            part = turn(nn(normed, weight_ref[:, width + c : width + c + WIDE]), cosine, sines)
            keys_ref[at, :, c : c + WIDE] = part.astype(BF16).reshape(pair, 2 * win, WIDE)
        values_ref[at] = nn(normed, weight_ref[:, 2 * width :]).astype(BF16).reshape(pair, 2 * win, width)


def bias_of(bounds_ref, row, lanes, first_key, keys):
    key = first_key + iota((keys, LANES), 0)
    first, last = bounds_ref[row, 0:1, lanes], bounds_ref[row, 1:2, lanes]
    return jnp.where((key >= first) & (key <= last), 0.0, -jnp.inf)


def probabilities(scores, bias):
    parts = []
    for c in range(0, scores.shape[1], LANES):
        part = scores[:, c : c + LANES] + bias
        part = jnp.exp(part - jnp.max(part, axis=0, keepdims=True))
        parts.append(part * (1.0 / jnp.sum(part, axis=0, keepdims=True)))
    return jnp.concatenate(parts, axis=1)


def attend_mid_kernel(queries_ref, keys_ref, values_ref, bounds_ref, attended_ref, probs_ref):
    rows, own_len, width = queries_ref.shape
    win = HALF_WIN
    mid = own_len - 2 * win
    start = lax.axis_index("seq") * own_len
    pair = 2

    @pl.loop(0, rows // pair)
    def _(i):
        for r in range(pair):
            row = i * pair + r
            bias = bias_of(bounds_ref, row, slice(0, mid), start, own_len)
            for g in range(width // WIDE):
                cols = slice(g * WIDE, (g + 1) * WIDE)
                probs = probabilities(
                    nt(keys_ref[row, :, cols], by_head(queries_ref[row, win : win + mid, cols], True)), bias
                )
                probs_ref[row, g] = probs
                out = tn(probs.astype(BF16), values_ref[row, :, cols])
                attended_ref[row, :, cols] = pick_heads(out, False).astype(BF16)


def wide_side(own, halo, side):
    win = HALF_WIN
    if side == 0:
        return jnp.concatenate([halo[:win], own[: 2 * win]], axis=0)
    return jnp.concatenate([own[own.shape[0] - 2 * win :], halo[win:]], axis=0)


def attend_out_kernel(
    queries_ref, keys_ref, values_ref, halo_keys_ref, halo_values_ref, bounds_ref, attended_ref, probs_ref
):
    rows, own_len, width = queries_ref.shape
    win = HALF_WIN
    mid = own_len - 2 * win
    start = lax.axis_index("seq") * own_len
    pair = 2

    @pl.loop(0, rows // pair)
    def _(i):
        for r in range(pair):
            row = i * pair + r
            for side in range(2):
                own = slice(0, win) if side == 0 else slice(own_len - win, own_len)
                lanes = slice(mid + side * LANES, mid + (side + 1) * LANES)
                bias = bias_of(bounds_ref, row, lanes, start + own.start - win, 3 * win)
                for g in range(width // WIDE):
                    cols = slice(g * WIDE, (g + 1) * WIDE)
                    keys = wide_side(keys_ref[row, :, cols], halo_keys_ref[row, :, cols], side)
                    values = wide_side(values_ref[row, :, cols], halo_values_ref[row, :, cols], side)
                    probs = probabilities(nt(keys, by_head(queries_ref[row, own, cols], True)), bias)
                    probs_ref[row, side, g] = probs
                    out = tn(probs.astype(BF16), values)
                    attended_ref[row, side * win : (side + 1) * win, cols] = pick_heads(out, False).astype(BF16)


def gelu_parts(gate):
    bell = jnp.exp(-0.5 * gate * gate)
    t = 1.0 / (1.0 + (0.3275911 * 0.7071067811865476) * jnp.abs(gate))
    tail = t * (
        0.5 * 0.254829592
        + t * (0.5 * -0.284496736 + t * (0.5 * 1.421413741 + t * (0.5 * -1.453152027 + t * (0.5 * 1.061405429))))
    )
    tail = tail * bell
    return jnp.where(gate < 0, tail, 1.0 - tail), gate * bell * 0.3989422804014327


def part_of(ref, at, outer):
    own_len, win = ref.shape[1], HALF_WIN
    if outer:
        return flat(jnp.concatenate([ref[at, :win], ref[at, own_len - win :]], axis=1))
    return flat(ref[at, win : own_len - win])


def dense_kernel(
    outer,
    tokens_ref,
    top_ref,
    attended_ref,
    out_ref,
    up_ref,
    down_ref,
    gain_ref,
    middle_ref,
    normed_ref,
    mixed_ref,
    grad_up_ref,
    grad_middle_ref,
    branch_ref,
    grad_attended_ref,
):
    rows, count, width = attended_ref.shape
    hidden = down_ref.shape[0]
    pair = 3

    @pl.loop(0, rows // pair)
    def _(i):
        at = pl.ds(i * pair, pair)

        def put(ref, values, cols=slice(None)):
            ref[at, :, cols] = values.reshape(pair, count, -1)

        top = part_of(top_ref, at, outer)
        middle = part_of(tokens_ref, at, outer).astype(F32) + nn(flat(attended_ref[at]), out_ref[...])
        put(middle_ref, middle)
        unit, inverse = normalize(middle)
        normed = (unit * gain_ref[...]).astype(BF16)
        put(normed_ref, normed)
        for c in range(0, hidden, 256):
            gate = nn(normed, up_ref[:, c : c + 256])
            lift = nn(normed, up_ref[:, hidden + c : hidden + c + 256])
            grad_mixed = nt(top, down_ref[c : c + 256])
            phi, slope = gelu_parts(gate)
            active = gate * phi
            put(mixed_ref, (active * lift).astype(BF16), slice(c, c + 256))
            put(grad_up_ref, (grad_mixed * lift * (phi + slope)).astype(BF16), slice(c, c + 256))
            put(grad_up_ref, (grad_mixed * active).astype(BF16), slice(hidden + c, hidden + c + 256))
        grad_normed = nt(flat(grad_up_ref[at]), up_ref[...])
        grad_middle = top.astype(F32) + norm_back(grad_normed * gain_ref[...], unit, inverse)
        put(grad_middle_ref, grad_middle)
        branch = grad_middle.astype(BF16)
        put(branch_ref, branch)
        put(grad_attended_ref, nt(branch, out_ref[...]).astype(BF16))


def both(mid_ref, out_ref, cols=slice(None)):
    return jnp.concatenate([flat(mid_ref[:, :, cols]), flat(out_ref[:, :, cols])], axis=0)


def store_blocks(keep_ref, send_ref, store):
    seq, dp = lax.axis_index("seq"), lax.axis_index("dp")
    place = (dp % 2) * 16 + (dp // 2) * 8 + (seq % 2) * 4 + (seq // 2) % 2 * 2 + (seq // 4) % 2
    for ref, base in ((keep_ref, 0), (send_ref, BLOCKS // 2)):

        @pl.loop(0, BLOCKS // 2)
        def _(i):
            store(ref, i, place ^ (i + base))


def weights_kernel(
    top_ref,
    mid_normed_ref,
    out_normed_ref,
    mid_grad_up_ref,
    out_grad_up_ref,
    mid_mixed_ref,
    out_mixed_ref,
    mid_attended_ref,
    out_attended_ref,
    mid_branch_ref,
    out_branch_ref,
    keep_ref,
    send_ref,
    up_sum,
    out_sum,
    down_sum,
):
    width = top_ref.shape[2]
    everything = slice(0, top_ref.shape[0])
    normed = both(mid_normed_ref, out_normed_ref)
    for c in range(0, up_sum.shape[1], 256):
        cols = slice(c, c + 256)
        up_sum[:, cols] = tn(normed, both(mid_grad_up_ref, out_grad_up_ref, cols)).astype(BF16)
    top = jnp.concatenate([part_of(top_ref, everything, False), part_of(top_ref, everything, True)], axis=0)
    for c in range(0, down_sum.shape[0], 256):
        down_sum[c : c + 256] = tn(both(mid_mixed_ref, out_mixed_ref, slice(c, c + 256)), top)
    out_sum[...] = tn(both(mid_attended_ref, out_attended_ref), both(mid_branch_ref, out_branch_ref)).astype(BF16)
    rows, down_rows = width // BLOCKS, down_sum.shape[0] // BLOCKS

    def store(ref, i, block):
        own = pl.ds(pl.multiple_of(block * rows, rows), rows)
        at = 0
        for c in range(0, up_sum.shape[1], width):
            ref[i, at : at + rows] = up_sum[own, c : c + width]
            at += rows
        ref[i, at : at + rows] = out_sum[own, :]
        at += rows
        ref[i, at:] = down_sum[pl.ds(pl.multiple_of(block * down_rows, down_rows), down_rows), :].astype(BF16)

    store_blocks(keep_ref, send_ref, store)


def attend_back_kernel(
    group,
    queries_ref,
    keys_ref,
    values_ref,
    halo_keys_ref,
    halo_values_ref,
    mid_grad_ref,
    out_grad_ref,
    mid_probs_ref,
    out_probs_ref,
    angles_ref,
    own_ref,
    halo_ref,
):
    rows, own_len, _ = queries_ref.shape
    win = HALF_WIN
    mid = own_len - 2 * win
    cols = slice(group * WIDE, (group + 1) * WIDE)
    cosine, sines = angles_ref[0], angles_ref[1]
    own_cos, own_sin = cosine[win : win + own_len], sines[win : win + own_len]
    halo_cos = jnp.concatenate([cosine[:win], cosine[win + own_len :]])
    halo_sin = jnp.concatenate([sines[:win], sines[win + own_len :]])
    pair = 2

    def unit(queries, keys, values, grads, probs):
        q4, g4 = by_head(queries, True), by_head(grads, False)
        grad_probs = nt(values, g4)
        lows, grad_scores = [], []
        for c in range(0, probs.shape[1], LANES):
            part, grad_part = probs[:, c : c + LANES], grad_probs[:, c : c + LANES]
            inner = jnp.sum(part * grad_part, axis=0, keepdims=True)
            lows.append(part.astype(BF16))
            grad_scores.append((part * (grad_part - inner)).astype(BF16))
        grad_scores = jnp.concatenate(grad_scores, axis=1)
        return (
            pick_heads(tn(grad_scores, keys), True),
            nn(grad_scores, q4),
            nn(jnp.concatenate(lows, axis=1), g4),
        )

    @pl.loop(0, rows // pair)
    def _(i):
        for r in range(pair):
            row = i * pair + r
            queries, keys, values = queries_ref[row, :, cols], keys_ref[row, :, cols], values_ref[row, :, cols]
            halo_keys, halo_values = halo_keys_ref[row, :, cols], halo_values_ref[row, :, cols]
            grads = out_grad_ref[row, :, cols]
            middle = unit(queries[win : win + mid], keys, values, mid_grad_ref[row, :, cols], mid_probs_ref[row, group])
            sides = [
                unit(
                    queries[:win] if side == 0 else queries[own_len - win :],
                    wide_side(keys, halo_keys, side),
                    wide_side(values, halo_values, side),
                    grads[side * win : (side + 1) * win],
                    out_probs_ref[row, side, group],
                )
                for side in range(2)
            ]
            low, high = sides
            own = [jnp.concatenate([low[0], middle[0], high[0]], axis=0) * SCALE]
            halo = []
            for k in (1, 2):
                own.append(middle[k] + jnp.concatenate([low[k][win:], high[k][: 2 * win]], axis=0))
                halo.append(jnp.concatenate([low[k][:win], high[k][2 * win :]], axis=0))
            own_ref[row, :, :WIDE] = turn_back(own[0], own_cos, own_sin).astype(BF16)
            own_ref[row, :, WIDE : 2 * WIDE] = turn_back(own[1], own_cos, own_sin).astype(BF16)
            own_ref[row, :, 2 * WIDE :] = own[2].astype(BF16)
            halo_ref[row, :, :WIDE] = turn_back(halo[0], halo_cos, halo_sin).astype(BF16)
            halo_ref[row, :, WIDE:] = halo[1].astype(BF16)


def weight_in_kernel(normed_ref, halo_normed_ref, *refs):
    *grads, total = refs
    width = normed_ref.shape[2]
    normed, halo_normed = flat(normed_ref[...]), flat(halo_normed_ref[...])
    normed_all = jnp.concatenate([normed, halo_normed], axis=0)
    order = halves_first()
    for g in range(len(grads) // 2):
        own, halo = grads[2 * g : 2 * g + 2]
        for k in range(3):
            part = flat(own[:, :, k * WIDE : (k + 1) * WIDE])
            if k == 0:
                part = tn(normed, part)
            else:
                part = tn(normed_all, jnp.concatenate([part, flat(halo[:, :, (k - 1) * WIDE : k * WIDE])], axis=0))
            part = part.astype(BF16)
            if k < 2:
                part = nt(part, order).astype(BF16)
            total[:, k * width + g * WIDE : k * width + (g + 1) * WIDE] = part


def split_kernel(total_ref, keep_ref, send_ref):
    rows, width = total_ref.shape[0] // BLOCKS, total_ref.shape[0]

    def store(ref, i, block):
        own = pl.ds(pl.multiple_of(block * rows, rows), rows)
        for k in range(3):
            ref[i, k * rows : (k + 1) * rows] = total_ref[own, k * width : (k + 1) * width]

    store_blocks(keep_ref, send_ref, store)


def grad_halo_kernel(weight_ref, *refs):
    *grads, inner_ref, other_ref = refs
    rows, win, width = inner_ref.shape
    total = None
    for g, ref in enumerate(grads):
        weight = jnp.concatenate(
            [weight_ref[:, k * width + g * WIDE : k * width + (g + 1) * WIDE] for k in (1, 2)], axis=1
        )
        part = nt(flat(ref[...]), weight)
        total = part if total is None else total + part
    total = total.astype(BF16).reshape(rows, 2 * win, width)
    inner_ref[...], other_ref[...] = by_side(total[:, :win], total[:, win:])


def backward_kernel(*refs):
    shared, (weight_ref, *grads, inner_ref, other_ref) = refs[:10], refs[10:]
    for group in range(len(grads) // 2):
        attend_back_kernel(group, *shared, *grads[2 * group : 2 * group + 2])
    grad_halo_kernel(weight_ref, *grads[1::2], inner_ref, other_ref)


def grad_own_kernel(weight_ref, *refs):
    *grads, out_ref = refs
    rows, own_len, width = out_ref.shape
    pair = 2
    groups = len(grads)

    @pl.loop(0, rows // pair)
    def _(i):
        at = pl.ds(i * pair, pair)
        grad = jnp.concatenate([flat(ref[at]) for ref in grads], axis=1)
        weight = jnp.concatenate(
            [
                weight_ref[:, k * width + g * WIDE : k * width + (g + 1) * WIDE]
                for g in range(groups)
                for k in range(3)
            ],
            axis=1,
        )
        out_ref[at] = nt(grad, weight).reshape(pair, own_len, width)


def result_kernel(mid_middle_ref, out_middle_ref, mid_mixed_ref, out_mixed_ref, down_ref, result_ref):
    own_len, win = result_ref.shape[1], HALF_WIN
    pair = 3

    @pl.loop(0, result_ref.shape[0] // pair)
    def _(i):
        at = pl.ds(i * pair, pair)

        def result(middle_ref, mixed_ref):
            total = flat(middle_ref[at]) + nn(flat(mixed_ref[at]), down_ref[...])
            return total.astype(BF16).reshape(middle_ref[at].shape)

        result_ref[at, win : own_len - win] = result(mid_middle_ref, mid_mixed_ref)
        outer = result(out_middle_ref, out_mixed_ref)
        result_ref[at, :win] = outer[:, :win]
        result_ref[at, own_len - win :] = outer[:, win:]


def finish_kernel(
    tokens_ref, own_ref, inner_ref, other_ref, mid_grad_ref, out_grad_ref, gain_ref, grad_ref
):
    own_len, win = tokens_ref.shape[1], HALF_WIN

    @pl.loop(0, tokens_ref.shape[0])
    def _(row):
        unit, inverse = normalize(tokens_ref[row].astype(F32))
        own = own_ref[row]
        low, high = by_side(inner_ref[row].astype(F32), other_ref[row].astype(F32))
        grads = jnp.concatenate(
            [own[:win] + low, own[win : own_len - win], own[own_len - win :] + high],
            axis=0,
        )
        outer = out_grad_ref[row]
        middle = jnp.concatenate([outer[:win], mid_grad_ref[row], outer[win:]], axis=0)
        grad_ref[row] = middle + norm_back(grads * gain_ref[...], unit, inverse)


def place_kernel(own_ref, other_ref, weight_ref, gain_ref, *out_refs):
    *out_refs, gain_grad_ref = out_refs

    def store(ref, i, block):
        at = 0
        for out in out_refs:
            rows = out.shape[0] // BLOCKS
            for c in range(0, out.shape[1], ref.shape[2]):
                out[pl.ds(pl.multiple_of(block * rows, rows), rows), c : c + ref.shape[2]] = ref[
                    i, at : at + rows
                ].astype(F32)
                at += rows

    store_blocks(own_ref, other_ref, store)
    total = None
    for c in range(0, weight_ref.shape[1], LANES):
        part = out_refs[0][:, c : c + LANES] * weight_ref[:, c : c + LANES].astype(F32)
        total = part if total is None else total + part
    gain_grad_ref[...] = jnp.sum(total.T, axis=0, keepdims=True) / gain_ref[...]


def add_kernel(count, *refs):
    parts, outs = refs[:count], refs[count:]
    size = parts[0].shape[0] // len(outs)
    for k, out in enumerate(outs):
        at = slice(k * size, (k + 1) * size)
        out[...] = sum(p[at].astype(F32) for p in parts).astype(BF16)


def join_kernel(*refs):
    *parts, out = refs
    size = parts[0].shape[0]
    for k, part in enumerate(parts):
        out[k * size : (k + 1) * size] = part[...]


def to_neighbours(inner, other):
    size = lax.axis_size("seq")
    pairs = [(i, i ^ 1) for i in range(size)]
    between = [p for i in range(1, size - 1, 2) for p in ((i, i + 1), (i + 1, i))]
    return lax.ppermute(inner, "seq", pairs), lax.ppermute(other, "seq", between)


def swap_route(core, x, y, z, rest):
    dp, seq = lax.axis_size("dp"), lax.axis_size("seq")

    def partner(i):
        d, s = divmod(i, seq)
        return (d ^ (core + 2 * x)) * seq + (s ^ (y + 2 * z + 8 * rest))

    return [(i, partner(i)) for i in range(dp * seq)]


def swap(values, core=0, x=0, y=0, z=0, rest=0):
    return lax.ppermute(values, ("dp", "seq"), swap_route(core, x, y, z, rest))


def shape(*dims, kind=BF16):
    return jax.ShapeDtypeStruct(dims, kind)


def call(name, kernel, outs, *args, after=(), token=False, grant=6, flops=1e9, scratch=()):
    outs = [*outs, shape(8, LANES, kind=F32)] if token else outs
    spec = pl.BlockSpec(memory_space=pltpu.VMEM)
    moved = sum(int(np.prod(a.shape)) * a.dtype.itemsize for a in (*args, *outs))

    def body(*refs):
        refs = refs[len(after) :]
        if token:
            at = len(args) + len(outs) - 1
            refs[at][...] = jnp.zeros_like(refs[at])
            refs = refs[:at] + refs[at + 1 :]
        return kernel(*refs)

    return pl.pallas_call(
        body,
        out_shape=outs,
        in_specs=[pl.BlockSpec(memory_space=pl.ANY)] * len(after) + [spec] * len(args),
        out_specs=[spec] * len(outs),
        scratch_shapes=scratch,
        compiler_params=pltpu.CompilerParams(vmem_limit_bytes=grant * MB),
        cost_estimate=pl.CostEstimate(flops=int(flops) // 100, bytes_accessed=moved // 100, transcendentals=0),
        name=name,
    )(*after, *args)


def add_up(parts, outs, after=()):
    return call("add", functools.partial(add_kernel, len(parts)), outs, *parts, after=after, grant=4, flops=1e6)


def join(parts, after=()):
    size = parts[0].shape
    out = shape(len(parts) * size[0], *size[1:])
    return call("join", join_kernel, [out], *parts, after=after, grant=4, flops=1e6)[0]


def swap_plane(parts):
    return [swap(parts[k], x=k >> 1, y=k & 1) for k in (1, 2, 3)]


def swap_rest(own):
    rest = 1
    while 8 * rest < lax.axis_size("seq"):
        (own,) = add_up([own, swap(own, rest=rest)], [shape(*own.shape)])
        rest *= 2
    return own


def angle_tables(own_len, pieces):
    inverse = ROTARY_BASE ** (-(np.arange(0, HEAD_DIM, 2) / HEAD_DIM))
    inverse = np.tile(inverse, LANES // HALF)
    base = np.arange(pieces)[:, None] * own_len * inverse
    local = (np.arange(own_len + 2 * HALF_WIN) - HALF_WIN)[:, None] * inverse
    return [jnp.asarray(np.stack([np.cos(a), np.sin(a)], axis=d), F32) for a, d in ((base, 1), (local, 0))]


def shards(
    tokens,
    document_starts,
    attention_in,
    attention_out,
    feedforward_in,
    feedforward_out,
    gain_first,
    gain_second,
    result_grad,
):
    rows, own_len, width = tokens.shape
    hidden = feedforward_out.shape[0]
    win = HALF_WIN
    mid = own_len - 2 * win
    seq = lax.axis_size("seq")
    groups = width // WIDE
    gain_one, gain_two = gain_first[None], gain_second[None]

    loaded = [tokens, document_starts, attention_in, gain_one, *angle_tables(own_len, seq)]
    outs = [pltpu.VMEM(a.shape, a.dtype) for a in loaded] + [pltpu.VMEM((rows, win, width), BF16)] * 2
    tokens, document_starts, attention_in, gain_one, *tables, inner_tokens, other_tokens = pl.pallas_call(
        functools.partial(load_kernel, len(loaded)),
        out_shape=outs,
        in_specs=[pl.BlockSpec(memory_space=pltpu.HBM)] * len(loaded),
        out_specs=[pl.BlockSpec(memory_space=pltpu.VMEM)] * len(outs),
        scratch_shapes=[pltpu.SemaphoreType.DMA((len(outs),))],
        compiler_params=pltpu.CompilerParams(vmem_limit_bytes=MB),
        name="load",
    )(*[pltpu.with_memory_space_constraint(a, pltpu.HBM) for a in loaded])
    inner_halo, other_halo = to_neighbours(inner_tokens, other_tokens)

    row_shape = shape(rows, own_len, width)
    normed, queries, keys, values, weight, angles, bounds = call(
        "project",
        project_kernel,
        [row_shape] * 4
        + [
            shape(*attention_in.shape),
            shape(2, own_len + 2 * win, LANES, kind=F32),
            shape(rows, 2, mid + 4 * win, kind=jnp.int32),
        ],
        tokens,
        document_starts,
        attention_in,
        gain_one,
        *tables,
        flops=3e9,
    )
    mid_attended, mid_probs = call(
        "attend_mid",
        attend_mid_kernel,
        [shape(rows, mid, width), shape(rows, groups, own_len, GROUP * mid, kind=F32)],
        queries,
        keys,
        values,
        bounds,
        flops=2e9,
    )

    def dense(name, outer, attended):
        count = attended.shape[1]
        return call(
            name,
            functools.partial(dense_kernel, outer),
            [
                shape(rows, count, width, kind=F32),
                shape(rows, count, width),
                shape(rows, count, hidden),
                shape(rows, count, 2 * hidden),
                shape(rows, count, width, kind=F32),
                shape(rows, count, width),
                shape(rows, count, width),
            ],
            tokens,
            result_grad,
            attended,
            attention_out,
            feedforward_in,
            feedforward_out,
            gain_two,
            flops=5e9,
        )

    mid_middle, mid_normed, mid_mixed, mid_grad_up, mid_grad, mid_branch, mid_grad_attended = dense(
        "dense_mid", False, mid_attended
    )

    halo_normed, halo_keys, halo_values = call(
        "halo",
        halo_kernel,
        [shape(rows, 2 * win, width)] * 3,
        inner_halo,
        other_halo,
        weight,
        gain_one,
        angles,
        flops=1e9,
    )
    out_attended, out_probs = call(
        "attend_out",
        attend_out_kernel,
        [shape(rows, 2 * win, width), shape(rows, 2, groups, 3 * win, GROUP * win, kind=F32)],
        queries,
        keys,
        values,
        halo_keys,
        halo_values,
        bounds,
        flops=2e9,
    )
    out_middle, out_normed, out_mixed, out_grad_up, out_grad, out_branch, out_grad_attended = dense(
        "dense_out", True, out_attended
    )

    piece = (feedforward_in.shape[1] // width * width + width + hidden) // BLOCKS
    keep_one, send_one = call(
        "weights",
        weights_kernel,
        [shape(BLOCKS // 2, piece, width)] * 2,
        result_grad,
        mid_normed,
        out_normed,
        mid_grad_up,
        out_grad_up,
        mid_mixed,
        out_mixed,
        mid_attended,
        out_attended,
        mid_branch,
        out_branch,
        flops=5e9,
        scratch=[
            pltpu.VMEM(feedforward_in.shape, BF16),
            pltpu.VMEM(attention_out.shape, BF16),
            pltpu.VMEM(feedforward_out.shape, F32),
        ],
    )

    def cut(blocks, parts):
        return [shape(blocks.shape[0] // parts, *blocks.shape[1:])] * parts

    activations, done_result = call(
        "result",
        result_kernel,
        [row_shape],
        mid_middle,
        out_middle,
        mid_mixed,
        out_mixed,
        feedforward_out,
        flops=2e9,
        after=[keep_one],
        token=True,
    )
    chip_one = add_up([keep_one, swap(send_one, core=1)], cut(keep_one, 4), after=[done_result])
    from_plane = swap_plane(chip_one)
    grad_shapes = [shape(rows, own_len, 3 * WIDE), shape(rows, 2 * win, 2 * WIDE)] * groups
    *grads, inner_grad, other_grad = call(
        "backward",
        backward_kernel,
        [shape(rows, own_len, 3 * WIDE), shape(rows, 2 * win, 2 * WIDE)] * groups + [shape(rows, win, width)] * 2,
        queries,
        keys,
        values,
        halo_keys,
        halo_values,
        mid_grad_attended,
        out_grad_attended,
        mid_probs,
        out_probs,
        angles,
        weight,
        flops=12e9,
        after=[chip_one[0]],
    )
    inner_grad, other_grad = to_neighbours(inner_grad, other_grad)
    (total_in,) = call(
        "weight_in",
        weight_in_kernel,
        [shape(*attention_in.shape)],
        normed,
        halo_normed,
        *grads,
        flops=4e9,
    )
    plane_one = add_up([chip_one[0], *from_plane], cut(chip_one[0], 2), after=[total_in])
    keep_two, send_two = call(
        "split",
        split_kernel,
        [shape(BLOCKS // 2, attention_in.shape[1] // BLOCKS, width)] * 2,
        total_in,
        flops=1e9,
        after=[plane_one[0]],
    )
    chip_two = add_up([keep_two, swap(send_two, core=1)], cut(keep_two, 4))
    near_one = add_up([plane_one[0], swap(plane_one[1], z=1)], cut(plane_one[0], 2), after=[chip_two[0]])
    from_plane = swap_plane(chip_two)
    own_grad, done_own = call(
        "grad_own",
        grad_own_kernel,
        [shape(rows, own_len, width, kind=F32)],
        weight,
        *grads[::2],
        flops=2e9,
        after=[near_one[0]],
        token=True,
    )
    (line_one,) = add_up([near_one[0], swap(near_one[1], z=2)], cut(near_one[0], 1), after=[done_own])
    line_one = swap_rest(line_one)
    plane_two = add_up([chip_two[0], *from_plane], cut(chip_two[0], 2), after=[line_one, inner_grad])
    line_one = join([line_one, swap(line_one, z=2)], after=[plane_two[0]])
    near_two = add_up([plane_two[0], swap(plane_two[1], z=1)], cut(plane_two[0], 2), after=[line_one])
    line_one = join([line_one, swap(line_one, z=1)], after=[near_two[0]])
    from_plane = swap_plane([line_one] * 4)
    (line_two,) = add_up([near_two[0], swap(near_two[1], z=2)], cut(near_two[0], 1), after=[line_one])
    line_two = swap_rest(line_two)
    line_two = join([line_two, swap(line_two, z=2)])
    line_two = join([line_two, swap(line_two, z=1)], after=[other_grad])
    from_plane_two = swap_plane([line_two] * 4)
    whole_one = join([line_one, *from_plane], after=[line_two])
    grad_tokens, done_finish = call(
        "finish",
        finish_kernel,
        [shape(rows, own_len, width, kind=F32)],
        tokens,
        own_grad,
        inner_grad,
        other_grad,
        mid_grad,
        out_grad,
        gain_one,
        flops=1e8,
        after=[whole_one],
        token=True,
    )

    def placed(parts, gain, *weights):
        outs = [shape(*w.shape, kind=F32) for w in weights] + [shape(1, width, kind=F32)]
        return call("place", place_kernel, outs, *parts, weights[0], gain, flops=1e6)

    grad_up, grad_out, grad_down, grad_gain_two = placed(
        (whole_one, swap(whole_one, core=1)), gain_two, feedforward_in, attention_out, feedforward_out
    )
    whole_two = join([line_two, *from_plane_two], after=[grad_gain_two, done_finish])
    grad_in, grad_gain_one = placed((whole_two, swap(whole_two, core=1)), gain_one, attention_in)
    return activations, grad_tokens, grad_in, grad_out, grad_up, grad_down, grad_gain_one[0], grad_gain_two[0]


def solution(mesh):
    token, rest = P("dp", "seq", None), P()
    return jax.shard_map(
        shards,
        mesh=mesh,
        in_specs=(token, P("dp", None)) + (rest,) * 6 + (token,),
        out_specs=(token, token) + (rest,) * 6,
        check_vma=False,
    )
```

```python
import functools

import jax
import jax.numpy as jnp
import numpy as np
from jax import lax
from jax.experimental import pallas as pl
from jax.experimental.pallas import tpu as pltpu
from jax.sharding import PartitionSpec as P

HEADS = 8
HEAD_DIM = 64
HALF = HEAD_DIM // 2
HALF_WIN = 64
EPSILON = 1e-05
ROTARY_BASE = 10000.0
SCALE = HEAD_DIM**-0.5
BLOCKS = 32
GROUP = 4
WIDE = GROUP * HEAD_DIM
LANES = 128
MB = 1024 * 1024

F32 = jnp.float32
BF16 = jnp.bfloat16


def dot(a, b, contract):
    return lax.dot_general(a, b, ((contract[:1], contract[1:]), ((), ())), preferred_element_type=F32)


def nn(a, b):
    return dot(a, b, (1, 0))


def nt(a, b):
    return dot(a, b, (1, 1))


def tn(a, b):
    return dot(a, b, (0, 0))


def iota(shape, dim):
    return lax.broadcasted_iota(jnp.int32, shape, dim)


def flat(values):
    return values.reshape(-1, values.shape[-1])


def normalize(values):
    shifted = values - jnp.mean(values, axis=-1, keepdims=True)
    inverse = lax.rsqrt(jnp.mean(shifted * shifted, axis=-1, keepdims=True) + EPSILON)
    return shifted * inverse, inverse


def norm_back(scaled_grad, unit, inverse):
    return (
        scaled_grad
        - jnp.mean(scaled_grad, axis=-1, keepdims=True)
        - unit * jnp.mean(scaled_grad * unit, axis=-1, keepdims=True)
    ) * inverse


def halves_first():
    old, new = iota((WIDE, WIDE), 0), iota((WIDE, WIDE), 1)
    moved = (old % HEAD_DIM) // HALF * LANES + old // HEAD_DIM * HALF + old % HALF
    return (moved == new).astype(BF16)


def head_of(shape, halved):
    lane = iota(shape, 1)
    return lane % LANES // HALF if halved else lane // HEAD_DIM


def by_head(values, halved):
    head = head_of(values.shape, halved)
    zero = jnp.zeros_like(values)
    return jnp.concatenate([jnp.where(head == h, values, zero) for h in range(GROUP)], axis=0)


def pick_heads(stacked, halved):
    count = stacked.shape[0] // GROUP
    head = head_of((count, stacked.shape[1]), halved)
    out = stacked[:count]
    for h in range(1, GROUP):
        out = jnp.where(head == h, stacked[h * count : (h + 1) * count], out)
    return out


def turn(values, cosine, sines):
    first, second = values[:, :LANES], values[:, LANES:]
    return jnp.concatenate([first * cosine - second * sines, second * cosine + first * sines], axis=1)


def turn_back(values, cosine, sines):
    first, second = values[:, :LANES], values[:, LANES:]
    return jnp.concatenate([first * cosine + second * sines, second * cosine - first * sines], axis=1)


def load_kernel(tokens_ref, *refs):
    count = len(refs) // 2 - 1
    sources, (inner_ref, other_ref, *outs), sems = refs[:count], refs[count:-1], refs[-1]
    own_len, win = tokens_ref.shape[1], HALF_WIN
    odd = lax.axis_index("seq") % 2
    copies = []
    for k, (out, high) in enumerate(((inner_ref, odd == 0), (other_ref, odd == 1))):
        at = pl.multiple_of(jnp.where(high, own_len - win, 0), win)
        copies.append(pltpu.make_async_copy(tokens_ref.at[:, pl.ds(at, win)], out, sems.at[k]))
    for k, (source, out) in enumerate(zip(sources, outs, strict=True)):
        copies.append(pltpu.make_async_copy(source, out, sems.at[k + 2]))
    for copy in copies:
        copy.start()
    for copy in copies:
        copy.wait()


def by_side(inner, other):
    odd = lax.axis_index("seq") % 2 == 1
    return jnp.where(odd, inner, other), jnp.where(odd, other, inner)


def project_kernel(
    tokens_ref,
    starts_ref,
    in_ref,
    gain_ref,
    base_ref,
    table_ref,
    normed_ref,
    queries_ref,
    keys_ref,
    values_ref,
    weight_ref,
    angles_ref,
    bounds_ref,
):
    rows, own_len, width = tokens_ref.shape
    win = HALF_WIN
    place = lax.axis_index("seq")
    start = place * own_len
    row_len = own_len * lax.axis_size("seq")

    base_cos, base_sin = base_ref[place, 0:1], base_ref[place, 1:2]
    angles_ref[0] = base_cos * table_ref[0] - base_sin * table_ref[1]
    angles_ref[1] = base_sin * table_ref[0] + base_cos * table_ref[1]

    lane = iota((rows, own_len - 2 * win + 4 * win), 1)
    mid = own_len - 2 * win
    pos = start + jnp.where(
        lane < mid, lane + win, jnp.where(lane < mid + 2 * win, lane % win, own_len - win + lane % win)
    )
    first, last = jnp.maximum(pos - win, 0), jnp.minimum(pos + win, row_len - 1)
    for j in range(starts_ref.shape[1]):
        cut = starts_ref[:, j : j + 1]
        first = jnp.maximum(first, jnp.where(cut <= pos, cut, 0))
        last = jnp.minimum(last, jnp.where(cut > pos, cut - 1, row_len))
    for r in range(rows):
        bounds_ref[r, 0:1] = first[r : r + 1]
        bounds_ref[r, 1:2] = last[r : r + 1]

    order = halves_first()
    for c in range(0, 2 * width, WIDE):
        weight_ref[:, c : c + WIDE] = nn(in_ref[:, c : c + WIDE], order).astype(BF16)
    weight_ref[:, 2 * width :] = in_ref[:, 2 * width :]

    pair = 6
    cosine, sines = angles_ref[0, win : win + own_len], angles_ref[1, win : win + own_len]
    cosine, sines = jnp.concatenate([cosine] * pair), jnp.concatenate([sines] * pair)

    @pl.loop(0, rows // pair)
    def _(i):
        at = pl.ds(i * pair, pair)
        unit, _ = normalize(flat(tokens_ref[at]).astype(F32))
        normed = (unit * gain_ref[...]).astype(BF16)
        normed_ref[at] = normed.reshape(pair, own_len, width)
        queries, keys = nn(normed, weight_ref[:, :width]), nn(normed, weight_ref[:, width : 2 * width])
        for c in range(0, width, WIDE):
            part = turn(queries[:, c : c + WIDE], cosine * SCALE, sines * SCALE)
            queries_ref[at, :, c : c + WIDE] = part.astype(BF16).reshape(pair, own_len, WIDE)
            part = turn(keys[:, c : c + WIDE], cosine, sines)
            keys_ref[at, :, c : c + WIDE] = part.astype(BF16).reshape(pair, own_len, WIDE)
        values_ref[at] = nn(normed, weight_ref[:, 2 * width :]).astype(BF16).reshape(pair, own_len, width)


def halo_kernel(inner_ref, other_ref, weight_ref, gain_ref, angles_ref, normed_ref, keys_ref, values_ref):
    rows, win, width = inner_ref.shape
    pair = 3
    span = angles_ref.shape[1]
    cosine = jnp.concatenate([angles_ref[0, :win], angles_ref[0, span - win :]] * pair)
    sines = jnp.concatenate([angles_ref[1, :win], angles_ref[1, span - win :]] * pair)

    @pl.loop(0, rows // pair)
    def _(i):
        at = pl.ds(i * pair, pair)
        sides = by_side(inner_ref[at], other_ref[at])
        unit, _ = normalize(flat(jnp.concatenate(sides, axis=1)).astype(F32))
        normed = (unit * gain_ref[...]).astype(BF16)
        normed_ref[at] = normed.reshape(pair, 2 * win, width)
        keys = nn(normed, weight_ref[:, width : 2 * width])
        for c in range(0, width, WIDE):
            part = turn(keys[:, c : c + WIDE], cosine, sines)
            keys_ref[at, :, c : c + WIDE] = part.astype(BF16).reshape(pair, 2 * win, WIDE)
        values_ref[at] = nn(normed, weight_ref[:, 2 * width :]).astype(BF16).reshape(pair, 2 * win, width)


def bias_of(bounds_ref, row, lanes, first_key, keys):
    key = first_key + iota((keys, LANES), 0)
    first, last = bounds_ref[row, 0:1, lanes], bounds_ref[row, 1:2, lanes]
    return jnp.where((key >= first) & (key <= last), 0.0, -jnp.inf)


def probabilities(scores, bias):
    parts = []
    for c in range(0, scores.shape[1], LANES):
        part = scores[:, c : c + LANES] + bias
        part = jnp.exp(part - jnp.max(part, axis=0, keepdims=True))
        parts.append(part * (1.0 / jnp.sum(part, axis=0, keepdims=True)))
    return jnp.concatenate(parts, axis=1)


def attend_mid_kernel(queries_ref, keys_ref, values_ref, bounds_ref, attended_ref, probs_ref):
    rows, own_len, width = queries_ref.shape
    win = HALF_WIN
    mid = own_len - 2 * win
    start = lax.axis_index("seq") * own_len
    pair = 6

    @pl.loop(0, rows // pair)
    def _(i):
        for r in range(pair):
            row = i * pair + r
            bias = bias_of(bounds_ref, row, slice(0, mid), start, own_len)
            for g in range(width // WIDE):
                cols = slice(g * WIDE, (g + 1) * WIDE)
                probs = probabilities(
                    nt(keys_ref[row, :, cols], by_head(queries_ref[row, win : win + mid, cols], True)), bias
                )
                probs_ref[row, g] = probs
                out = tn(probs.astype(BF16), values_ref[row, :, cols])
                attended_ref[row, :, cols] = pick_heads(out, False).astype(BF16)


def wide_side(own, halo, side):
    win = HALF_WIN
    if side == 0:
        return jnp.concatenate([halo[:win], own[: 2 * win]], axis=0)
    return jnp.concatenate([own[own.shape[0] - 2 * win :], halo[win:]], axis=0)


def attend_out_kernel(
    queries_ref, keys_ref, values_ref, halo_keys_ref, halo_values_ref, bounds_ref, attended_ref, probs_ref
):
    rows, own_len, width = queries_ref.shape
    win = HALF_WIN
    mid = own_len - 2 * win
    start = lax.axis_index("seq") * own_len
    pair = 6

    @pl.loop(0, rows // pair)
    def _(i):
        for r in range(pair):
            row = i * pair + r
            for side in range(2):
                own = slice(0, win) if side == 0 else slice(own_len - win, own_len)
                lanes = slice(mid + side * LANES, mid + (side + 1) * LANES)
                bias = bias_of(bounds_ref, row, lanes, start + own.start - win, 3 * win)
                for g in range(width // WIDE):
                    cols = slice(g * WIDE, (g + 1) * WIDE)
                    keys = wide_side(keys_ref[row, :, cols], halo_keys_ref[row, :, cols], side)
                    values = wide_side(values_ref[row, :, cols], halo_values_ref[row, :, cols], side)
                    probs = probabilities(nt(keys, by_head(queries_ref[row, own, cols], True)), bias)
                    probs_ref[row, side, g] = probs
                    out = tn(probs.astype(BF16), values)
                    attended_ref[row, side * win : (side + 1) * win, cols] = pick_heads(out, False).astype(BF16)


def gelu_parts(gate):
    bell = jnp.exp(-0.5 * gate * gate)
    t = 1.0 / (1.0 + (0.3275911 * 0.7071067811865476) * jnp.abs(gate))
    tail = t * (
        0.5 * 0.254829592
        + t * (0.5 * -0.284496736 + t * (0.5 * 1.421413741 + t * (0.5 * -1.453152027 + t * (0.5 * 1.061405429))))
    )
    tail = tail * bell
    return jnp.where(gate < 0, tail, 1.0 - tail), gate * bell * 0.3989422804014327


def part_of(ref, at, outer):
    own_len, win = ref.shape[1], HALF_WIN
    if outer:
        return flat(jnp.concatenate([ref[at, :win], ref[at, own_len - win :]], axis=1))
    return flat(ref[at, win : own_len - win])


def dense_kernel(
    outer,
    tokens_ref,
    top_ref,
    attended_ref,
    out_ref,
    up_ref,
    down_ref,
    gain_ref,
    middle_ref,
    normed_ref,
    mixed_ref,
    grad_up_ref,
    grad_middle_ref,
    branch_ref,
    grad_attended_ref,
):
    rows, count, width = attended_ref.shape
    hidden = down_ref.shape[0]
    pair = 6

    @pl.loop(0, rows // pair)
    def _(i):
        at = pl.ds(i * pair, pair)

        def put(ref, values, cols=slice(None)):
            ref[at, :, cols] = values.reshape(pair, count, -1)

        top = part_of(top_ref, at, outer)
        middle = part_of(tokens_ref, at, outer).astype(F32) + nn(flat(attended_ref[at]), out_ref[...])
        put(middle_ref, middle)
        unit, inverse = normalize(middle)
        normed = (unit * gain_ref[...]).astype(BF16)
        put(normed_ref, normed)
        grad_hidden = [nt(top, down_ref[:512]), nt(top, down_ref[512:])]
        for c in range(0, hidden, 256):
            halves = [up_ref[:, c : c + 256], up_ref[:, hidden + c : hidden + c + 256]]
            both = nn(normed, jnp.concatenate(halves, axis=1))
            gate, lift = both[:, :256], both[:, 256:]
            grad_mixed = grad_hidden[c // 512][:, c % 512 : c % 512 + 256]
            phi, slope = gelu_parts(gate)
            active = gate * phi
            put(mixed_ref, (active * lift).astype(BF16), slice(c, c + 256))
            put(grad_up_ref, (grad_mixed * lift * (phi + slope)).astype(BF16), slice(c, c + 256))
            put(grad_up_ref, (grad_mixed * active).astype(BF16), slice(hidden + c, hidden + c + 256))
        grad_normed = nt(flat(grad_up_ref[at]), up_ref[...])
        grad_middle = top.astype(F32) + norm_back(grad_normed * gain_ref[...], unit, inverse)
        put(grad_middle_ref, grad_middle)
        branch = grad_middle.astype(BF16)
        put(branch_ref, branch)
        put(grad_attended_ref, nt(branch, out_ref[...]).astype(BF16))


def store_blocks(keep_ref, send_ref, store):
    seq, dp = lax.axis_index("seq"), lax.axis_index("dp")
    place = (dp % 2) * 16 + (dp // 2) * 8 + (seq % 2) * 4 + (seq // 2) % 2 * 2 + (seq // 4) % 2
    for ref, base in ((keep_ref, 0), (send_ref, BLOCKS // 2)):

        @pl.loop(0, BLOCKS // 2)
        def _(i):
            store(ref, i, place ^ (i + base))


def weights_kernel(
    outer,
    top_ref,
    normed_ref,
    grad_up_ref,
    mixed_ref,
    attended_ref,
    branch_ref,
    *refs,
):
    begun, (*sums,) = (refs[:3], refs[3:]) if outer else ((None,) * 3, refs)
    if outer:
        keep_ref, send_ref, *sums = sums
    up_sum, down_sum, out_sum = sums
    width = top_ref.shape[2]

    def add(part, ref, at):
        return part if ref is None else part + ref[at].astype(F32)

    normed = flat(normed_ref[...])
    for c in range(0, up_sum.shape[1], 512):
        at = (slice(None), slice(c, c + 512))
        up_sum[at] = add(tn(normed, flat(grad_up_ref[:, :, c : c + 512])), begun[0], at).astype(BF16)
    top = part_of(top_ref, slice(0, top_ref.shape[0]), outer)
    for c in range(0, down_sum.shape[0], 256):
        at = (slice(c, c + 256), slice(None))
        down_sum[at] = add(tn(flat(mixed_ref[:, :, c : c + 256]), top), begun[1], at).astype(down_sum.dtype)
    at = (slice(None), slice(None))
    out_sum[at] = add(tn(flat(attended_ref[...]), flat(branch_ref[...])), begun[2], at).astype(BF16)
    if not outer:
        return
    rows, down_rows = width // BLOCKS, down_sum.shape[0] // BLOCKS

    def store(ref, i, block):
        own = pl.ds(pl.multiple_of(block * rows, rows), rows)
        at = 0
        for c in range(0, up_sum.shape[1], width):
            ref[i, at : at + rows] = up_sum[own, c : c + width]
            at += rows
        ref[i, at : at + rows] = out_sum[own, :]
        at += rows
        ref[i, at:] = down_sum[pl.ds(pl.multiple_of(block * down_rows, down_rows), down_rows), :].astype(BF16)

    store_blocks(keep_ref, send_ref, store)


def attend_back_kernel(
    group,
    queries_ref,
    keys_ref,
    values_ref,
    halo_keys_ref,
    halo_values_ref,
    mid_grad_ref,
    out_grad_ref,
    mid_probs_ref,
    out_probs_ref,
    angles_ref,
    own_ref,
    halo_ref,
):
    rows, own_len, _ = queries_ref.shape
    win = HALF_WIN
    mid = own_len - 2 * win
    cols = slice(group * WIDE, (group + 1) * WIDE)
    cosine, sines = angles_ref[0], angles_ref[1]
    own_cos, own_sin = cosine[win : win + own_len], sines[win : win + own_len]
    halo_cos = jnp.concatenate([cosine[:win], cosine[win + own_len :]])
    halo_sin = jnp.concatenate([sines[:win], sines[win + own_len :]])
    pair = 6

    def unit(queries, keys, values, grads, probs):
        q4, g4 = by_head(queries, True), by_head(grads, False)
        grad_probs = nt(values, g4)
        lows, grad_scores = [], []
        for c in range(0, probs.shape[1], LANES):
            part, grad_part = probs[:, c : c + LANES], grad_probs[:, c : c + LANES]
            inner = jnp.sum(part * grad_part, axis=0, keepdims=True)
            lows.append(part.astype(BF16))
            grad_scores.append((part * (grad_part - inner)).astype(BF16))
        grad_scores = jnp.concatenate(grad_scores, axis=1)
        return (
            pick_heads(tn(grad_scores, keys), True),
            nn(grad_scores, q4),
            nn(jnp.concatenate(lows, axis=1), g4),
        )

    @pl.loop(0, rows // pair)
    def _(i):
        for r in range(pair):
            row = i * pair + r
            queries, keys, values = queries_ref[row, :, cols], keys_ref[row, :, cols], values_ref[row, :, cols]
            halo_keys, halo_values = halo_keys_ref[row, :, cols], halo_values_ref[row, :, cols]
            grads = out_grad_ref[row, :, cols]
            middle = unit(queries[win : win + mid], keys, values, mid_grad_ref[row, :, cols], mid_probs_ref[row, group])
            sides = [
                unit(
                    queries[:win] if side == 0 else queries[own_len - win :],
                    wide_side(keys, halo_keys, side),
                    wide_side(values, halo_values, side),
                    grads[side * win : (side + 1) * win],
                    out_probs_ref[row, side, group],
                )
                for side in range(2)
            ]
            low, high = sides
            own = [jnp.concatenate([low[0], middle[0], high[0]], axis=0) * SCALE]
            halo = []
            for k in (1, 2):
                own.append(middle[k] + jnp.concatenate([low[k][win:], high[k][: 2 * win]], axis=0))
                halo.append(jnp.concatenate([low[k][:win], high[k][2 * win :]], axis=0))
            own_ref[row, :, :WIDE] = turn_back(own[0], own_cos, own_sin).astype(BF16)
            own_ref[row, :, WIDE : 2 * WIDE] = turn_back(own[1], own_cos, own_sin).astype(BF16)
            own_ref[row, :, 2 * WIDE :] = own[2].astype(BF16)
            halo_ref[row, :, :WIDE] = turn_back(halo[0], halo_cos, halo_sin).astype(BF16)
            halo_ref[row, :, WIDE:] = halo[1].astype(BF16)


def weight_in_kernel(normed_ref, halo_normed_ref, *refs):
    *grads, total = refs
    width = normed_ref.shape[2]
    normed, halo_normed = flat(normed_ref[...]), flat(halo_normed_ref[...])
    order = halves_first()
    for k in range(3):
        part = tn(normed, jnp.concatenate([flat(own[:, :, k * WIDE : (k + 1) * WIDE]) for own in grads[::2]], axis=1))
        if k > 0:
            halo = [flat(halo[:, :, (k - 1) * WIDE : k * WIDE]) for halo in grads[1::2]]
            part = part + tn(halo_normed, jnp.concatenate(halo, axis=1))
        part = part.astype(BF16)
        if k < 2:
            part = [nt(part[:, c : c + WIDE], order).astype(BF16) for c in range(0, width, WIDE)]
            part = jnp.concatenate(part, axis=1)
        total[:, k * width : (k + 1) * width] = part


def split_kernel(total_ref, keep_ref, send_ref):
    rows, width = total_ref.shape[0] // BLOCKS, total_ref.shape[0]

    def store(ref, i, block):
        own = pl.ds(pl.multiple_of(block * rows, rows), rows)
        for k in range(3):
            ref[i, k * rows : (k + 1) * rows] = total_ref[own, k * width : (k + 1) * width]

    store_blocks(keep_ref, send_ref, store)


def grad_halo_kernel(weight_ref, *refs):
    *grads, inner_ref, other_ref = refs
    rows, win, width = inner_ref.shape
    total = None
    for g, ref in enumerate(grads):
        weight = jnp.concatenate(
            [weight_ref[:, k * width + g * WIDE : k * width + (g + 1) * WIDE] for k in (1, 2)], axis=1
        )
        part = nt(flat(ref[...]), weight)
        total = part if total is None else total + part
    total = total.astype(BF16).reshape(rows, 2 * win, width)
    inner_ref[...], other_ref[...] = by_side(total[:, :win], total[:, win:])


def backward_kernel(*refs):
    shared, (weight_ref, *grads, inner_ref, other_ref) = refs[:10], refs[10:]
    for group in range(len(grads) // 2):
        attend_back_kernel(group, *shared, *grads[2 * group : 2 * group + 2])
    grad_halo_kernel(weight_ref, *grads[1::2], inner_ref, other_ref)


def grad_own_kernel(weight_ref, *refs):
    *grads, out_ref = refs
    rows, own_len, width = out_ref.shape
    pair = 2
    groups = len(grads)

    @pl.loop(0, rows // pair)
    def _(i):
        at = pl.ds(i * pair, pair)
        grad = jnp.concatenate([flat(ref[at]) for ref in grads], axis=1)
        weight = jnp.concatenate(
            [
                weight_ref[:, k * width + g * WIDE : k * width + (g + 1) * WIDE]
                for g in range(groups)
                for k in range(3)
            ],
            axis=1,
        )
        out_ref[at] = nt(grad, weight).reshape(pair, own_len, width)


def result_kernel(mid_middle_ref, out_middle_ref, mid_mixed_ref, out_mixed_ref, down_ref, result_ref):
    own_len, win = result_ref.shape[1], HALF_WIN
    pair = 3

    @pl.loop(0, result_ref.shape[0] // pair)
    def _(i):
        at = pl.ds(i * pair, pair)

        def result(middle_ref, mixed_ref):
            total = flat(middle_ref[at]) + nn(flat(mixed_ref[at]), down_ref[...])
            return total.astype(BF16).reshape(middle_ref[at].shape)

        result_ref[at, win : own_len - win] = result(mid_middle_ref, mid_mixed_ref)
        outer = result(out_middle_ref, out_mixed_ref)
        result_ref[at, :win] = outer[:, :win]
        result_ref[at, own_len - win :] = outer[:, win:]


def finish_kernel(
    tokens_ref, own_ref, inner_ref, other_ref, mid_grad_ref, out_grad_ref, gain_ref, grad_ref
):
    own_len, win = tokens_ref.shape[1], HALF_WIN

    @pl.loop(0, tokens_ref.shape[0])
    def _(row):
        unit, inverse = normalize(tokens_ref[row].astype(F32))
        own = own_ref[row]
        low, high = by_side(inner_ref[row].astype(F32), other_ref[row].astype(F32))
        grads = jnp.concatenate(
            [own[:win] + low, own[win : own_len - win], own[own_len - win :] + high],
            axis=0,
        )
        outer = out_grad_ref[row]
        middle = jnp.concatenate([outer[:win], mid_grad_ref[row], outer[win:]], axis=0)
        grad_ref[row] = middle + norm_back(grads * gain_ref[...], unit, inverse)


def place_kernel(own_ref, other_ref, weight_ref, gain_ref, *out_refs):
    *out_refs, gain_grad_ref = out_refs

    def store(ref, i, block):
        at = 0
        for out in out_refs:
            rows = out.shape[0] // BLOCKS
            for c in range(0, out.shape[1], ref.shape[2]):
                out[pl.ds(pl.multiple_of(block * rows, rows), rows), c : c + ref.shape[2]] = ref[
                    i, at : at + rows
                ].astype(F32)
                at += rows

    store_blocks(own_ref, other_ref, store)
    total = None
    for c in range(0, weight_ref.shape[1], LANES):
        part = out_refs[0][:, c : c + LANES] * weight_ref[:, c : c + LANES].astype(F32)
        total = part if total is None else total + part
    gain_grad_ref[...] = jnp.sum(total.T, axis=0, keepdims=True) / gain_ref[...]


def add_kernel(count, *refs):
    parts, outs = refs[:count], refs[count:]
    size = parts[0].shape[0] // len(outs)
    for k, out in enumerate(outs):
        at = slice(k * size, (k + 1) * size)
        out[...] = sum(p[at].astype(F32) for p in parts).astype(BF16)


def join_kernel(*refs):
    *parts, out = refs
    size = parts[0].shape[0]
    for k, part in enumerate(parts):
        out[k * size : (k + 1) * size] = part[...]


def to_neighbours(inner, other):
    size = lax.axis_size("seq")
    pairs = [(i, i ^ 1) for i in range(size)]
    between = [p for i in range(1, size - 1, 2) for p in ((i, i + 1), (i + 1, i))]
    return lax.ppermute(inner, "seq", pairs), lax.ppermute(other, "seq", between)


def swap_route(core, x, y, z, rest):
    dp, seq = lax.axis_size("dp"), lax.axis_size("seq")

    def partner(i):
        d, s = divmod(i, seq)
        return (d ^ (core + 2 * x)) * seq + (s ^ (y + 2 * z + 8 * rest))

    return [(i, partner(i)) for i in range(dp * seq)]


def swap(values, core=0, x=0, y=0, z=0, rest=0):
    return lax.ppermute(values, ("dp", "seq"), swap_route(core, x, y, z, rest))


def shape(*dims, kind=BF16):
    return jax.ShapeDtypeStruct(dims, kind)


def call(name, kernel, outs, *args, after=(), token=False, grant=6, flops=1e9, scratch=()):
    outs = [*outs, shape(8, LANES, kind=F32)] if token else outs
    spec = pl.BlockSpec(memory_space=pltpu.VMEM)
    moved = sum(int(np.prod(a.shape)) * a.dtype.itemsize for a in (*args, *outs))

    def body(*refs):
        refs = refs[len(after) :]
        if token:
            at = len(args) + len(outs) - 1
            refs[at][...] = jnp.zeros_like(refs[at])
            refs = refs[:at] + refs[at + 1 :]
        return kernel(*refs)

    return pl.pallas_call(
        body,
        out_shape=outs,
        in_specs=[pl.BlockSpec(memory_space=pl.ANY)] * len(after) + [spec] * len(args),
        out_specs=[spec] * len(outs),
        scratch_shapes=scratch,
        compiler_params=pltpu.CompilerParams(vmem_limit_bytes=grant * MB),
        cost_estimate=pl.CostEstimate(flops=int(flops) // 100, bytes_accessed=moved // 100, transcendentals=0),
        name=name,
    )(*after, *args)


def add_up(parts, outs, after=()):
    return call("add", functools.partial(add_kernel, len(parts)), outs, *parts, after=after, grant=4, flops=1e6)


def join(parts, after=()):
    size = parts[0].shape
    out = shape(len(parts) * size[0], *size[1:])
    return call("join", join_kernel, [out], *parts, after=after, grant=4, flops=1e6)[0]


def swap_plane(parts):
    return [swap(parts[k], x=k >> 1, y=k & 1) for k in (1, 2, 3)]


def swap_rest(own):
    rest = 1
    while 8 * rest < lax.axis_size("seq"):
        (own,) = add_up([own, swap(own, rest=rest)], [shape(*own.shape)])
        rest *= 2
    return own


def angle_tables(own_len, pieces):
    inverse = ROTARY_BASE ** (-(np.arange(0, HEAD_DIM, 2) / HEAD_DIM))
    inverse = np.tile(inverse, LANES // HALF)
    base = np.arange(pieces)[:, None] * own_len * inverse
    local = (np.arange(own_len + 2 * HALF_WIN) - HALF_WIN)[:, None] * inverse
    return [jnp.asarray(np.stack([np.cos(a), np.sin(a)], axis=d), F32) for a, d in ((base, 1), (local, 0))]


def shards(
    tokens,
    document_starts,
    attention_in,
    attention_out,
    feedforward_in,
    feedforward_out,
    gain_first,
    gain_second,
    result_grad,
):
    rows, own_len, width = tokens.shape
    hidden = feedforward_out.shape[0]
    win = HALF_WIN
    mid = own_len - 2 * win
    seq = lax.axis_size("seq")
    groups = width // WIDE
    gain_one, gain_two = gain_first[None], gain_second[None]

    small = [document_starts, gain_one, attention_in, *angle_tables(own_len, seq)]
    outs = [pltpu.VMEM((rows, win, width), BF16)] * 2 + [pltpu.VMEM(a.shape, a.dtype) for a in small]
    inner_tokens, other_tokens, document_starts, gain_one, attention_in, *tables = pl.pallas_call(
        load_kernel,
        out_shape=outs,
        in_specs=[pl.BlockSpec(memory_space=pltpu.HBM)] * (1 + len(small)),
        out_specs=[pl.BlockSpec(memory_space=pltpu.VMEM)] * len(outs),
        scratch_shapes=[pltpu.SemaphoreType.DMA((len(outs),))],
        compiler_params=pltpu.CompilerParams(vmem_limit_bytes=MB),
        name="load",
    )(*[pltpu.with_memory_space_constraint(a, pltpu.HBM) for a in (tokens, *small)])
    inner_halo, other_halo = to_neighbours(inner_tokens, other_tokens)

    row_shape = shape(rows, own_len, width)
    normed, queries, keys, values, weight, angles, bounds = call(
        "project",
        project_kernel,
        [row_shape] * 4
        + [
            shape(*attention_in.shape),
            shape(2, own_len + 2 * win, LANES, kind=F32),
            shape(rows, 2, mid + 4 * win, kind=jnp.int32),
        ],
        tokens,
        document_starts,
        attention_in,
        gain_one,
        *tables,
        flops=3e9,
    )
    mid_attended, mid_probs = call(
        "attend_mid",
        attend_mid_kernel,
        [shape(rows, mid, width), shape(rows, groups, own_len, GROUP * mid, kind=F32)],
        queries,
        keys,
        values,
        bounds,
        flops=2e9,
    )

    def dense(name, outer, attended):
        count = attended.shape[1]
        return call(
            name,
            functools.partial(dense_kernel, outer),
            [
                shape(rows, count, width, kind=F32),
                shape(rows, count, width),
                shape(rows, count, hidden),
                shape(rows, count, 2 * hidden),
                shape(rows, count, width, kind=F32),
                shape(rows, count, width),
                shape(rows, count, width),
            ],
            tokens,
            result_grad,
            attended,
            attention_out,
            feedforward_in,
            feedforward_out,
            gain_two,
            flops=5e9,
            grant=14,
        )

    mid_middle, mid_normed, mid_mixed, mid_grad_up, mid_grad, mid_branch, mid_grad_attended = dense(
        "dense_mid", False, mid_attended
    )

    begun = call(
        "begin",
        functools.partial(weights_kernel, False),
        [shape(*w.shape) for w in (feedforward_in, feedforward_out, attention_out)],
        result_grad,
        mid_normed,
        mid_grad_up,
        mid_mixed,
        mid_attended,
        mid_branch,
        flops=3e9,
    )

    halo_normed, halo_keys, halo_values = call(
        "halo",
        halo_kernel,
        [shape(rows, 2 * win, width)] * 3,
        inner_halo,
        other_halo,
        weight,
        gain_one,
        angles,
        flops=1e9,
        after=[begun[2]],
    )
    out_attended, out_probs = call(
        "attend_out",
        attend_out_kernel,
        [shape(rows, 2 * win, width), shape(rows, 2, groups, 3 * win, GROUP * win, kind=F32)],
        queries,
        keys,
        values,
        halo_keys,
        halo_values,
        bounds,
        flops=2e9,
    )
    out_middle, out_normed, out_mixed, out_grad_up, out_grad, out_branch, out_grad_attended = dense(
        "dense_out", True, out_attended
    )

    piece = (feedforward_in.shape[1] // width * width + width + hidden) // BLOCKS
    keep_one, send_one = call(
        "weights",
        functools.partial(weights_kernel, True),
        [shape(BLOCKS // 2, piece, width)] * 2,
        result_grad,
        out_normed,
        out_grad_up,
        out_mixed,
        out_attended,
        out_branch,
        *begun,
        flops=5e9,
        scratch=[
            pltpu.VMEM(feedforward_in.shape, BF16),
            pltpu.VMEM(feedforward_out.shape, F32),
            pltpu.VMEM(attention_out.shape, BF16),
        ],
    )

    def cut(blocks, parts):
        return [shape(blocks.shape[0] // parts, *blocks.shape[1:])] * parts

    activations, done_result = call(
        "result",
        result_kernel,
        [row_shape],
        mid_middle,
        out_middle,
        mid_mixed,
        out_mixed,
        feedforward_out,
        flops=2e9,
        after=[keep_one],
        token=True,
    )
    chip_one = add_up([keep_one, swap(send_one, core=1)], cut(keep_one, 4), after=[done_result])
    from_plane = swap_plane(chip_one)
    grad_shapes = [shape(rows, own_len, 3 * WIDE), shape(rows, 2 * win, 2 * WIDE)] * groups
    *grads, inner_grad, other_grad = call(
        "backward",
        backward_kernel,
        [shape(rows, own_len, 3 * WIDE), shape(rows, 2 * win, 2 * WIDE)] * groups + [shape(rows, win, width)] * 2,
        queries,
        keys,
        values,
        halo_keys,
        halo_values,
        mid_grad_attended,
        out_grad_attended,
        mid_probs,
        out_probs,
        angles,
        weight,
        flops=12e9,
        after=[chip_one[0]],
    )
    inner_grad, other_grad = to_neighbours(inner_grad, other_grad)
    (total_in,) = call(
        "weight_in",
        weight_in_kernel,
        [shape(*attention_in.shape)],
        normed,
        halo_normed,
        *grads,
        flops=4e9,
    )
    plane_one = add_up([chip_one[0], *from_plane], cut(chip_one[0], 2), after=[total_in])
    keep_two, send_two = call(
        "split",
        split_kernel,
        [shape(BLOCKS // 2, attention_in.shape[1] // BLOCKS, width)] * 2,
        total_in,
        flops=1e9,
        after=[plane_one[0]],
    )
    chip_two = add_up([keep_two, swap(send_two, core=1)], cut(keep_two, 4))
    near_one = add_up([plane_one[0], swap(plane_one[1], z=1)], cut(plane_one[0], 2), after=[chip_two[0]])
    from_plane = swap_plane(chip_two)
    own_grad, done_own = call(
        "grad_own",
        grad_own_kernel,
        [shape(rows, own_len, width, kind=F32)],
        weight,
        *grads[::2],
        flops=2e9,
        after=[near_one[0]],
        token=True,
    )
    (line_one,) = add_up([near_one[0], swap(near_one[1], z=2)], cut(near_one[0], 1), after=[done_own])
    line_one = swap_rest(line_one)
    plane_two = add_up([chip_two[0], *from_plane], cut(chip_two[0], 2), after=[line_one, inner_grad])
    line_one = join([line_one, swap(line_one, z=2)], after=[plane_two[0]])
    near_two = add_up([plane_two[0], swap(plane_two[1], z=1)], cut(plane_two[0], 2), after=[line_one])
    line_one = join([line_one, swap(line_one, z=1)], after=[near_two[0]])
    from_plane = swap_plane([line_one] * 4)
    (line_two,) = add_up([near_two[0], swap(near_two[1], z=2)], cut(near_two[0], 1), after=[line_one])
    line_two = swap_rest(line_two)
    line_two = join([line_two, swap(line_two, z=2)])
    line_two = join([line_two, swap(line_two, z=1)], after=[other_grad])
    from_plane_two = swap_plane([line_two] * 4)
    whole_one = join([line_one, *from_plane], after=[line_two])
    grad_tokens, done_finish = call(
        "finish",
        finish_kernel,
        [shape(rows, own_len, width, kind=F32)],
        tokens,
        own_grad,
        inner_grad,
        other_grad,
        mid_grad,
        out_grad,
        gain_one,
        flops=1e8,
        after=[whole_one],
        token=True,
    )

    def placed(parts, gain, *weights):
        outs = [shape(*w.shape, kind=F32) for w in weights] + [shape(1, width, kind=F32)]
        return call("place", place_kernel, outs, *parts, weights[0], gain, flops=1e6)

    grad_up, grad_out, grad_down, grad_gain_two = placed(
        (whole_one, swap(whole_one, core=1)), gain_two, feedforward_in, attention_out, feedforward_out
    )
    whole_two = join([line_two, *from_plane_two], after=[grad_gain_two, done_finish])
    grad_in, grad_gain_one = placed((whole_two, swap(whole_two, core=1)), gain_one, attention_in)
    return activations, grad_tokens, grad_in, grad_out, grad_up, grad_down, grad_gain_one[0], grad_gain_two[0]


def solution(mesh):
    token, rest = P("dp", "seq", None), P()
    return jax.shard_map(
        shards,
        mesh=mesh,
        in_specs=(token, P("dp", None)) + (rest,) * 6 + (token,),
        out_specs=(token, token) + (rest,) * 6,
        check_vma=False,
    )
```

```python
import functools

import jax
import jax.numpy as jnp
import numpy as np
from jax import lax
from jax.experimental import pallas as pl
from jax.experimental.pallas import tpu as pltpu
from jax.sharding import PartitionSpec as P

HEADS = 8
HEAD_DIM = 64
HALF = HEAD_DIM // 2
HALF_WIN = 64
EPSILON = 1e-05
ROTARY_BASE = 10000.0
SCALE = HEAD_DIM**-0.5
BLOCKS = 32
GROUP = 4
WIDE = GROUP * HEAD_DIM
LANES = 128
MB = 1024 * 1024

F32 = jnp.float32
BF16 = jnp.bfloat16


def dot(a, b, contract):
    return lax.dot_general(a, b, ((contract[:1], contract[1:]), ((), ())), preferred_element_type=F32)


def nn(a, b):
    return dot(a, b, (1, 0))


def nt(a, b):
    return dot(a, b, (1, 1))


def tn(a, b):
    return dot(a, b, (0, 0))


def iota(shape, dim):
    return lax.broadcasted_iota(jnp.int32, shape, dim)


def flat(values):
    return values.reshape(-1, values.shape[-1])


def normalize(values):
    shifted = values - jnp.mean(values, axis=-1, keepdims=True)
    inverse = lax.rsqrt(jnp.mean(shifted * shifted, axis=-1, keepdims=True) + EPSILON)
    return shifted * inverse, inverse


def norm_back(scaled_grad, unit, inverse):
    return (
        scaled_grad
        - jnp.mean(scaled_grad, axis=-1, keepdims=True)
        - unit * jnp.mean(scaled_grad * unit, axis=-1, keepdims=True)
    ) * inverse


def halves_first():
    old, new = iota((WIDE, WIDE), 0), iota((WIDE, WIDE), 1)
    moved = (old % HEAD_DIM) // HALF * LANES + old // HEAD_DIM * HALF + old % HALF
    return (moved == new).astype(BF16)


def head_of(shape, halved):
    lane = iota(shape, 1)
    return lane % LANES // HALF if halved else lane // HEAD_DIM


def by_head(values, halved):
    head = head_of(values.shape, halved)
    zero = jnp.zeros_like(values)
    return jnp.concatenate([jnp.where(head == h, values, zero) for h in range(GROUP)], axis=0)


def pick_heads(stacked, halved):
    count = stacked.shape[0] // GROUP
    head = head_of((count, stacked.shape[1]), halved)
    out = stacked[:count]
    for h in range(1, GROUP):
        out = jnp.where(head == h, stacked[h * count : (h + 1) * count], out)
    return out


def turn(values, cosine, sines):
    first, second = values[:, :LANES], values[:, LANES:]
    return jnp.concatenate([first * cosine - second * sines, second * cosine + first * sines], axis=1)


def turn_back(values, cosine, sines):
    first, second = values[:, :LANES], values[:, LANES:]
    return jnp.concatenate([first * cosine + second * sines, second * cosine - first * sines], axis=1)


def load_kernel(tokens_ref, *refs):
    count = len(refs) // 2 - 1
    sources, (inner_ref, other_ref, *outs), sems = refs[:count], refs[count:-1], refs[-1]
    own_len, win = tokens_ref.shape[1], HALF_WIN
    odd = lax.axis_index("seq") % 2
    copies = []
    for k, (out, high) in enumerate(((inner_ref, odd == 0), (other_ref, odd == 1))):
        at = pl.multiple_of(jnp.where(high, own_len - win, 0), win)
        copies.append(pltpu.make_async_copy(tokens_ref.at[:, pl.ds(at, win)], out, sems.at[k]))
    for k, (source, out) in enumerate(zip(sources, outs, strict=True)):
        copies.append(pltpu.make_async_copy(source, out, sems.at[k + 2]))
    for copy in copies:
        copy.start()
    for copy in copies:
        copy.wait()


def by_side(inner, other):
    odd = lax.axis_index("seq") % 2 == 1
    return jnp.where(odd, inner, other), jnp.where(odd, other, inner)


def project_kernel(
    tokens_ref,
    starts_ref,
    in_ref,
    gain_ref,
    base_ref,
    table_ref,
    normed_ref,
    queries_ref,
    keys_ref,
    values_ref,
    weight_ref,
    angles_ref,
    bounds_ref,
):
    rows, own_len, width = tokens_ref.shape
    win = HALF_WIN
    place = lax.axis_index("seq")
    start = place * own_len
    row_len = own_len * lax.axis_size("seq")

    base_cos, base_sin = base_ref[place, 0:1], base_ref[place, 1:2]
    angles_ref[0] = base_cos * table_ref[0] - base_sin * table_ref[1]
    angles_ref[1] = base_sin * table_ref[0] + base_cos * table_ref[1]

    lane = iota((rows, own_len - 2 * win + 4 * win), 1)
    mid = own_len - 2 * win
    pos = start + jnp.where(
        lane < mid, lane + win, jnp.where(lane < mid + 2 * win, lane % win, own_len - win + lane % win)
    )
    first, last = jnp.maximum(pos - win, 0), jnp.minimum(pos + win, row_len - 1)
    for j in range(starts_ref.shape[1]):
        cut = starts_ref[:, j : j + 1]
        first = jnp.maximum(first, jnp.where(cut <= pos, cut, 0))
        last = jnp.minimum(last, jnp.where(cut > pos, cut - 1, row_len))
    for r in range(rows):
        bounds_ref[r, 0:1] = first[r : r + 1]
        bounds_ref[r, 1:2] = last[r : r + 1]

    order = halves_first()
    for c in range(0, 2 * width, WIDE):
        weight_ref[:, c : c + WIDE] = nn(in_ref[:, c : c + WIDE], order).astype(BF16)
    weight_ref[:, 2 * width :] = in_ref[:, 2 * width :]

    pair = 6
    cosine, sines = angles_ref[0, win : win + own_len], angles_ref[1, win : win + own_len]
    cosine, sines = jnp.concatenate([cosine] * pair), jnp.concatenate([sines] * pair)

    @pl.loop(0, rows // pair)
    def _(i):
        at = pl.ds(i * pair, pair)
        unit, _ = normalize(flat(tokens_ref[at]).astype(F32))
        normed = (unit * gain_ref[...]).astype(BF16)
        normed_ref[at] = normed.reshape(pair, own_len, width)
        queries, keys = nn(normed, weight_ref[:, :width]), nn(normed, weight_ref[:, width : 2 * width])
        for c in range(0, width, WIDE):
            part = turn(queries[:, c : c + WIDE], cosine * SCALE, sines * SCALE)
            queries_ref[at, :, c : c + WIDE] = part.astype(BF16).reshape(pair, own_len, WIDE)
            part = turn(keys[:, c : c + WIDE], cosine, sines)
            keys_ref[at, :, c : c + WIDE] = part.astype(BF16).reshape(pair, own_len, WIDE)
        values_ref[at] = nn(normed, weight_ref[:, 2 * width :]).astype(BF16).reshape(pair, own_len, width)


def halo_kernel(inner_ref, other_ref, weight_ref, gain_ref, angles_ref, normed_ref, keys_ref, values_ref):
    rows, win, width = inner_ref.shape
    pair = 3
    span = angles_ref.shape[1]
    cosine = jnp.concatenate([angles_ref[0, :win], angles_ref[0, span - win :]] * pair)
    sines = jnp.concatenate([angles_ref[1, :win], angles_ref[1, span - win :]] * pair)

    @pl.loop(0, rows // pair)
    def _(i):
        at = pl.ds(i * pair, pair)
        sides = by_side(inner_ref[at], other_ref[at])
        unit, _ = normalize(flat(jnp.concatenate(sides, axis=1)).astype(F32))
        normed = (unit * gain_ref[...]).astype(BF16)
        normed_ref[at] = normed.reshape(pair, 2 * win, width)
        keys = nn(normed, weight_ref[:, width : 2 * width])
        for c in range(0, width, WIDE):
            part = turn(keys[:, c : c + WIDE], cosine, sines)
            keys_ref[at, :, c : c + WIDE] = part.astype(BF16).reshape(pair, 2 * win, WIDE)
        values_ref[at] = nn(normed, weight_ref[:, 2 * width :]).astype(BF16).reshape(pair, 2 * win, width)


def bias_of(bounds_ref, row, lanes, first_key, keys):
    key = first_key + iota((keys, LANES), 0)
    first, last = bounds_ref[row, 0:1, lanes], bounds_ref[row, 1:2, lanes]
    return jnp.where((key >= first) & (key <= last), 0.0, -jnp.inf)


def probabilities(scores, bias):
    parts = []
    for c in range(0, scores.shape[1], LANES):
        part = scores[:, c : c + LANES] + bias
        part = jnp.exp(part - jnp.max(part, axis=0, keepdims=True))
        parts.append(part * (1.0 / jnp.sum(part, axis=0, keepdims=True)))
    return jnp.concatenate(parts, axis=1)


def attend_mid_kernel(queries_ref, keys_ref, values_ref, bounds_ref, attended_ref, probs_ref):
    rows, own_len, width = queries_ref.shape
    win = HALF_WIN
    mid = own_len - 2 * win
    start = lax.axis_index("seq") * own_len
    pair = 6

    @pl.loop(0, rows // pair)
    def _(i):
        for r in range(pair):
            row = i * pair + r
            bias = bias_of(bounds_ref, row, slice(0, mid), start, own_len)
            for g in range(width // WIDE):
                cols = slice(g * WIDE, (g + 1) * WIDE)
                probs = probabilities(
                    nt(keys_ref[row, :, cols], by_head(queries_ref[row, win : win + mid, cols], True)), bias
                )
                probs_ref[row, g] = probs
                out = tn(probs.astype(BF16), values_ref[row, :, cols])
                attended_ref[row, :, cols] = pick_heads(out, False).astype(BF16)


def wide_side(own, halo, side):
    win = HALF_WIN
    if side == 0:
        return jnp.concatenate([halo[:win], own[: 2 * win]], axis=0)
    return jnp.concatenate([own[own.shape[0] - 2 * win :], halo[win:]], axis=0)


def attend_out_kernel(
    queries_ref, keys_ref, values_ref, halo_keys_ref, halo_values_ref, bounds_ref, attended_ref, probs_ref
):
    rows, own_len, width = queries_ref.shape
    win = HALF_WIN
    mid = own_len - 2 * win
    start = lax.axis_index("seq") * own_len
    pair = 6

    @pl.loop(0, rows // pair)
    def _(i):
        for r in range(pair):
            row = i * pair + r
            for side in range(2):
                own = slice(0, win) if side == 0 else slice(own_len - win, own_len)
                lanes = slice(mid + side * LANES, mid + (side + 1) * LANES)
                bias = bias_of(bounds_ref, row, lanes, start + own.start - win, 3 * win)
                for g in range(width // WIDE):
                    cols = slice(g * WIDE, (g + 1) * WIDE)
                    keys = wide_side(keys_ref[row, :, cols], halo_keys_ref[row, :, cols], side)
                    values = wide_side(values_ref[row, :, cols], halo_values_ref[row, :, cols], side)
                    probs = probabilities(nt(keys, by_head(queries_ref[row, own, cols], True)), bias)
                    probs_ref[row, side, g] = probs
                    out = tn(probs.astype(BF16), values)
                    attended_ref[row, side * win : (side + 1) * win, cols] = pick_heads(out, False).astype(BF16)


def gelu_parts(gate):
    bell = jnp.exp(-0.5 * gate * gate)
    t = 1.0 / (1.0 + (0.3275911 * 0.7071067811865476) * jnp.abs(gate))
    tail = t * (
        0.5 * 0.254829592
        + t * (0.5 * -0.284496736 + t * (0.5 * 1.421413741 + t * (0.5 * -1.453152027 + t * (0.5 * 1.061405429))))
    )
    tail = tail * bell
    return jnp.where(gate < 0, tail, 1.0 - tail), gate * bell * 0.3989422804014327


def part_of(ref, at, outer):
    own_len, win = ref.shape[1], HALF_WIN
    if outer:
        return flat(jnp.concatenate([ref[at, :win], ref[at, own_len - win :]], axis=1))
    return flat(ref[at, win : own_len - win])


def dense_kernel(
    outer,
    tokens_ref,
    top_ref,
    attended_ref,
    out_ref,
    up_ref,
    down_ref,
    gain_ref,
    middle_ref,
    normed_ref,
    mixed_ref,
    grad_up_ref,
    grad_middle_ref,
    branch_ref,
    grad_attended_ref,
):
    rows, count, width = attended_ref.shape
    hidden = down_ref.shape[0]
    pair = 3

    @pl.loop(0, rows // pair)
    def _(i):
        at = pl.ds(i * pair, pair)

        def put(ref, values, cols=slice(None)):
            ref[at, :, cols] = values.reshape(pair, count, -1)

        top = part_of(top_ref, at, outer)
        middle = part_of(tokens_ref, at, outer).astype(F32) + nn(flat(attended_ref[at]), out_ref[...])
        put(middle_ref, middle)
        unit, inverse = normalize(middle)
        normed = (unit * gain_ref[...]).astype(BF16)
        put(normed_ref, normed)
        grad_hidden = [nt(top, down_ref[:512]), nt(top, down_ref[512:])]
        for c in range(0, hidden, 256):
            halves = [up_ref[:, c : c + 256], up_ref[:, hidden + c : hidden + c + 256]]
            both = nn(normed, jnp.concatenate(halves, axis=1))
            gate, lift = both[:, :256], both[:, 256:]
            grad_mixed = grad_hidden[c // 512][:, c % 512 : c % 512 + 256]
            phi, slope = gelu_parts(gate)
            active = gate * phi
            put(mixed_ref, (active * lift).astype(BF16), slice(c, c + 256))
            put(grad_up_ref, (grad_mixed * lift * (phi + slope)).astype(BF16), slice(c, c + 256))
            put(grad_up_ref, (grad_mixed * active).astype(BF16), slice(hidden + c, hidden + c + 256))
        grad_normed = nt(flat(grad_up_ref[at]), up_ref[...])
        grad_middle = top.astype(F32) + norm_back(grad_normed * gain_ref[...], unit, inverse)
        put(grad_middle_ref, grad_middle)
        branch = grad_middle.astype(BF16)
        put(branch_ref, branch)
        put(grad_attended_ref, nt(branch, out_ref[...]).astype(BF16))


def store_blocks(keep_ref, send_ref, store):
    seq, dp = lax.axis_index("seq"), lax.axis_index("dp")
    place = (dp % 2) * 16 + (dp // 2) * 8 + (seq % 2) * 4 + (seq // 2) % 2 * 2 + (seq // 4) % 2
    for ref, base in ((keep_ref, 0), (send_ref, BLOCKS // 2)):

        @pl.loop(0, BLOCKS // 2)
        def _(i):
            store(ref, i, place ^ (i + base))


def weights_kernel(
    outer,
    top_ref,
    normed_ref,
    grad_up_ref,
    mixed_ref,
    attended_ref,
    branch_ref,
    *refs,
):
    begun, (*sums,) = (refs[:3], refs[3:]) if outer else ((None,) * 3, refs)
    if outer:
        keep_ref, send_ref, *sums = sums
    up_sum, down_sum, out_sum = sums
    width = top_ref.shape[2]

    def add(part, ref, at):
        return part if ref is None else part + ref[at].astype(F32)

    normed = flat(normed_ref[...])
    for c in range(0, up_sum.shape[1], 512):
        at = (slice(None), slice(c, c + 512))
        up_sum[at] = add(tn(normed, flat(grad_up_ref[:, :, c : c + 512])), begun[0], at).astype(BF16)
    top = part_of(top_ref, slice(0, top_ref.shape[0]), outer)
    for c in range(0, down_sum.shape[0], 256):
        at = (slice(c, c + 256), slice(None))
        down_sum[at] = add(tn(flat(mixed_ref[:, :, c : c + 256]), top), begun[1], at).astype(down_sum.dtype)
    at = (slice(None), slice(None))
    out_sum[at] = add(tn(flat(attended_ref[...]), flat(branch_ref[...])), begun[2], at).astype(BF16)
    if not outer:
        return
    rows, down_rows = width // BLOCKS, down_sum.shape[0] // BLOCKS

    def store(ref, i, block):
        own = pl.ds(pl.multiple_of(block * rows, rows), rows)
        at = 0
        for c in range(0, up_sum.shape[1], width):
            ref[i, at : at + rows] = up_sum[own, c : c + width]
            at += rows
        ref[i, at : at + rows] = out_sum[own, :]
        at += rows
        ref[i, at:] = down_sum[pl.ds(pl.multiple_of(block * down_rows, down_rows), down_rows), :].astype(BF16)

    store_blocks(keep_ref, send_ref, store)


def attend_back_kernel(
    group,
    queries_ref,
    keys_ref,
    values_ref,
    halo_keys_ref,
    halo_values_ref,
    mid_grad_ref,
    out_grad_ref,
    mid_probs_ref,
    out_probs_ref,
    angles_ref,
    own_ref,
    halo_ref,
):
    rows, own_len, _ = queries_ref.shape
    win = HALF_WIN
    mid = own_len - 2 * win
    cols = slice(group * WIDE, (group + 1) * WIDE)
    cosine, sines = angles_ref[0], angles_ref[1]
    own_cos, own_sin = cosine[win : win + own_len], sines[win : win + own_len]
    halo_cos = jnp.concatenate([cosine[:win], cosine[win + own_len :]])
    halo_sin = jnp.concatenate([sines[:win], sines[win + own_len :]])
    pair = 2

    def unit(queries, keys, values, grads, probs):
        q4, g4 = by_head(queries, True), by_head(grads, False)
        grad_probs = nt(values, g4)
        lows, grad_scores = [], []
        for c in range(0, probs.shape[1], LANES):
            part, grad_part = probs[:, c : c + LANES], grad_probs[:, c : c + LANES]
            inner = jnp.sum(part * grad_part, axis=0, keepdims=True)
            lows.append(part.astype(BF16))
            grad_scores.append((part * (grad_part - inner)).astype(BF16))
        grad_scores = jnp.concatenate(grad_scores, axis=1)
        return (
            pick_heads(tn(grad_scores, keys), True),
            nn(grad_scores, q4),
            nn(jnp.concatenate(lows, axis=1), g4),
        )

    @pl.loop(0, rows // pair)
    def _(i):
        for r in range(pair):
            row = i * pair + r
            queries, keys, values = queries_ref[row, :, cols], keys_ref[row, :, cols], values_ref[row, :, cols]
            halo_keys, halo_values = halo_keys_ref[row, :, cols], halo_values_ref[row, :, cols]
            grads = out_grad_ref[row, :, cols]
            middle = unit(queries[win : win + mid], keys, values, mid_grad_ref[row, :, cols], mid_probs_ref[row, group])
            sides = [
                unit(
                    queries[:win] if side == 0 else queries[own_len - win :],
                    wide_side(keys, halo_keys, side),
                    wide_side(values, halo_values, side),
                    grads[side * win : (side + 1) * win],
                    out_probs_ref[row, side, group],
                )
                for side in range(2)
            ]
            low, high = sides
            own = [jnp.concatenate([low[0], middle[0], high[0]], axis=0) * SCALE]
            halo = []
            for k in (1, 2):
                own.append(middle[k] + jnp.concatenate([low[k][win:], high[k][: 2 * win]], axis=0))
                halo.append(jnp.concatenate([low[k][:win], high[k][2 * win :]], axis=0))
            own_ref[row, :, :WIDE] = turn_back(own[0], own_cos, own_sin).astype(BF16)
            own_ref[row, :, WIDE : 2 * WIDE] = turn_back(own[1], own_cos, own_sin).astype(BF16)
            own_ref[row, :, 2 * WIDE :] = own[2].astype(BF16)
            halo_ref[row, :, :WIDE] = turn_back(halo[0], halo_cos, halo_sin).astype(BF16)
            halo_ref[row, :, WIDE:] = halo[1].astype(BF16)


def weight_in_kernel(normed_ref, halo_normed_ref, *refs):
    *grads, total = refs
    width = normed_ref.shape[2]
    normed, halo_normed = flat(normed_ref[...]), flat(halo_normed_ref[...])
    order = halves_first()
    for k in range(3):
        part = tn(normed, jnp.concatenate([flat(own[:, :, k * WIDE : (k + 1) * WIDE]) for own in grads[::2]], axis=1))
        if k > 0:
            halo = [flat(halo[:, :, (k - 1) * WIDE : k * WIDE]) for halo in grads[1::2]]
            part = part + tn(halo_normed, jnp.concatenate(halo, axis=1))
        part = part.astype(BF16)
        if k < 2:
            part = [nt(part[:, c : c + WIDE], order).astype(BF16) for c in range(0, width, WIDE)]
            part = jnp.concatenate(part, axis=1)
        total[:, k * width : (k + 1) * width] = part


def split_kernel(total_ref, keep_ref, send_ref):
    rows, width = total_ref.shape[0] // BLOCKS, total_ref.shape[0]

    def store(ref, i, block):
        own = pl.ds(pl.multiple_of(block * rows, rows), rows)
        for k in range(3):
            ref[i, k * rows : (k + 1) * rows] = total_ref[own, k * width : (k + 1) * width]

    store_blocks(keep_ref, send_ref, store)


def grad_halo_kernel(weight_ref, *refs):
    *grads, inner_ref, other_ref = refs
    rows, win, width = inner_ref.shape
    total = None
    for g, ref in enumerate(grads):
        weight = jnp.concatenate(
            [weight_ref[:, k * width + g * WIDE : k * width + (g + 1) * WIDE] for k in (1, 2)], axis=1
        )
        part = nt(flat(ref[...]), weight)
        total = part if total is None else total + part
    total = total.astype(BF16).reshape(rows, 2 * win, width)
    inner_ref[...], other_ref[...] = by_side(total[:, :win], total[:, win:])


def backward_kernel(*refs):
    shared, (weight_ref, *grads, inner_ref, other_ref) = refs[:10], refs[10:]
    for group in range(len(grads) // 2):
        attend_back_kernel(group, *shared, *grads[2 * group : 2 * group + 2])
    grad_halo_kernel(weight_ref, *grads[1::2], inner_ref, other_ref)


def grad_own_kernel(weight_ref, *refs):
    *grads, out_ref = refs
    rows, own_len, width = out_ref.shape
    pair = 2
    groups = len(grads)

    @pl.loop(0, rows // pair)
    def _(i):
        at = pl.ds(i * pair, pair)
        grad = jnp.concatenate([flat(ref[at]) for ref in grads], axis=1)
        weight = jnp.concatenate(
            [
                weight_ref[:, k * width + g * WIDE : k * width + (g + 1) * WIDE]
                for g in range(groups)
                for k in range(3)
            ],
            axis=1,
        )
        out_ref[at] = nt(grad, weight).reshape(pair, own_len, width)


def result_kernel(mid_middle_ref, out_middle_ref, mid_mixed_ref, out_mixed_ref, down_ref, result_ref):
    own_len, win = result_ref.shape[1], HALF_WIN
    pair = 3

    @pl.loop(0, result_ref.shape[0] // pair)
    def _(i):
        at = pl.ds(i * pair, pair)

        def result(middle_ref, mixed_ref):
            total = flat(middle_ref[at]) + nn(flat(mixed_ref[at]), down_ref[...])
            return total.astype(BF16).reshape(middle_ref[at].shape)

        result_ref[at, win : own_len - win] = result(mid_middle_ref, mid_mixed_ref)
        outer = result(out_middle_ref, out_mixed_ref)
        result_ref[at, :win] = outer[:, :win]
        result_ref[at, own_len - win :] = outer[:, win:]


def finish_kernel(
    tokens_ref, own_ref, inner_ref, other_ref, mid_grad_ref, out_grad_ref, gain_ref, grad_ref
):
    own_len, win = tokens_ref.shape[1], HALF_WIN

    @pl.loop(0, tokens_ref.shape[0])
    def _(row):
        unit, inverse = normalize(tokens_ref[row].astype(F32))
        own = own_ref[row]
        low, high = by_side(inner_ref[row].astype(F32), other_ref[row].astype(F32))
        grads = jnp.concatenate(
            [own[:win] + low, own[win : own_len - win], own[own_len - win :] + high],
            axis=0,
        )
        outer = out_grad_ref[row]
        middle = jnp.concatenate([outer[:win], mid_grad_ref[row], outer[win:]], axis=0)
        grad_ref[row] = middle + norm_back(grads * gain_ref[...], unit, inverse)


def place_kernel(own_ref, other_ref, weight_ref, gain_ref, *out_refs):
    *out_refs, gain_grad_ref = out_refs

    def store(ref, i, block):
        at = 0
        for out in out_refs:
            rows = out.shape[0] // BLOCKS
            for c in range(0, out.shape[1], ref.shape[2]):
                out[pl.ds(pl.multiple_of(block * rows, rows), rows), c : c + ref.shape[2]] = ref[
                    i, at : at + rows
                ].astype(F32)
                at += rows

    store_blocks(own_ref, other_ref, store)
    total = None
    for c in range(0, weight_ref.shape[1], LANES):
        part = out_refs[0][:, c : c + LANES] * weight_ref[:, c : c + LANES].astype(F32)
        total = part if total is None else total + part
    gain_grad_ref[...] = jnp.sum(total.T, axis=0, keepdims=True) / gain_ref[...]


def add_kernel(count, *refs):
    parts, outs = refs[:count], refs[count:]
    size = parts[0].shape[0] // len(outs)
    for k, out in enumerate(outs):
        at = slice(k * size, (k + 1) * size)
        out[...] = sum(p[at].astype(F32) for p in parts).astype(BF16)


def join_kernel(*refs):
    *parts, out = refs
    size = parts[0].shape[0]
    for k, part in enumerate(parts):
        out[k * size : (k + 1) * size] = part[...]


def to_neighbours(inner, other):
    size = lax.axis_size("seq")
    pairs = [(i, i ^ 1) for i in range(size)]
    between = [p for i in range(1, size - 1, 2) for p in ((i, i + 1), (i + 1, i))]
    return lax.ppermute(inner, "seq", pairs), lax.ppermute(other, "seq", between)


def swap_route(core, x, y, z, rest):
    dp, seq = lax.axis_size("dp"), lax.axis_size("seq")

    def partner(i):
        d, s = divmod(i, seq)
        return (d ^ (core + 2 * x)) * seq + (s ^ (y + 2 * z + 8 * rest))

    return [(i, partner(i)) for i in range(dp * seq)]


def swap(values, core=0, x=0, y=0, z=0, rest=0):
    return lax.ppermute(values, ("dp", "seq"), swap_route(core, x, y, z, rest))


def shape(*dims, kind=BF16):
    return jax.ShapeDtypeStruct(dims, kind)


def call(name, kernel, outs, *args, after=(), token=False, grant=6, flops=1e9, scratch=()):
    outs = [*outs, shape(8, LANES, kind=F32)] if token else outs
    spec = pl.BlockSpec(memory_space=pltpu.VMEM)
    moved = sum(int(np.prod(a.shape)) * a.dtype.itemsize for a in (*args, *outs))

    def body(*refs):
        refs = refs[len(after) :]
        if token:
            at = len(args) + len(outs) - 1
            refs[at][...] = jnp.zeros_like(refs[at])
            refs = refs[:at] + refs[at + 1 :]
        return kernel(*refs)

    return pl.pallas_call(
        body,
        out_shape=outs,
        in_specs=[pl.BlockSpec(memory_space=pl.ANY)] * len(after) + [spec] * len(args),
        out_specs=[spec] * len(outs),
        scratch_shapes=scratch,
        compiler_params=pltpu.CompilerParams(vmem_limit_bytes=grant * MB),
        cost_estimate=pl.CostEstimate(flops=int(flops) // 100, bytes_accessed=moved // 100, transcendentals=0),
        name=name,
    )(*after, *args)


def add_up(parts, outs, after=()):
    return call("add", functools.partial(add_kernel, len(parts)), outs, *parts, after=after, grant=4, flops=1e6)


def join(parts, after=()):
    size = parts[0].shape
    out = shape(len(parts) * size[0], *size[1:])
    return call("join", join_kernel, [out], *parts, after=after, grant=4, flops=1e6)[0]


def swap_plane(parts):
    return [swap(parts[k], x=k >> 1, y=k & 1) for k in (1, 2, 3)]


def swap_rest(own):
    rest = 1
    while 8 * rest < lax.axis_size("seq"):
        (own,) = add_up([own, swap(own, rest=rest)], [shape(*own.shape)])
        rest *= 2
    return own


def angle_tables(own_len, pieces):
    inverse = ROTARY_BASE ** (-(np.arange(0, HEAD_DIM, 2) / HEAD_DIM))
    inverse = np.tile(inverse, LANES // HALF)
    base = np.arange(pieces)[:, None] * own_len * inverse
    local = (np.arange(own_len + 2 * HALF_WIN) - HALF_WIN)[:, None] * inverse
    return [jnp.asarray(np.stack([np.cos(a), np.sin(a)], axis=d), F32) for a, d in ((base, 1), (local, 0))]


def shards(
    tokens,
    document_starts,
    attention_in,
    attention_out,
    feedforward_in,
    feedforward_out,
    gain_first,
    gain_second,
    result_grad,
):
    rows, own_len, width = tokens.shape
    hidden = feedforward_out.shape[0]
    win = HALF_WIN
    mid = own_len - 2 * win
    seq = lax.axis_size("seq")
    groups = width // WIDE
    gain_one, gain_two = gain_first[None], gain_second[None]

    small = [document_starts, gain_one, attention_in, *angle_tables(own_len, seq)]
    outs = [pltpu.VMEM((rows, win, width), BF16)] * 2 + [pltpu.VMEM(a.shape, a.dtype) for a in small]
    inner_tokens, other_tokens, document_starts, gain_one, attention_in, *tables = pl.pallas_call(
        load_kernel,
        out_shape=outs,
        in_specs=[pl.BlockSpec(memory_space=pltpu.HBM)] * (1 + len(small)),
        out_specs=[pl.BlockSpec(memory_space=pltpu.VMEM)] * len(outs),
        scratch_shapes=[pltpu.SemaphoreType.DMA((len(outs),))],
        compiler_params=pltpu.CompilerParams(vmem_limit_bytes=MB),
        name="load",
    )(*[pltpu.with_memory_space_constraint(a, pltpu.HBM) for a in (tokens, *small)])
    inner_halo, other_halo = to_neighbours(inner_tokens, other_tokens)

    row_shape = shape(rows, own_len, width)
    normed, queries, keys, values, weight, angles, bounds = call(
        "project",
        project_kernel,
        [row_shape] * 4
        + [
            shape(*attention_in.shape),
            shape(2, own_len + 2 * win, LANES, kind=F32),
            shape(rows, 2, mid + 4 * win, kind=jnp.int32),
        ],
        tokens,
        document_starts,
        attention_in,
        gain_one,
        *tables,
        flops=3e9,
    )
    mid_attended, mid_probs = call(
        "attend_mid",
        attend_mid_kernel,
        [shape(rows, mid, width), shape(rows, groups, own_len, GROUP * mid, kind=F32)],
        queries,
        keys,
        values,
        bounds,
        flops=2e9,
    )

    def dense(name, outer, attended):
        count = attended.shape[1]
        return call(
            name,
            functools.partial(dense_kernel, outer),
            [
                shape(rows, count, width, kind=F32),
                shape(rows, count, width),
                shape(rows, count, hidden),
                shape(rows, count, 2 * hidden),
                shape(rows, count, width, kind=F32),
                shape(rows, count, width),
                shape(rows, count, width),
            ],
            tokens,
            result_grad,
            attended,
            attention_out,
            feedforward_in,
            feedforward_out,
            gain_two,
            flops=5e9,
            grant=14,
        )

    mid_middle, mid_normed, mid_mixed, mid_grad_up, mid_grad, mid_branch, mid_grad_attended = dense(
        "dense_mid", False, mid_attended
    )

    begun = call(
        "begin",
        functools.partial(weights_kernel, False),
        [shape(*w.shape) for w in (feedforward_in, feedforward_out, attention_out)],
        result_grad,
        mid_normed,
        mid_grad_up,
        mid_mixed,
        mid_attended,
        mid_branch,
        flops=3e9,
    )

    halo_normed, halo_keys, halo_values = call(
        "halo",
        halo_kernel,
        [shape(rows, 2 * win, width)] * 3,
        inner_halo,
        other_halo,
        weight,
        gain_one,
        angles,
        flops=1e9,
        after=[begun[2]],
    )
    out_attended, out_probs = call(
        "attend_out",
        attend_out_kernel,
        [shape(rows, 2 * win, width), shape(rows, 2, groups, 3 * win, GROUP * win, kind=F32)],
        queries,
        keys,
        values,
        halo_keys,
        halo_values,
        bounds,
        flops=2e9,
    )
    out_middle, out_normed, out_mixed, out_grad_up, out_grad, out_branch, out_grad_attended = dense(
        "dense_out", True, out_attended
    )

    piece = (feedforward_in.shape[1] // width * width + width + hidden) // BLOCKS
    keep_one, send_one = call(
        "weights",
        functools.partial(weights_kernel, True),
        [shape(BLOCKS // 2, piece, width)] * 2,
        result_grad,
        out_normed,
        out_grad_up,
        out_mixed,
        out_attended,
        out_branch,
        *begun,
        flops=5e9,
        scratch=[
            pltpu.VMEM(feedforward_in.shape, BF16),
            pltpu.VMEM(feedforward_out.shape, F32),
            pltpu.VMEM(attention_out.shape, BF16),
        ],
    )

    def cut(blocks, parts):
        return [shape(blocks.shape[0] // parts, *blocks.shape[1:])] * parts

    activations, done_result = call(
        "result",
        result_kernel,
        [row_shape],
        mid_middle,
        out_middle,
        mid_mixed,
        out_mixed,
        feedforward_out,
        flops=2e9,
        after=[keep_one],
        token=True,
    )
    chip_one = add_up([keep_one, swap(send_one, core=1)], cut(keep_one, 4), after=[done_result])
    from_plane = swap_plane(chip_one)
    grad_shapes = [shape(rows, own_len, 3 * WIDE), shape(rows, 2 * win, 2 * WIDE)] * groups
    *grads, inner_grad, other_grad = call(
        "backward",
        backward_kernel,
        [shape(rows, own_len, 3 * WIDE), shape(rows, 2 * win, 2 * WIDE)] * groups + [shape(rows, win, width)] * 2,
        queries,
        keys,
        values,
        halo_keys,
        halo_values,
        mid_grad_attended,
        out_grad_attended,
        mid_probs,
        out_probs,
        angles,
        weight,
        flops=12e9,
        after=[chip_one[0]],
    )
    inner_grad, other_grad = to_neighbours(inner_grad, other_grad)
    (total_in,) = call(
        "weight_in",
        weight_in_kernel,
        [shape(*attention_in.shape)],
        normed,
        halo_normed,
        *grads,
        flops=4e9,
    )
    plane_one = add_up([chip_one[0], *from_plane], cut(chip_one[0], 2), after=[total_in])
    keep_two, send_two = call(
        "split",
        split_kernel,
        [shape(BLOCKS // 2, attention_in.shape[1] // BLOCKS, width)] * 2,
        total_in,
        flops=1e9,
        after=[plane_one[0]],
    )
    chip_two = add_up([keep_two, swap(send_two, core=1)], cut(keep_two, 4))
    near_one = add_up([plane_one[0], swap(plane_one[1], z=1)], cut(plane_one[0], 2), after=[chip_two[0]])
    from_plane = swap_plane(chip_two)
    own_grad, done_own = call(
        "grad_own",
        grad_own_kernel,
        [shape(rows, own_len, width, kind=F32)],
        weight,
        *grads[::2],
        flops=2e9,
        after=[near_one[0]],
        token=True,
    )
    (line_one,) = add_up([near_one[0], swap(near_one[1], z=2)], cut(near_one[0], 1), after=[done_own])
    line_one = swap_rest(line_one)
    plane_two = add_up([chip_two[0], *from_plane], cut(chip_two[0], 2), after=[line_one, inner_grad])
    line_one = join([line_one, swap(line_one, z=2)], after=[plane_two[0]])
    near_two = add_up([plane_two[0], swap(plane_two[1], z=1)], cut(plane_two[0], 2), after=[line_one])
    line_one = join([line_one, swap(line_one, z=1)], after=[near_two[0]])
    from_plane = swap_plane([line_one] * 4)
    (line_two,) = add_up([near_two[0], swap(near_two[1], z=2)], cut(near_two[0], 1), after=[line_one])
    line_two = swap_rest(line_two)
    line_two = join([line_two, swap(line_two, z=2)])
    line_two = join([line_two, swap(line_two, z=1)], after=[other_grad])
    from_plane_two = swap_plane([line_two] * 4)
    whole_one = join([line_one, *from_plane], after=[line_two])
    grad_tokens, done_finish = call(
        "finish",
        finish_kernel,
        [shape(rows, own_len, width, kind=F32)],
        tokens,
        own_grad,
        inner_grad,
        other_grad,
        mid_grad,
        out_grad,
        gain_one,
        flops=1e8,
        after=[whole_one],
        token=True,
    )

    def placed(parts, gain, *weights):
        outs = [shape(*w.shape, kind=F32) for w in weights] + [shape(1, width, kind=F32)]
        return call("place", place_kernel, outs, *parts, weights[0], gain, flops=1e6)

    grad_up, grad_out, grad_down, grad_gain_two = placed(
        (whole_one, swap(whole_one, core=1)), gain_two, feedforward_in, attention_out, feedforward_out
    )
    whole_two = join([line_two, *from_plane_two], after=[grad_gain_two, done_finish])
    grad_in, grad_gain_one = placed((whole_two, swap(whole_two, core=1)), gain_one, attention_in)
    return activations, grad_tokens, grad_in, grad_out, grad_up, grad_down, grad_gain_one[0], grad_gain_two[0]


def solution(mesh):
    token, rest = P("dp", "seq", None), P()
    return jax.shard_map(
        shards,
        mesh=mesh,
        in_specs=(token, P("dp", None)) + (rest,) * 6 + (token,),
        out_specs=(token, token) + (rest,) * 6,
        check_vma=False,
    )
```

```python
import functools

import jax
import jax.numpy as jnp
import numpy as np
from jax import lax
from jax.experimental import pallas as pl
from jax.experimental.pallas import tpu as pltpu
from jax.sharding import PartitionSpec as P

HEADS = 8
HEAD_DIM = 64
HALF = HEAD_DIM // 2
HALF_WIN = 64
EPSILON = 1e-05
ROTARY_BASE = 10000.0
SCALE = HEAD_DIM**-0.5
BLOCKS = 32
GROUP = 4
WIDE = GROUP * HEAD_DIM
LANES = 128
MB = 1024 * 1024

F32 = jnp.float32
BF16 = jnp.bfloat16


def dot(a, b, contract):
    return lax.dot_general(a, b, ((contract[:1], contract[1:]), ((), ())), preferred_element_type=F32)


def nn(a, b):
    return dot(a, b, (1, 0))


def nt(a, b):
    return dot(a, b, (1, 1))


def tn(a, b):
    return dot(a, b, (0, 0))


def iota(shape, dim):
    return lax.broadcasted_iota(jnp.int32, shape, dim)


def flat(values):
    return values.reshape(-1, values.shape[-1])


def normalize(values):
    shifted = values - jnp.mean(values, axis=-1, keepdims=True)
    inverse = lax.rsqrt(jnp.mean(shifted * shifted, axis=-1, keepdims=True) + EPSILON)
    return shifted * inverse, inverse


def norm_back(scaled_grad, unit, inverse):
    return (
        scaled_grad
        - jnp.mean(scaled_grad, axis=-1, keepdims=True)
        - unit * jnp.mean(scaled_grad * unit, axis=-1, keepdims=True)
    ) * inverse


def halves_first():
    old, new = iota((WIDE, WIDE), 0), iota((WIDE, WIDE), 1)
    moved = (old % HEAD_DIM) // HALF * LANES + old // HEAD_DIM * HALF + old % HALF
    return (moved == new).astype(BF16)


def head_of(shape, halved):
    lane = iota(shape, 1)
    return lane % LANES // HALF if halved else lane // HEAD_DIM


def by_head(values, halved):
    head = head_of(values.shape, halved)
    zero = jnp.zeros_like(values)
    return jnp.concatenate([jnp.where(head == h, values, zero) for h in range(GROUP)], axis=0)


def pick_heads(stacked, halved):
    count = stacked.shape[0] // GROUP
    head = head_of((count, stacked.shape[1]), halved)
    out = stacked[:count]
    for h in range(1, GROUP):
        out = jnp.where(head == h, stacked[h * count : (h + 1) * count], out)
    return out


def turn(values, cosine, sines):
    first, second = values[:, :LANES], values[:, LANES:]
    return jnp.concatenate([first * cosine - second * sines, second * cosine + first * sines], axis=1)


def turn_back(values, cosine, sines):
    first, second = values[:, :LANES], values[:, LANES:]
    return jnp.concatenate([first * cosine + second * sines, second * cosine - first * sines], axis=1)


def load_kernel(tokens_ref, *refs):
    count = len(refs) // 2 - 1
    sources, (inner_ref, other_ref, *outs), sems = refs[:count], refs[count:-1], refs[-1]
    own_len, win = tokens_ref.shape[1], HALF_WIN
    odd = lax.axis_index("seq") % 2
    copies = []
    for k, (out, high) in enumerate(((inner_ref, odd == 0), (other_ref, odd == 1))):
        at = pl.multiple_of(jnp.where(high, own_len - win, 0), win)
        copies.append(pltpu.make_async_copy(tokens_ref.at[:, pl.ds(at, win)], out, sems.at[k]))
    for k, (source, out) in enumerate(zip(sources, outs, strict=True)):
        copies.append(pltpu.make_async_copy(source, out, sems.at[k + 2]))
    for copy in copies:
        copy.start()
    for copy in copies:
        copy.wait()


def by_side(inner, other):
    odd = lax.axis_index("seq") % 2 == 1
    return jnp.where(odd, inner, other), jnp.where(odd, other, inner)


def project_kernel(
    tokens_ref,
    starts_ref,
    in_ref,
    gain_ref,
    base_ref,
    table_ref,
    normed_ref,
    queries_ref,
    keys_ref,
    values_ref,
    weight_ref,
    angles_ref,
    bounds_ref,
):
    rows, own_len, width = tokens_ref.shape
    win = HALF_WIN
    place = lax.axis_index("seq")
    start = place * own_len
    row_len = own_len * lax.axis_size("seq")

    base_cos, base_sin = base_ref[place, 0:1], base_ref[place, 1:2]
    angles_ref[0] = base_cos * table_ref[0] - base_sin * table_ref[1]
    angles_ref[1] = base_sin * table_ref[0] + base_cos * table_ref[1]

    lane = iota((rows, own_len - 2 * win + 4 * win), 1)
    mid = own_len - 2 * win
    pos = start + jnp.where(
        lane < mid, lane + win, jnp.where(lane < mid + 2 * win, lane % win, own_len - win + lane % win)
    )
    first, last = jnp.maximum(pos - win, 0), jnp.minimum(pos + win, row_len - 1)
    for j in range(starts_ref.shape[1]):
        cut = starts_ref[:, j : j + 1]
        first = jnp.maximum(first, jnp.where(cut <= pos, cut, 0))
        last = jnp.minimum(last, jnp.where(cut > pos, cut - 1, row_len))
    for r in range(rows):
        bounds_ref[r, 0:1] = first[r : r + 1]
        bounds_ref[r, 1:2] = last[r : r + 1]

    order = halves_first()
    for c in range(0, 2 * width, WIDE):
        weight_ref[:, c : c + WIDE] = nn(in_ref[:, c : c + WIDE], order).astype(BF16)
    weight_ref[:, 2 * width :] = in_ref[:, 2 * width :]

    pair = 6
    cosine, sines = angles_ref[0, win : win + own_len], angles_ref[1, win : win + own_len]
    cosine, sines = jnp.concatenate([cosine] * pair), jnp.concatenate([sines] * pair)

    @pl.loop(0, rows // pair)
    def _(i):
        at = pl.ds(i * pair, pair)
        unit, _ = normalize(flat(tokens_ref[at]).astype(F32))
        normed = (unit * gain_ref[...]).astype(BF16)
        normed_ref[at] = normed.reshape(pair, own_len, width)
        queries, keys = nn(normed, weight_ref[:, :width]), nn(normed, weight_ref[:, width : 2 * width])
        for c in range(0, width, WIDE):
            part = turn(queries[:, c : c + WIDE], cosine * SCALE, sines * SCALE)
            queries_ref[at, :, c : c + WIDE] = part.astype(BF16).reshape(pair, own_len, WIDE)
            part = turn(keys[:, c : c + WIDE], cosine, sines)
            keys_ref[at, :, c : c + WIDE] = part.astype(BF16).reshape(pair, own_len, WIDE)
        values_ref[at] = nn(normed, weight_ref[:, 2 * width :]).astype(BF16).reshape(pair, own_len, width)


def halo_kernel(inner_ref, other_ref, weight_ref, gain_ref, angles_ref, normed_ref, keys_ref, values_ref):
    rows, win, width = inner_ref.shape
    pair = 3
    span = angles_ref.shape[1]
    cosine = jnp.concatenate([angles_ref[0, :win], angles_ref[0, span - win :]] * pair)
    sines = jnp.concatenate([angles_ref[1, :win], angles_ref[1, span - win :]] * pair)

    @pl.loop(0, rows // pair)
    def _(i):
        at = pl.ds(i * pair, pair)
        sides = by_side(inner_ref[at], other_ref[at])
        unit, _ = normalize(flat(jnp.concatenate(sides, axis=1)).astype(F32))
        normed = (unit * gain_ref[...]).astype(BF16)
        normed_ref[at] = normed.reshape(pair, 2 * win, width)
        keys = nn(normed, weight_ref[:, width : 2 * width])
        for c in range(0, width, WIDE):
            part = turn(keys[:, c : c + WIDE], cosine, sines)
            keys_ref[at, :, c : c + WIDE] = part.astype(BF16).reshape(pair, 2 * win, WIDE)
        values_ref[at] = nn(normed, weight_ref[:, 2 * width :]).astype(BF16).reshape(pair, 2 * win, width)


def bias_of(bounds_ref, row, lanes, first_key, keys):
    key = first_key + iota((keys, LANES), 0)
    first, last = bounds_ref[row, 0:1, lanes], bounds_ref[row, 1:2, lanes]
    return jnp.where((key >= first) & (key <= last), 0.0, -jnp.inf)


def probabilities(scores, bias):
    parts = []
    for c in range(0, scores.shape[1], LANES):
        part = scores[:, c : c + LANES] + bias
        part = jnp.exp(part - jnp.max(part, axis=0, keepdims=True))
        parts.append(part * (1.0 / jnp.sum(part, axis=0, keepdims=True)))
    return jnp.concatenate(parts, axis=1)


def attend_mid_kernel(queries_ref, keys_ref, values_ref, bounds_ref, attended_ref, probs_ref):
    rows, own_len, width = queries_ref.shape
    win = HALF_WIN
    mid = own_len - 2 * win
    start = lax.axis_index("seq") * own_len
    pair = 6

    @pl.loop(0, rows // pair)
    def _(i):
        for r in range(pair):
            row = i * pair + r
            bias = bias_of(bounds_ref, row, slice(0, mid), start, own_len)
            for g in range(width // WIDE):
                cols = slice(g * WIDE, (g + 1) * WIDE)
                probs = probabilities(
                    nt(keys_ref[row, :, cols], by_head(queries_ref[row, win : win + mid, cols], True)), bias
                )
                probs_ref[row, g] = probs
                out = tn(probs.astype(BF16), values_ref[row, :, cols])
                attended_ref[row, :, cols] = pick_heads(out, False).astype(BF16)


def wide_side(own, halo, side):
    win = HALF_WIN
    if side == 0:
        return jnp.concatenate([halo[:win], own[: 2 * win]], axis=0)
    return jnp.concatenate([own[own.shape[0] - 2 * win :], halo[win:]], axis=0)


def attend_out_kernel(
    queries_ref, keys_ref, values_ref, halo_keys_ref, halo_values_ref, bounds_ref, attended_ref, probs_ref
):
    rows, own_len, width = queries_ref.shape
    win = HALF_WIN
    mid = own_len - 2 * win
    start = lax.axis_index("seq") * own_len
    pair = 6

    @pl.loop(0, rows // pair)
    def _(i):
        for r in range(pair):
            row = i * pair + r
            for side in range(2):
                own = slice(0, win) if side == 0 else slice(own_len - win, own_len)
                lanes = slice(mid + side * LANES, mid + (side + 1) * LANES)
                bias = bias_of(bounds_ref, row, lanes, start + own.start - win, 3 * win)
                for g in range(width // WIDE):
                    cols = slice(g * WIDE, (g + 1) * WIDE)
                    keys = wide_side(keys_ref[row, :, cols], halo_keys_ref[row, :, cols], side)
                    values = wide_side(values_ref[row, :, cols], halo_values_ref[row, :, cols], side)
                    probs = probabilities(nt(keys, by_head(queries_ref[row, own, cols], True)), bias)
                    probs_ref[row, side, g] = probs
                    out = tn(probs.astype(BF16), values)
                    attended_ref[row, side * win : (side + 1) * win, cols] = pick_heads(out, False).astype(BF16)


def gelu_parts(gate):
    bell = jnp.exp(-0.5 * gate * gate)
    t = 1.0 / (1.0 + (0.3275911 * 0.7071067811865476) * jnp.abs(gate))
    tail = t * (
        0.5 * 0.254829592
        + t * (0.5 * -0.284496736 + t * (0.5 * 1.421413741 + t * (0.5 * -1.453152027 + t * (0.5 * 1.061405429))))
    )
    tail = tail * bell
    return jnp.where(gate < 0, tail, 1.0 - tail), gate * bell * 0.3989422804014327


def part_of(ref, at, outer):
    own_len, win = ref.shape[1], HALF_WIN
    if outer:
        return flat(jnp.concatenate([ref[at, :win], ref[at, own_len - win :]], axis=1))
    return flat(ref[at, win : own_len - win])


def dense_kernel(
    outer,
    tokens_ref,
    top_ref,
    attended_ref,
    out_ref,
    up_ref,
    down_ref,
    gain_ref,
    middle_ref,
    normed_ref,
    mixed_ref,
    grad_up_ref,
    grad_middle_ref,
    branch_ref,
    grad_attended_ref,
):
    rows, count, width = attended_ref.shape
    hidden = down_ref.shape[0]
    pair = 3

    @pl.loop(0, rows // pair)
    def _(i):
        at = pl.ds(i * pair, pair)

        def put(ref, values, cols=slice(None)):
            ref[at, :, cols] = values.reshape(pair, count, -1)

        top = part_of(top_ref, at, outer)
        middle = part_of(tokens_ref, at, outer).astype(F32) + nn(flat(attended_ref[at]), out_ref[...])
        put(middle_ref, middle)
        unit, inverse = normalize(middle)
        normed = (unit * gain_ref[...]).astype(BF16)
        put(normed_ref, normed)
        grad_hidden = [nt(top, down_ref[:512]), nt(top, down_ref[512:])]
        for c in range(0, hidden, 256):
            halves = [up_ref[:, c : c + 256], up_ref[:, hidden + c : hidden + c + 256]]
            both = nn(normed, jnp.concatenate(halves, axis=1))
            gate, lift = both[:, :256], both[:, 256:]
            grad_mixed = grad_hidden[c // 512][:, c % 512 : c % 512 + 256]
            phi, slope = gelu_parts(gate)
            active = gate * phi
            put(mixed_ref, (active * lift).astype(BF16), slice(c, c + 256))
            put(grad_up_ref, (grad_mixed * lift * (phi + slope)).astype(BF16), slice(c, c + 256))
            put(grad_up_ref, (grad_mixed * active).astype(BF16), slice(hidden + c, hidden + c + 256))
        grad_normed = nt(flat(grad_up_ref[at]), up_ref[...])
        grad_middle = top.astype(F32) + norm_back(grad_normed * gain_ref[...], unit, inverse)
        put(grad_middle_ref, grad_middle)
        branch = grad_middle.astype(BF16)
        put(branch_ref, branch)
        put(grad_attended_ref, nt(branch, out_ref[...]).astype(BF16))


def store_blocks(keep_ref, send_ref, store):
    seq, dp = lax.axis_index("seq"), lax.axis_index("dp")
    place = (dp % 2) * 16 + (dp // 2) * 8 + (seq % 2) * 4 + (seq // 2) % 2 * 2 + (seq // 4) % 2
    for ref, base in ((keep_ref, 0), (send_ref, BLOCKS // 2)):

        @pl.loop(0, BLOCKS // 2)
        def _(i):
            store(ref, i, place ^ (i + base))


def weights_kernel(
    outer,
    top_ref,
    normed_ref,
    grad_up_ref,
    mixed_ref,
    attended_ref,
    branch_ref,
    *refs,
):
    begun, (*sums,) = (refs[:3], refs[3:]) if outer else ((None,) * 3, refs)
    if outer:
        keep_ref, send_ref, *sums = sums
    up_sum, down_sum, out_sum = sums
    width = top_ref.shape[2]

    def add(part, ref, at):
        return part if ref is None else part + ref[at].astype(F32)

    normed = flat(normed_ref[...])
    for c in range(0, up_sum.shape[1], 512):
        at = (slice(None), slice(c, c + 512))
        up_sum[at] = add(tn(normed, flat(grad_up_ref[:, :, c : c + 512])), begun[0], at).astype(BF16)
    top = part_of(top_ref, slice(0, top_ref.shape[0]), outer)
    for c in range(0, down_sum.shape[0], 256):
        at = (slice(c, c + 256), slice(None))
        down_sum[at] = add(tn(flat(mixed_ref[:, :, c : c + 256]), top), begun[1], at).astype(down_sum.dtype)
    at = (slice(None), slice(None))
    out_sum[at] = add(tn(flat(attended_ref[...]), flat(branch_ref[...])), begun[2], at).astype(BF16)
    if not outer:
        return
    rows, down_rows = width // BLOCKS, down_sum.shape[0] // BLOCKS

    def store(ref, i, block):
        own = pl.ds(pl.multiple_of(block * rows, rows), rows)
        at = 0
        for c in range(0, up_sum.shape[1], width):
            ref[i, at : at + rows] = up_sum[own, c : c + width]
            at += rows
        ref[i, at : at + rows] = out_sum[own, :]
        at += rows
        ref[i, at:] = down_sum[pl.ds(pl.multiple_of(block * down_rows, down_rows), down_rows), :].astype(BF16)

    store_blocks(keep_ref, send_ref, store)


def attend_back_kernel(
    group,
    queries_ref,
    keys_ref,
    values_ref,
    halo_keys_ref,
    halo_values_ref,
    mid_grad_ref,
    out_grad_ref,
    mid_probs_ref,
    out_probs_ref,
    angles_ref,
    own_ref,
    halo_ref,
):
    rows, own_len, _ = queries_ref.shape
    win = HALF_WIN
    mid = own_len - 2 * win
    cols = slice(group * WIDE, (group + 1) * WIDE)
    cosine, sines = angles_ref[0], angles_ref[1]
    own_cos, own_sin = cosine[win : win + own_len], sines[win : win + own_len]
    halo_cos = jnp.concatenate([cosine[:win], cosine[win + own_len :]])
    halo_sin = jnp.concatenate([sines[:win], sines[win + own_len :]])
    pair = 2

    def unit(queries, keys, values, grads, probs):
        q4, g4 = by_head(queries, True), by_head(grads, False)
        grad_probs = nt(values, g4)
        lows, grad_scores = [], []
        for c in range(0, probs.shape[1], LANES):
            part, grad_part = probs[:, c : c + LANES], grad_probs[:, c : c + LANES]
            inner = jnp.sum(part * grad_part, axis=0, keepdims=True)
            lows.append(part.astype(BF16))
            grad_scores.append((part * (grad_part - inner)).astype(BF16))
        grad_scores = jnp.concatenate(grad_scores, axis=1)
        return (
            pick_heads(tn(grad_scores, keys), True),
            nn(grad_scores, q4),
            nn(jnp.concatenate(lows, axis=1), g4),
        )

    @pl.loop(0, rows // pair)
    def _(i):
        for r in range(pair):
            row = i * pair + r
            queries, keys, values = queries_ref[row, :, cols], keys_ref[row, :, cols], values_ref[row, :, cols]
            halo_keys, halo_values = halo_keys_ref[row, :, cols], halo_values_ref[row, :, cols]
            grads = out_grad_ref[row, :, cols]
            middle = unit(queries[win : win + mid], keys, values, mid_grad_ref[row, :, cols], mid_probs_ref[row, group])
            sides = [
                unit(
                    queries[:win] if side == 0 else queries[own_len - win :],
                    wide_side(keys, halo_keys, side),
                    wide_side(values, halo_values, side),
                    grads[side * win : (side + 1) * win],
                    out_probs_ref[row, side, group],
                )
                for side in range(2)
            ]
            low, high = sides
            own = [jnp.concatenate([low[0], middle[0], high[0]], axis=0) * SCALE]
            halo = []
            for k in (1, 2):
                own.append(middle[k] + jnp.concatenate([low[k][win:], high[k][: 2 * win]], axis=0))
                halo.append(jnp.concatenate([low[k][:win], high[k][2 * win :]], axis=0))
            own_ref[row, :, :WIDE] = turn_back(own[0], own_cos, own_sin).astype(BF16)
            own_ref[row, :, WIDE : 2 * WIDE] = turn_back(own[1], own_cos, own_sin).astype(BF16)
            own_ref[row, :, 2 * WIDE :] = own[2].astype(BF16)
            halo_ref[row, :, :WIDE] = turn_back(halo[0], halo_cos, halo_sin).astype(BF16)
            halo_ref[row, :, WIDE:] = halo[1].astype(BF16)


def weight_in_kernel(normed_ref, halo_normed_ref, *refs):
    *grads, total = refs
    width = normed_ref.shape[2]
    normed, halo_normed = flat(normed_ref[...]), flat(halo_normed_ref[...])
    order = halves_first()
    for k in range(3):
        part = tn(normed, jnp.concatenate([flat(own[:, :, k * WIDE : (k + 1) * WIDE]) for own in grads[::2]], axis=1))
        if k > 0:
            halo = [flat(halo[:, :, (k - 1) * WIDE : k * WIDE]) for halo in grads[1::2]]
            part = part + tn(halo_normed, jnp.concatenate(halo, axis=1))
        part = part.astype(BF16)
        if k < 2:
            part = [nt(part[:, c : c + WIDE], order).astype(BF16) for c in range(0, width, WIDE)]
            part = jnp.concatenate(part, axis=1)
        total[:, k * width : (k + 1) * width] = part


def split_kernel(total_ref, keep_ref, send_ref):
    rows, width = total_ref.shape[0] // BLOCKS, total_ref.shape[0]

    def store(ref, i, block):
        own = pl.ds(pl.multiple_of(block * rows, rows), rows)
        for k in range(3):
            ref[i, k * rows : (k + 1) * rows] = total_ref[own, k * width : (k + 1) * width]

    store_blocks(keep_ref, send_ref, store)


def grad_halo_kernel(weight_ref, *refs):
    *grads, inner_ref, other_ref = refs
    rows, win, width = inner_ref.shape
    total = None
    for g, ref in enumerate(grads):
        weight = jnp.concatenate(
            [weight_ref[:, k * width + g * WIDE : k * width + (g + 1) * WIDE] for k in (1, 2)], axis=1
        )
        part = nt(flat(ref[...]), weight)
        total = part if total is None else total + part
    total = total.astype(BF16).reshape(rows, 2 * win, width)
    inner_ref[...], other_ref[...] = by_side(total[:, :win], total[:, win:])


def backward_kernel(*refs):
    shared, (weight_ref, *grads, inner_ref, other_ref) = refs[:10], refs[10:]
    for group in range(len(grads) // 2):
        attend_back_kernel(group, *shared, *grads[2 * group : 2 * group + 2])
    grad_halo_kernel(weight_ref, *grads[1::2], inner_ref, other_ref)


def grad_own_kernel(weight_ref, *refs):
    *grads, out_ref = refs
    rows, own_len, width = out_ref.shape
    pair = 2
    groups = len(grads)

    @pl.loop(0, rows // pair)
    def _(i):
        at = pl.ds(i * pair, pair)
        grad = jnp.concatenate([flat(ref[at]) for ref in grads], axis=1)
        weight = jnp.concatenate(
            [
                weight_ref[:, k * width + g * WIDE : k * width + (g + 1) * WIDE]
                for g in range(groups)
                for k in range(3)
            ],
            axis=1,
        )
        out_ref[at] = nt(grad, weight).reshape(pair, own_len, width)


def result_kernel(mid_middle_ref, out_middle_ref, mid_mixed_ref, out_mixed_ref, down_ref, result_ref):
    own_len, win = result_ref.shape[1], HALF_WIN
    pair = 3

    @pl.loop(0, result_ref.shape[0] // pair)
    def _(i):
        at = pl.ds(i * pair, pair)

        def result(middle_ref, mixed_ref):
            total = flat(middle_ref[at]) + nn(flat(mixed_ref[at]), down_ref[...])
            return total.astype(BF16).reshape(middle_ref[at].shape)

        result_ref[at, win : own_len - win] = result(mid_middle_ref, mid_mixed_ref)
        outer = result(out_middle_ref, out_mixed_ref)
        result_ref[at, :win] = outer[:, :win]
        result_ref[at, own_len - win :] = outer[:, win:]


def finish_kernel(
    tokens_ref, own_ref, inner_ref, other_ref, mid_grad_ref, out_grad_ref, gain_ref, grad_ref
):
    own_len, win = tokens_ref.shape[1], HALF_WIN

    @pl.loop(0, tokens_ref.shape[0])
    def _(row):
        unit, inverse = normalize(tokens_ref[row].astype(F32))
        own = own_ref[row]
        low, high = by_side(inner_ref[row].astype(F32), other_ref[row].astype(F32))
        grads = jnp.concatenate(
            [own[:win] + low, own[win : own_len - win], own[own_len - win :] + high],
            axis=0,
        )
        outer = out_grad_ref[row]
        middle = jnp.concatenate([outer[:win], mid_grad_ref[row], outer[win:]], axis=0)
        grad_ref[row] = middle + norm_back(grads * gain_ref[...], unit, inverse)


def place_kernel(own_ref, other_ref, weight_ref, gain_ref, *out_refs):
    *out_refs, gain_grad_ref = out_refs

    def store(ref, i, block):
        at = 0
        for out in out_refs:
            rows = out.shape[0] // BLOCKS
            for c in range(0, out.shape[1], ref.shape[2]):
                out[pl.ds(pl.multiple_of(block * rows, rows), rows), c : c + ref.shape[2]] = ref[
                    i, at : at + rows
                ].astype(F32)
                at += rows

    store_blocks(own_ref, other_ref, store)
    total = None
    for c in range(0, weight_ref.shape[1], LANES):
        part = out_refs[0][:, c : c + LANES] * weight_ref[:, c : c + LANES].astype(F32)
        total = part if total is None else total + part
    gain_grad_ref[...] = jnp.sum(total.T, axis=0, keepdims=True) / gain_ref[...]


def add_kernel(count, *refs):
    parts, outs = refs[:count], refs[count:]
    size = parts[0].shape[0] // len(outs)
    for k, out in enumerate(outs):
        at = slice(k * size, (k + 1) * size)
        out[...] = sum(p[at].astype(F32) for p in parts).astype(BF16)


def join_kernel(*refs):
    *parts, out = refs
    size = parts[0].shape[0]
    for k, part in enumerate(parts):
        out[k * size : (k + 1) * size] = part[...]


def to_neighbours(inner, other):
    size = lax.axis_size("seq")
    pairs = [(i, i ^ 1) for i in range(size)]
    between = [p for i in range(1, size - 1, 2) for p in ((i, i + 1), (i + 1, i))]
    return lax.ppermute(inner, "seq", pairs), lax.ppermute(other, "seq", between)


def swap_route(core, x, y, z, rest):
    dp, seq = lax.axis_size("dp"), lax.axis_size("seq")

    def partner(i):
        d, s = divmod(i, seq)
        return (d ^ (core + 2 * x)) * seq + (s ^ (y + 2 * z + 8 * rest))

    return [(i, partner(i)) for i in range(dp * seq)]


def swap(values, core=0, x=0, y=0, z=0, rest=0):
    return lax.ppermute(values, ("dp", "seq"), swap_route(core, x, y, z, rest))


def shape(*dims, kind=BF16):
    return jax.ShapeDtypeStruct(dims, kind)


def call(name, kernel, outs, *args, after=(), token=False, grant=6, flops=1e9, scratch=()):
    outs = [*outs, shape(8, LANES, kind=F32)] if token else outs
    spec = pl.BlockSpec(memory_space=pltpu.VMEM)
    moved = sum(int(np.prod(a.shape)) * a.dtype.itemsize for a in (*args, *outs))

    def body(*refs):
        refs = refs[len(after) :]
        if token:
            at = len(args) + len(outs) - 1
            refs[at][...] = jnp.zeros_like(refs[at])
            refs = refs[:at] + refs[at + 1 :]
        return kernel(*refs)

    return pl.pallas_call(
        body,
        out_shape=outs,
        in_specs=[pl.BlockSpec(memory_space=pl.ANY)] * len(after) + [spec] * len(args),
        out_specs=[spec] * len(outs),
        scratch_shapes=scratch,
        compiler_params=pltpu.CompilerParams(vmem_limit_bytes=grant * MB),
        cost_estimate=pl.CostEstimate(flops=int(flops) // 100, bytes_accessed=moved // 100, transcendentals=0),
        name=name,
    )(*after, *args)


def add_up(parts, outs, after=()):
    return call("add", functools.partial(add_kernel, len(parts)), outs, *parts, after=after, grant=4, flops=1e6)


def join(parts, after=()):
    size = parts[0].shape
    out = shape(len(parts) * size[0], *size[1:])
    return call("join", join_kernel, [out], *parts, after=after, grant=4, flops=1e6)[0]


def swap_plane(parts):
    return [swap(parts[k], x=k >> 1, y=k & 1) for k in (1, 2, 3)]


def swap_rest(own):
    rest = 1
    while 8 * rest < lax.axis_size("seq"):
        (own,) = add_up([own, swap(own, rest=rest)], [shape(*own.shape)])
        rest *= 2
    return own


def angle_tables(own_len, pieces):
    inverse = ROTARY_BASE ** (-(np.arange(0, HEAD_DIM, 2) / HEAD_DIM))
    inverse = np.tile(inverse, LANES // HALF)
    base = np.arange(pieces)[:, None] * own_len * inverse
    local = (np.arange(own_len + 2 * HALF_WIN) - HALF_WIN)[:, None] * inverse
    return [jnp.asarray(np.stack([np.cos(a), np.sin(a)], axis=d), F32) for a, d in ((base, 1), (local, 0))]


def shards(
    tokens,
    document_starts,
    attention_in,
    attention_out,
    feedforward_in,
    feedforward_out,
    gain_first,
    gain_second,
    result_grad,
):
    rows, own_len, width = tokens.shape
    hidden = feedforward_out.shape[0]
    win = HALF_WIN
    mid = own_len - 2 * win
    seq = lax.axis_size("seq")
    groups = width // WIDE
    gain_one, gain_two = gain_first[None], gain_second[None]

    small = [document_starts, gain_one, attention_in, *angle_tables(own_len, seq)]
    outs = [pltpu.VMEM((rows, win, width), BF16)] * 2 + [pltpu.VMEM(a.shape, a.dtype) for a in small]
    inner_tokens, other_tokens, document_starts, gain_one, attention_in, *tables = pl.pallas_call(
        load_kernel,
        out_shape=outs,
        in_specs=[pl.BlockSpec(memory_space=pltpu.HBM)] * (1 + len(small)),
        out_specs=[pl.BlockSpec(memory_space=pltpu.VMEM)] * len(outs),
        scratch_shapes=[pltpu.SemaphoreType.DMA((len(outs),))],
        compiler_params=pltpu.CompilerParams(vmem_limit_bytes=MB),
        name="load",
    )(*[pltpu.with_memory_space_constraint(a, pltpu.HBM) for a in (tokens, *small)])
    inner_halo, other_halo = to_neighbours(inner_tokens, other_tokens)

    row_shape = shape(rows, own_len, width)
    normed, queries, keys, values, weight, angles, bounds = call(
        "project",
        project_kernel,
        [row_shape] * 4
        + [
            shape(*attention_in.shape),
            shape(2, own_len + 2 * win, LANES, kind=F32),
            shape(rows, 2, mid + 4 * win, kind=jnp.int32),
        ],
        tokens,
        document_starts,
        attention_in,
        gain_one,
        *tables,
        flops=3e9,
    )
    mid_attended, mid_probs = call(
        "attend_mid",
        attend_mid_kernel,
        [shape(rows, mid, width), shape(rows, groups, own_len, GROUP * mid, kind=F32)],
        queries,
        keys,
        values,
        bounds,
        flops=2e9,
    )

    def dense(name, outer, attended):
        count = attended.shape[1]
        return call(
            name,
            functools.partial(dense_kernel, outer),
            [
                shape(rows, count, width, kind=F32),
                shape(rows, count, width),
                shape(rows, count, hidden),
                shape(rows, count, 2 * hidden),
                shape(rows, count, width, kind=F32),
                shape(rows, count, width),
                shape(rows, count, width),
            ],
            tokens,
            result_grad,
            attended,
            attention_out,
            feedforward_in,
            feedforward_out,
            gain_two,
            flops=5e9,
            grant=14,
        )

    mid_middle, mid_normed, mid_mixed, mid_grad_up, mid_grad, mid_branch, mid_grad_attended = dense(
        "dense_mid", False, mid_attended
    )

    begun = call(
        "begin",
        functools.partial(weights_kernel, False),
        [shape(*w.shape) for w in (feedforward_in, feedforward_out, attention_out)],
        result_grad,
        mid_normed,
        mid_grad_up,
        mid_mixed,
        mid_attended,
        mid_branch,
        flops=3e9,
    )

    halo_normed, halo_keys, halo_values = call(
        "halo",
        halo_kernel,
        [shape(rows, 2 * win, width)] * 3,
        inner_halo,
        other_halo,
        weight,
        gain_one,
        angles,
        flops=1e9,
        after=[begun[2]],
    )
    out_attended, out_probs = call(
        "attend_out",
        attend_out_kernel,
        [shape(rows, 2 * win, width), shape(rows, 2, groups, 3 * win, GROUP * win, kind=F32)],
        queries,
        keys,
        values,
        halo_keys,
        halo_values,
        bounds,
        flops=2e9,
    )
    out_middle, out_normed, out_mixed, out_grad_up, out_grad, out_branch, out_grad_attended = dense(
        "dense_out", True, out_attended
    )

    piece = (feedforward_in.shape[1] // width * width + width + hidden) // BLOCKS
    keep_one, send_one = call(
        "weights",
        functools.partial(weights_kernel, True),
        [shape(BLOCKS // 2, piece, width)] * 2,
        result_grad,
        out_normed,
        out_grad_up,
        out_mixed,
        out_attended,
        out_branch,
        *begun,
        flops=5e9,
        scratch=[
            pltpu.VMEM(feedforward_in.shape, BF16),
            pltpu.VMEM(feedforward_out.shape, F32),
            pltpu.VMEM(attention_out.shape, BF16),
        ],
    )

    def cut(blocks, parts):
        return [shape(blocks.shape[0] // parts, *blocks.shape[1:])] * parts

    activations, done_result = call(
        "result",
        result_kernel,
        [row_shape],
        mid_middle,
        out_middle,
        mid_mixed,
        out_mixed,
        feedforward_out,
        flops=2e9,
        after=[keep_one],
        token=True,
    )
    chip_one = add_up([keep_one, swap(send_one, core=1)], cut(keep_one, 4), after=[done_result])
    from_plane = swap_plane(chip_one)
    grad_shapes = [shape(rows, own_len, 3 * WIDE), shape(rows, 2 * win, 2 * WIDE)] * groups
    *grads, inner_grad, other_grad = call(
        "backward",
        backward_kernel,
        [shape(rows, own_len, 3 * WIDE), shape(rows, 2 * win, 2 * WIDE)] * groups + [shape(rows, win, width)] * 2,
        queries,
        keys,
        values,
        halo_keys,
        halo_values,
        mid_grad_attended,
        out_grad_attended,
        mid_probs,
        out_probs,
        angles,
        weight,
        flops=12e9,
        after=[chip_one[0]],
    )
    inner_grad, other_grad = to_neighbours(inner_grad, other_grad)
    (total_in,) = call(
        "weight_in",
        weight_in_kernel,
        [shape(*attention_in.shape)],
        normed,
        halo_normed,
        *grads,
        flops=4e9,
    )
    plane_one = add_up([chip_one[0], *from_plane], cut(chip_one[0], 2), after=[total_in])
    keep_two, send_two = call(
        "split",
        split_kernel,
        [shape(BLOCKS // 2, attention_in.shape[1] // BLOCKS, width)] * 2,
        total_in,
        flops=1e9,
        after=[plane_one[0]],
    )
    chip_two = add_up([keep_two, swap(send_two, core=1)], cut(keep_two, 4))
    from_plane_rs = swap_plane(chip_two)
    near_one = add_up([plane_one[0], swap(plane_one[1], z=1)], cut(plane_one[0], 2), after=[chip_two[0]])
    own_grad, done_own = call(
        "grad_own",
        grad_own_kernel,
        [shape(rows, own_len, width, kind=F32)],
        weight,
        *grads[::2],
        flops=2e9,
        after=[near_one[0]],
        token=True,
    )
    (line_one0,) = add_up([near_one[0], swap(near_one[1], z=2)], cut(near_one[0], 1), after=[done_own])
    line_one0 = swap_rest(line_one0)
    plane_two = add_up([chip_two[0], *from_plane_rs], cut(chip_two[0], 2), after=[inner_grad])
    line_one6 = join([line_one0, swap(line_one0, z=2)], after=[done_own])
    near_two = add_up([plane_two[0], swap(plane_two[1], z=1)], cut(plane_two[0], 2), after=[line_one6])
    line_one7 = join([line_one6, swap(line_one6, z=1)], after=[near_two[0]])
    from_plane = swap_plane([line_one7] * 4)
    (line_two0,) = add_up([near_two[0], swap(near_two[1], z=2)], cut(near_two[0], 1), after=[line_one6])
    line_two0 = swap_rest(line_two0)
    line_two8 = join([line_two0, swap(line_two0, z=2)], after=[])
    line_two9 = join([line_two8, swap(line_two8, z=1)], after=[other_grad])
    from_plane_two = swap_plane([line_two9] * 4)
    line_two = line_two9
    whole_one = join([line_one7, *from_plane], after=[line_two9])
    grad_tokens, done_finish = call(
        "finish",
        finish_kernel,
        [shape(rows, own_len, width, kind=F32)],
        tokens,
        own_grad,
        inner_grad,
        other_grad,
        mid_grad,
        out_grad,
        gain_one,
        flops=1e8,
        after=[whole_one],
        token=True,
    )

    def placed(parts, gain, *weights):
        outs = [shape(*w.shape, kind=F32) for w in weights] + [shape(1, width, kind=F32)]
        return call("place", place_kernel, outs, *parts, weights[0], gain, flops=1e6, token=True)

    grad_up, grad_out, grad_down, grad_gain_two, done_one = placed(
        (whole_one, swap(whole_one, core=1)), gain_two, feedforward_in, attention_out, feedforward_out
    )
    whole_two = join([line_two, *from_plane_two], after=[done_one, done_finish])
    grad_in, grad_gain_one, _ = placed((whole_two, swap(whole_two, core=1)), gain_one, attention_in)
    return activations, grad_tokens, grad_in, grad_out, grad_up, grad_down, grad_gain_one[0], grad_gain_two[0]


def solution(mesh):
    token, rest = P("dp", "seq", None), P()
    return jax.shard_map(
        shards,
        mesh=mesh,
        in_specs=(token, P("dp", None)) + (rest,) * 6 + (token,),
        out_specs=(token, token) + (rest,) * 6,
        check_vma=False,
    )
```

```python
import functools

import jax
import jax.numpy as jnp
import numpy as np
from jax import lax
from jax.experimental import pallas as pl
from jax.experimental.pallas import tpu as pltpu
from jax.sharding import PartitionSpec as P

HEADS = 8
HEAD_DIM = 64
HALF = HEAD_DIM // 2
HALF_WIN = 64
EPSILON = 1e-05
ROTARY_BASE = 10000.0
SCALE = HEAD_DIM**-0.5
BLOCKS = 32
GROUP = 4
WIDE = GROUP * HEAD_DIM
LANES = 128
MB = 1024 * 1024

F32 = jnp.float32
BF16 = jnp.bfloat16


def dot(a, b, contract):
    return lax.dot_general(a, b, ((contract[:1], contract[1:]), ((), ())), preferred_element_type=F32)


def nn(a, b):
    return dot(a, b, (1, 0))


def nt(a, b):
    return dot(a, b, (1, 1))


def tn(a, b):
    return dot(a, b, (0, 0))


def iota(shape, dim):
    return lax.broadcasted_iota(jnp.int32, shape, dim)


def flat(values):
    return values.reshape(-1, values.shape[-1])


def normalize(values):
    shifted = values - jnp.mean(values, axis=-1, keepdims=True)
    inverse = lax.rsqrt(jnp.mean(shifted * shifted, axis=-1, keepdims=True) + EPSILON)
    return shifted * inverse, inverse


def norm_back(scaled_grad, unit, inverse):
    return (
        scaled_grad
        - jnp.mean(scaled_grad, axis=-1, keepdims=True)
        - unit * jnp.mean(scaled_grad * unit, axis=-1, keepdims=True)
    ) * inverse


def halves_first():
    old, new = iota((WIDE, WIDE), 0), iota((WIDE, WIDE), 1)
    moved = (old % HEAD_DIM) // HALF * LANES + old // HEAD_DIM * HALF + old % HALF
    return (moved == new).astype(BF16)


def head_of(shape, halved):
    lane = iota(shape, 1)
    return lane % LANES // HALF if halved else lane // HEAD_DIM


def by_head(values, halved):
    head = head_of(values.shape, halved)
    zero = jnp.zeros_like(values)
    return jnp.concatenate([jnp.where(head == h, values, zero) for h in range(GROUP)], axis=0)


def pick_heads(stacked, halved):
    count = stacked.shape[0] // GROUP
    head = head_of((count, stacked.shape[1]), halved)
    out = stacked[:count]
    for h in range(1, GROUP):
        out = jnp.where(head == h, stacked[h * count : (h + 1) * count], out)
    return out


def turn(values, cosine, sines):
    first, second = values[:, :LANES], values[:, LANES:]
    return jnp.concatenate([first * cosine - second * sines, second * cosine + first * sines], axis=1)


def turn_back(values, cosine, sines):
    first, second = values[:, :LANES], values[:, LANES:]
    return jnp.concatenate([first * cosine + second * sines, second * cosine - first * sines], axis=1)


def load_kernel(tokens_ref, *refs):
    count = len(refs) // 2 - 1
    sources, (inner_ref, other_ref, *outs), sems = refs[:count], refs[count:-1], refs[-1]
    own_len, win = tokens_ref.shape[1], HALF_WIN
    odd = lax.axis_index("seq") % 2
    copies = []
    for k, (out, high) in enumerate(((inner_ref, odd == 0), (other_ref, odd == 1))):
        at = pl.multiple_of(jnp.where(high, own_len - win, 0), win)
        copies.append(pltpu.make_async_copy(tokens_ref.at[:, pl.ds(at, win)], out, sems.at[k]))
    for k, (source, out) in enumerate(zip(sources, outs, strict=True)):
        copies.append(pltpu.make_async_copy(source, out, sems.at[k + 2]))
    for copy in copies:
        copy.start()
    for copy in copies:
        copy.wait()


def by_side(inner, other):
    odd = lax.axis_index("seq") % 2 == 1
    return jnp.where(odd, inner, other), jnp.where(odd, other, inner)


def project_kernel(
    tokens_ref,
    starts_ref,
    in_ref,
    gain_ref,
    base_ref,
    table_ref,
    normed_ref,
    queries_ref,
    keys_ref,
    values_ref,
    weight_ref,
    angles_ref,
    bounds_ref,
):
    rows, own_len, width = tokens_ref.shape
    win = HALF_WIN
    place = lax.axis_index("seq")
    start = place * own_len
    row_len = own_len * lax.axis_size("seq")

    base_cos, base_sin = base_ref[place, 0:1], base_ref[place, 1:2]
    angles_ref[0] = base_cos * table_ref[0] - base_sin * table_ref[1]
    angles_ref[1] = base_sin * table_ref[0] + base_cos * table_ref[1]

    lane = iota((rows, own_len - 2 * win + 4 * win), 1)
    mid = own_len - 2 * win
    pos = start + jnp.where(
        lane < mid, lane + win, jnp.where(lane < mid + 2 * win, lane % win, own_len - win + lane % win)
    )
    first, last = jnp.maximum(pos - win, 0), jnp.minimum(pos + win, row_len - 1)
    for j in range(starts_ref.shape[1]):
        cut = starts_ref[:, j : j + 1]
        first = jnp.maximum(first, jnp.where(cut <= pos, cut, 0))
        last = jnp.minimum(last, jnp.where(cut > pos, cut - 1, row_len))
    for r in range(rows):
        bounds_ref[r, 0:1] = first[r : r + 1]
        bounds_ref[r, 1:2] = last[r : r + 1]

    order = halves_first()
    for c in range(0, 2 * width, WIDE):
        weight_ref[:, c : c + WIDE] = nn(in_ref[:, c : c + WIDE], order).astype(BF16)
    weight_ref[:, 2 * width :] = in_ref[:, 2 * width :]

    pair = 6
    cosine, sines = angles_ref[0, win : win + own_len], angles_ref[1, win : win + own_len]
    cosine, sines = jnp.concatenate([cosine] * pair), jnp.concatenate([sines] * pair)

    @pl.loop(0, rows // pair)
    def _(i):
        at = pl.ds(i * pair, pair)
        unit, _ = normalize(flat(tokens_ref[at]).astype(F32))
        normed = (unit * gain_ref[...]).astype(BF16)
        normed_ref[at] = normed.reshape(pair, own_len, width)
        queries, keys = nn(normed, weight_ref[:, :width]), nn(normed, weight_ref[:, width : 2 * width])
        for c in range(0, width, WIDE):
            part = turn(queries[:, c : c + WIDE], cosine * SCALE, sines * SCALE)
            queries_ref[at, :, c : c + WIDE] = part.astype(BF16).reshape(pair, own_len, WIDE)
            part = turn(keys[:, c : c + WIDE], cosine, sines)
            keys_ref[at, :, c : c + WIDE] = part.astype(BF16).reshape(pair, own_len, WIDE)
        values_ref[at] = nn(normed, weight_ref[:, 2 * width :]).astype(BF16).reshape(pair, own_len, width)


def halo_kernel(inner_ref, other_ref, weight_ref, gain_ref, angles_ref, normed_ref, keys_ref, values_ref):
    rows, win, width = inner_ref.shape
    pair = 3
    span = angles_ref.shape[1]
    cosine = jnp.concatenate([angles_ref[0, :win], angles_ref[0, span - win :]] * pair)
    sines = jnp.concatenate([angles_ref[1, :win], angles_ref[1, span - win :]] * pair)

    @pl.loop(0, rows // pair)
    def _(i):
        at = pl.ds(i * pair, pair)
        sides = by_side(inner_ref[at], other_ref[at])
        unit, _ = normalize(flat(jnp.concatenate(sides, axis=1)).astype(F32))
        normed = (unit * gain_ref[...]).astype(BF16)
        normed_ref[at] = normed.reshape(pair, 2 * win, width)
        keys = nn(normed, weight_ref[:, width : 2 * width])
        for c in range(0, width, WIDE):
            part = turn(keys[:, c : c + WIDE], cosine, sines)
            keys_ref[at, :, c : c + WIDE] = part.astype(BF16).reshape(pair, 2 * win, WIDE)
        values_ref[at] = nn(normed, weight_ref[:, 2 * width :]).astype(BF16).reshape(pair, 2 * win, width)


def bias_of(bounds_ref, row, lanes, first_key, keys):
    key = first_key + iota((keys, LANES), 0)
    first, last = bounds_ref[row, 0:1, lanes], bounds_ref[row, 1:2, lanes]
    return jnp.where((key >= first) & (key <= last), 0.0, -jnp.inf)


def probabilities(scores, bias):
    parts = []
    for c in range(0, scores.shape[1], LANES):
        part = scores[:, c : c + LANES] + bias
        part = jnp.exp(part - jnp.max(part, axis=0, keepdims=True))
        parts.append(part * (1.0 / jnp.sum(part, axis=0, keepdims=True)))
    return jnp.concatenate(parts, axis=1)


def attend_mid_kernel(queries_ref, keys_ref, values_ref, bounds_ref, attended_ref, probs_ref):
    rows, own_len, width = queries_ref.shape
    win = HALF_WIN
    mid = own_len - 2 * win
    start = lax.axis_index("seq") * own_len
    pair = 6

    @pl.loop(0, rows // pair)
    def _(i):
        for r in range(pair):
            row = i * pair + r
            bias = bias_of(bounds_ref, row, slice(0, mid), start, own_len)
            for g in range(width // WIDE):
                cols = slice(g * WIDE, (g + 1) * WIDE)
                probs = probabilities(
                    nt(keys_ref[row, :, cols], by_head(queries_ref[row, win : win + mid, cols], True)), bias
                )
                probs_ref[row, g] = probs
                out = tn(probs.astype(BF16), values_ref[row, :, cols])
                attended_ref[row, :, cols] = pick_heads(out, False).astype(BF16)


def wide_side(own, halo, side):
    win = HALF_WIN
    if side == 0:
        return jnp.concatenate([halo[:win], own[: 2 * win]], axis=0)
    return jnp.concatenate([own[own.shape[0] - 2 * win :], halo[win:]], axis=0)


def attend_out_kernel(
    queries_ref, keys_ref, values_ref, halo_keys_ref, halo_values_ref, bounds_ref, attended_ref, probs_ref
):
    rows, own_len, width = queries_ref.shape
    win = HALF_WIN
    mid = own_len - 2 * win
    start = lax.axis_index("seq") * own_len
    pair = 6

    @pl.loop(0, rows // pair)
    def _(i):
        for r in range(pair):
            row = i * pair + r
            for side in range(2):
                own = slice(0, win) if side == 0 else slice(own_len - win, own_len)
                lanes = slice(mid + side * LANES, mid + (side + 1) * LANES)
                bias = bias_of(bounds_ref, row, lanes, start + own.start - win, 3 * win)
                for g in range(width // WIDE):
                    cols = slice(g * WIDE, (g + 1) * WIDE)
                    keys = wide_side(keys_ref[row, :, cols], halo_keys_ref[row, :, cols], side)
                    values = wide_side(values_ref[row, :, cols], halo_values_ref[row, :, cols], side)
                    probs = probabilities(nt(keys, by_head(queries_ref[row, own, cols], True)), bias)
                    probs_ref[row, side, g] = probs
                    out = tn(probs.astype(BF16), values)
                    attended_ref[row, side * win : (side + 1) * win, cols] = pick_heads(out, False).astype(BF16)


def gelu_parts(gate):
    bell = jnp.exp(-0.5 * gate * gate)
    t = 1.0 / (1.0 + (0.3275911 * 0.7071067811865476) * jnp.abs(gate))
    tail = t * (
        0.5 * 0.254829592
        + t * (0.5 * -0.284496736 + t * (0.5 * 1.421413741 + t * (0.5 * -1.453152027 + t * (0.5 * 1.061405429))))
    )
    tail = tail * bell
    return jnp.where(gate < 0, tail, 1.0 - tail), gate * bell * 0.3989422804014327


def part_of(ref, at, outer):
    own_len, win = ref.shape[1], HALF_WIN
    if outer:
        return flat(jnp.concatenate([ref[at, :win], ref[at, own_len - win :]], axis=1))
    return flat(ref[at, win : own_len - win])


def dense_kernel(
    outer,
    tokens_ref,
    top_ref,
    attended_ref,
    out_ref,
    up_ref,
    down_ref,
    gain_ref,
    middle_ref,
    normed_ref,
    mixed_ref,
    grad_up_ref,
    grad_middle_ref,
    branch_ref,
    grad_attended_ref,
):
    rows, count, width = attended_ref.shape
    hidden = down_ref.shape[0]
    pair = 3

    @pl.loop(0, rows // pair)
    def _(i):
        at = pl.ds(i * pair, pair)

        def put(ref, values, cols=slice(None)):
            ref[at, :, cols] = values.reshape(pair, count, -1)

        top = part_of(top_ref, at, outer)
        middle = part_of(tokens_ref, at, outer).astype(F32) + nn(flat(attended_ref[at]), out_ref[...])
        put(middle_ref, middle)
        unit, inverse = normalize(middle)
        normed = (unit * gain_ref[...]).astype(BF16)
        put(normed_ref, normed)
        grad_hidden = [nt(top, down_ref[:512]), nt(top, down_ref[512:])]
        for c in range(0, hidden, 256):
            halves = [up_ref[:, c : c + 256], up_ref[:, hidden + c : hidden + c + 256]]
            both = nn(normed, jnp.concatenate(halves, axis=1))
            gate, lift = both[:, :256], both[:, 256:]
            grad_mixed = grad_hidden[c // 512][:, c % 512 : c % 512 + 256]
            phi, slope = gelu_parts(gate)
            active = gate * phi
            put(mixed_ref, (active * lift).astype(BF16), slice(c, c + 256))
            put(grad_up_ref, (grad_mixed * lift * (phi + slope)).astype(BF16), slice(c, c + 256))
            put(grad_up_ref, (grad_mixed * active).astype(BF16), slice(hidden + c, hidden + c + 256))
        grad_normed = nt(flat(grad_up_ref[at]), up_ref[...])
        grad_middle = top.astype(F32) + norm_back(grad_normed * gain_ref[...], unit, inverse)
        put(grad_middle_ref, grad_middle)
        branch = grad_middle.astype(BF16)
        put(branch_ref, branch)
        put(grad_attended_ref, nt(branch, out_ref[...]).astype(BF16))


def store_blocks(keep_ref, send_ref, store):
    seq, dp = lax.axis_index("seq"), lax.axis_index("dp")
    place = (dp % 2) * 16 + (dp // 2) * 8 + (seq % 2) * 4 + (seq // 2) % 2 * 2 + (seq // 4) % 2
    for ref, base in ((keep_ref, 0), (send_ref, BLOCKS // 2)):

        @pl.loop(0, BLOCKS // 2)
        def _(i):
            store(ref, i, place ^ (i + base))


def weights_kernel(
    outer,
    top_ref,
    normed_ref,
    grad_up_ref,
    mixed_ref,
    attended_ref,
    branch_ref,
    *refs,
):
    begun, (*sums,) = (refs[:3], refs[3:]) if outer else ((None,) * 3, refs)
    if outer:
        keep_ref, send_ref, *sums = sums
    up_sum, down_sum, out_sum = sums
    width = top_ref.shape[2]

    def add(part, ref, at):
        return part if ref is None else part + ref[at].astype(F32)

    normed = flat(normed_ref[...])
    for c in range(0, up_sum.shape[1], 512):
        at = (slice(None), slice(c, c + 512))
        up_sum[at] = add(tn(normed, flat(grad_up_ref[:, :, c : c + 512])), begun[0], at).astype(BF16)
    top = part_of(top_ref, slice(0, top_ref.shape[0]), outer)
    for c in range(0, down_sum.shape[0], 256):
        at = (slice(c, c + 256), slice(None))
        down_sum[at] = add(tn(flat(mixed_ref[:, :, c : c + 256]), top), begun[1], at).astype(down_sum.dtype)
    at = (slice(None), slice(None))
    out_sum[at] = add(tn(flat(attended_ref[...]), flat(branch_ref[...])), begun[2], at).astype(BF16)
    if not outer:
        return
    rows, down_rows = width // BLOCKS, down_sum.shape[0] // BLOCKS

    def store(ref, i, block):
        own = pl.ds(pl.multiple_of(block * rows, rows), rows)
        at = 0
        for c in range(0, up_sum.shape[1], width):
            ref[i, at : at + rows] = up_sum[own, c : c + width]
            at += rows
        ref[i, at : at + rows] = out_sum[own, :]
        at += rows
        ref[i, at:] = down_sum[pl.ds(pl.multiple_of(block * down_rows, down_rows), down_rows), :].astype(BF16)

    store_blocks(keep_ref, send_ref, store)


def attend_back_kernel(
    group,
    queries_ref,
    keys_ref,
    values_ref,
    halo_keys_ref,
    halo_values_ref,
    mid_grad_ref,
    out_grad_ref,
    mid_probs_ref,
    out_probs_ref,
    angles_ref,
    own_ref,
    halo_ref,
):
    rows, own_len, _ = queries_ref.shape
    win = HALF_WIN
    mid = own_len - 2 * win
    cols = slice(group * WIDE, (group + 1) * WIDE)
    cosine, sines = angles_ref[0], angles_ref[1]
    own_cos, own_sin = cosine[win : win + own_len], sines[win : win + own_len]
    halo_cos = jnp.concatenate([cosine[:win], cosine[win + own_len :]])
    halo_sin = jnp.concatenate([sines[:win], sines[win + own_len :]])
    pair = 2

    def unit(queries, keys, values, grads, probs):
        q4, g4 = by_head(queries, True), by_head(grads, False)
        grad_probs = nt(values, g4)
        lows, grad_scores = [], []
        for c in range(0, probs.shape[1], LANES):
            part, grad_part = probs[:, c : c + LANES], grad_probs[:, c : c + LANES]
            inner = jnp.sum(part * grad_part, axis=0, keepdims=True)
            lows.append(part.astype(BF16))
            grad_scores.append((part * (grad_part - inner)).astype(BF16))
        grad_scores = jnp.concatenate(grad_scores, axis=1)
        return (
            pick_heads(tn(grad_scores, keys), True),
            nn(grad_scores, q4),
            nn(jnp.concatenate(lows, axis=1), g4),
        )

    @pl.loop(0, rows // pair)
    def _(i):
        for r in range(pair):
            row = i * pair + r
            queries, keys, values = queries_ref[row, :, cols], keys_ref[row, :, cols], values_ref[row, :, cols]
            halo_keys, halo_values = halo_keys_ref[row, :, cols], halo_values_ref[row, :, cols]
            grads = out_grad_ref[row, :, cols]
            middle = unit(queries[win : win + mid], keys, values, mid_grad_ref[row, :, cols], mid_probs_ref[row, group])
            sides = [
                unit(
                    queries[:win] if side == 0 else queries[own_len - win :],
                    wide_side(keys, halo_keys, side),
                    wide_side(values, halo_values, side),
                    grads[side * win : (side + 1) * win],
                    out_probs_ref[row, side, group],
                )
                for side in range(2)
            ]
            low, high = sides
            own = [jnp.concatenate([low[0], middle[0], high[0]], axis=0) * SCALE]
            halo = []
            for k in (1, 2):
                own.append(middle[k] + jnp.concatenate([low[k][win:], high[k][: 2 * win]], axis=0))
                halo.append(jnp.concatenate([low[k][:win], high[k][2 * win :]], axis=0))
            own_ref[row, :, :WIDE] = turn_back(own[0], own_cos, own_sin).astype(BF16)
            own_ref[row, :, WIDE : 2 * WIDE] = turn_back(own[1], own_cos, own_sin).astype(BF16)
            own_ref[row, :, 2 * WIDE :] = own[2].astype(BF16)
            halo_ref[row, :, :WIDE] = turn_back(halo[0], halo_cos, halo_sin).astype(BF16)
            halo_ref[row, :, WIDE:] = halo[1].astype(BF16)


def weight_in_kernel(normed_ref, halo_normed_ref, *refs):
    *grads, total = refs
    width = normed_ref.shape[2]
    normed, halo_normed = flat(normed_ref[...]), flat(halo_normed_ref[...])
    order = halves_first()
    for k in range(3):
        part = tn(normed, jnp.concatenate([flat(own[:, :, k * WIDE : (k + 1) * WIDE]) for own in grads[::2]], axis=1))
        if k > 0:
            halo = [flat(halo[:, :, (k - 1) * WIDE : k * WIDE]) for halo in grads[1::2]]
            part = part + tn(halo_normed, jnp.concatenate(halo, axis=1))
        part = part.astype(BF16)
        if k < 2:
            part = [nt(part[:, c : c + WIDE], order).astype(BF16) for c in range(0, width, WIDE)]
            part = jnp.concatenate(part, axis=1)
        total[:, k * width : (k + 1) * width] = part


def split_kernel(total_ref, keep_ref, send_ref):
    rows, width = total_ref.shape[0] // BLOCKS, total_ref.shape[0]

    def store(ref, i, block):
        own = pl.ds(pl.multiple_of(block * rows, rows), rows)
        for k in range(3):
            ref[i, k * rows : (k + 1) * rows] = total_ref[own, k * width : (k + 1) * width]

    store_blocks(keep_ref, send_ref, store)


def grad_halo_kernel(weight_ref, *refs):
    *grads, inner_ref, other_ref = refs
    rows, win, width = inner_ref.shape
    total = None
    for g, ref in enumerate(grads):
        weight = jnp.concatenate(
            [weight_ref[:, k * width + g * WIDE : k * width + (g + 1) * WIDE] for k in (1, 2)], axis=1
        )
        part = nt(flat(ref[...]), weight)
        total = part if total is None else total + part
    total = total.astype(BF16).reshape(rows, 2 * win, width)
    inner_ref[...], other_ref[...] = by_side(total[:, :win], total[:, win:])


def backward_kernel(*refs):
    shared, (weight_ref, *grads, inner_ref, other_ref) = refs[:10], refs[10:]
    for group in range(len(grads) // 2):
        attend_back_kernel(group, *shared, *grads[2 * group : 2 * group + 2])
    grad_halo_kernel(weight_ref, *grads[1::2], inner_ref, other_ref)


def grad_own_kernel(weight_ref, *refs):
    *grads, out_ref = refs
    rows, own_len, width = out_ref.shape
    pair = 2
    groups = len(grads)

    @pl.loop(0, rows // pair)
    def _(i):
        at = pl.ds(i * pair, pair)
        grad = jnp.concatenate([flat(ref[at]) for ref in grads], axis=1)
        weight = jnp.concatenate(
            [
                weight_ref[:, k * width + g * WIDE : k * width + (g + 1) * WIDE]
                for g in range(groups)
                for k in range(3)
            ],
            axis=1,
        )
        out_ref[at] = nt(grad, weight).reshape(pair, own_len, width)


def result_kernel(mid_middle_ref, out_middle_ref, mid_mixed_ref, out_mixed_ref, down_ref, result_ref):
    own_len, win = result_ref.shape[1], HALF_WIN
    pair = 3

    @pl.loop(0, result_ref.shape[0] // pair)
    def _(i):
        at = pl.ds(i * pair, pair)

        def result(middle_ref, mixed_ref):
            total = flat(middle_ref[at]) + nn(flat(mixed_ref[at]), down_ref[...])
            return total.astype(BF16).reshape(middle_ref[at].shape)

        result_ref[at, win : own_len - win] = result(mid_middle_ref, mid_mixed_ref)
        outer = result(out_middle_ref, out_mixed_ref)
        result_ref[at, :win] = outer[:, :win]
        result_ref[at, own_len - win :] = outer[:, win:]


def finish_kernel(
    tokens_ref, own_ref, inner_ref, other_ref, mid_grad_ref, out_grad_ref, gain_ref, grad_ref
):
    own_len, win = tokens_ref.shape[1], HALF_WIN

    @pl.loop(0, tokens_ref.shape[0])
    def _(row):
        unit, inverse = normalize(tokens_ref[row].astype(F32))
        own = own_ref[row]
        low, high = by_side(inner_ref[row].astype(F32), other_ref[row].astype(F32))
        grads = jnp.concatenate(
            [own[:win] + low, own[win : own_len - win], own[own_len - win :] + high],
            axis=0,
        )
        outer = out_grad_ref[row]
        middle = jnp.concatenate([outer[:win], mid_grad_ref[row], outer[win:]], axis=0)
        grad_ref[row] = middle + norm_back(grads * gain_ref[...], unit, inverse)


def place_kernel(own_ref, other_ref, weight_ref, gain_ref, *out_refs):
    *out_refs, gain_grad_ref = out_refs

    def store(ref, i, block):
        at = 0
        for out in out_refs:
            rows = out.shape[0] // BLOCKS
            for c in range(0, out.shape[1], ref.shape[2]):
                out[pl.ds(pl.multiple_of(block * rows, rows), rows), c : c + ref.shape[2]] = ref[
                    i, at : at + rows
                ].astype(F32)
                at += rows

    store_blocks(own_ref, other_ref, store)
    total = None
    for c in range(0, weight_ref.shape[1], LANES):
        part = out_refs[0][:, c : c + LANES] * weight_ref[:, c : c + LANES].astype(F32)
        total = part if total is None else total + part
    gain_grad_ref[...] = jnp.sum(total.T, axis=0, keepdims=True) / gain_ref[...]


def add_kernel(count, *refs):
    parts, outs = refs[:count], refs[count:]
    size = parts[0].shape[0] // len(outs)
    for k, out in enumerate(outs):
        at = slice(k * size, (k + 1) * size)
        out[...] = sum(p[at].astype(F32) for p in parts).astype(BF16)


def join_kernel(*refs):
    *parts, out = refs
    size = parts[0].shape[0]
    for k, part in enumerate(parts):
        out[k * size : (k + 1) * size] = part[...]


def to_neighbours(inner, other):
    size = lax.axis_size("seq")
    pairs = [(i, i ^ 1) for i in range(size)]
    between = [p for i in range(1, size - 1, 2) for p in ((i, i + 1), (i + 1, i))]
    return lax.ppermute(inner, "seq", pairs), lax.ppermute(other, "seq", between)


def swap_route(core, x, y, z, rest):
    dp, seq = lax.axis_size("dp"), lax.axis_size("seq")

    def partner(i):
        d, s = divmod(i, seq)
        return (d ^ (core + 2 * x)) * seq + (s ^ (y + 2 * z + 8 * rest))

    return [(i, partner(i)) for i in range(dp * seq)]


def swap(values, core=0, x=0, y=0, z=0, rest=0):
    return lax.ppermute(values, ("dp", "seq"), swap_route(core, x, y, z, rest))


def shape(*dims, kind=BF16):
    return jax.ShapeDtypeStruct(dims, kind)


def call(name, kernel, outs, *args, after=(), token=False, grant=6, flops=1e9, scratch=()):
    outs = [*outs, shape(8, LANES, kind=F32)] if token else outs
    spec = pl.BlockSpec(memory_space=pltpu.VMEM)
    moved = sum(int(np.prod(a.shape)) * a.dtype.itemsize for a in (*args, *outs))

    def body(*refs):
        refs = refs[len(after) :]
        if token:
            at = len(args) + len(outs) - 1
            refs[at][...] = jnp.zeros_like(refs[at])
            refs = refs[:at] + refs[at + 1 :]
        return kernel(*refs)

    return pl.pallas_call(
        body,
        out_shape=outs,
        in_specs=[pl.BlockSpec(memory_space=pl.ANY)] * len(after) + [spec] * len(args),
        out_specs=[spec] * len(outs),
        scratch_shapes=scratch,
        compiler_params=pltpu.CompilerParams(vmem_limit_bytes=grant * MB),
        cost_estimate=pl.CostEstimate(flops=int(flops) // 100, bytes_accessed=moved // 100, transcendentals=0),
        name=name,
    )(*after, *args)


def add_up(parts, outs, after=()):
    return call("add", functools.partial(add_kernel, len(parts)), outs, *parts, after=after, grant=4, flops=1e6)


def join(parts, after=()):
    size = parts[0].shape
    out = shape(len(parts) * size[0], *size[1:])
    return call("join", join_kernel, [out], *parts, after=after, grant=4, flops=1e6)[0]


def swap_plane(parts):
    return [swap(parts[k], x=k >> 1, y=k & 1) for k in (1, 2, 3)]


def swap_line(parts):
    return [swap(parts[k], z=(k >> 1) + 2 * (k & 1)) for k in (1, 2, 3)]


def swap_rest(own):
    rest = 1
    while 8 * rest < lax.axis_size("seq"):
        (own,) = add_up([own, swap(own, rest=rest)], [shape(*own.shape)])
        rest *= 2
    return own


def angle_tables(own_len, pieces):
    inverse = ROTARY_BASE ** (-(np.arange(0, HEAD_DIM, 2) / HEAD_DIM))
    inverse = np.tile(inverse, LANES // HALF)
    base = np.arange(pieces)[:, None] * own_len * inverse
    local = (np.arange(own_len + 2 * HALF_WIN) - HALF_WIN)[:, None] * inverse
    return [jnp.asarray(np.stack([np.cos(a), np.sin(a)], axis=d), F32) for a, d in ((base, 1), (local, 0))]


def shards(
    tokens,
    document_starts,
    attention_in,
    attention_out,
    feedforward_in,
    feedforward_out,
    gain_first,
    gain_second,
    result_grad,
):
    rows, own_len, width = tokens.shape
    hidden = feedforward_out.shape[0]
    win = HALF_WIN
    mid = own_len - 2 * win
    seq = lax.axis_size("seq")
    groups = width // WIDE
    gain_one, gain_two = gain_first[None], gain_second[None]

    small = [document_starts, gain_one, attention_in, *angle_tables(own_len, seq)]
    outs = [pltpu.VMEM((rows, win, width), BF16)] * 2 + [pltpu.VMEM(a.shape, a.dtype) for a in small]
    inner_tokens, other_tokens, document_starts, gain_one, attention_in, *tables = pl.pallas_call(
        load_kernel,
        out_shape=outs,
        in_specs=[pl.BlockSpec(memory_space=pltpu.HBM)] * (1 + len(small)),
        out_specs=[pl.BlockSpec(memory_space=pltpu.VMEM)] * len(outs),
        scratch_shapes=[pltpu.SemaphoreType.DMA((len(outs),))],
        compiler_params=pltpu.CompilerParams(vmem_limit_bytes=MB),
        name="load",
    )(*[pltpu.with_memory_space_constraint(a, pltpu.HBM) for a in (tokens, *small)])
    inner_halo, other_halo = to_neighbours(inner_tokens, other_tokens)

    row_shape = shape(rows, own_len, width)
    normed, queries, keys, values, weight, angles, bounds = call(
        "project",
        project_kernel,
        [row_shape] * 4
        + [
            shape(*attention_in.shape),
            shape(2, own_len + 2 * win, LANES, kind=F32),
            shape(rows, 2, mid + 4 * win, kind=jnp.int32),
        ],
        tokens,
        document_starts,
        attention_in,
        gain_one,
        *tables,
        flops=3e9,
    )
    mid_attended, mid_probs = call(
        "attend_mid",
        attend_mid_kernel,
        [shape(rows, mid, width), shape(rows, groups, own_len, GROUP * mid, kind=F32)],
        queries,
        keys,
        values,
        bounds,
        flops=2e9,
    )

    def dense(name, outer, attended):
        count = attended.shape[1]
        return call(
            name,
            functools.partial(dense_kernel, outer),
            [
                shape(rows, count, width, kind=F32),
                shape(rows, count, width),
                shape(rows, count, hidden),
                shape(rows, count, 2 * hidden),
                shape(rows, count, width, kind=F32),
                shape(rows, count, width),
                shape(rows, count, width),
            ],
            tokens,
            result_grad,
            attended,
            attention_out,
            feedforward_in,
            feedforward_out,
            gain_two,
            flops=5e9,
            grant=14,
        )

    mid_middle, mid_normed, mid_mixed, mid_grad_up, mid_grad, mid_branch, mid_grad_attended = dense(
        "dense_mid", False, mid_attended
    )

    begun = call(
        "begin",
        functools.partial(weights_kernel, False),
        [shape(*w.shape) for w in (feedforward_in, feedforward_out, attention_out)],
        result_grad,
        mid_normed,
        mid_grad_up,
        mid_mixed,
        mid_attended,
        mid_branch,
        flops=3e9,
    )

    halo_normed, halo_keys, halo_values = call(
        "halo",
        halo_kernel,
        [shape(rows, 2 * win, width)] * 3,
        inner_halo,
        other_halo,
        weight,
        gain_one,
        angles,
        flops=1e9,
        after=[begun[2]],
    )
    out_attended, out_probs = call(
        "attend_out",
        attend_out_kernel,
        [shape(rows, 2 * win, width), shape(rows, 2, groups, 3 * win, GROUP * win, kind=F32)],
        queries,
        keys,
        values,
        halo_keys,
        halo_values,
        bounds,
        flops=2e9,
    )
    out_middle, out_normed, out_mixed, out_grad_up, out_grad, out_branch, out_grad_attended = dense(
        "dense_out", True, out_attended
    )

    piece = (feedforward_in.shape[1] // width * width + width + hidden) // BLOCKS
    keep_one, send_one = call(
        "weights",
        functools.partial(weights_kernel, True),
        [shape(BLOCKS // 2, piece, width)] * 2,
        result_grad,
        out_normed,
        out_grad_up,
        out_mixed,
        out_attended,
        out_branch,
        *begun,
        flops=5e9,
        scratch=[
            pltpu.VMEM(feedforward_in.shape, BF16),
            pltpu.VMEM(feedforward_out.shape, F32),
            pltpu.VMEM(attention_out.shape, BF16),
        ],
    )

    def cut(blocks, parts):
        return [shape(blocks.shape[0] // parts, *blocks.shape[1:])] * parts

    activations, done_result = call(
        "result",
        result_kernel,
        [row_shape],
        mid_middle,
        out_middle,
        mid_mixed,
        out_mixed,
        feedforward_out,
        flops=2e9,
        after=[keep_one],
        token=True,
    )
    chip_one = add_up([keep_one, swap(send_one, core=1)], cut(keep_one, 4), after=[done_result])
    from_plane = swap_plane(chip_one)
    grad_shapes = [shape(rows, own_len, 3 * WIDE), shape(rows, 2 * win, 2 * WIDE)] * groups
    *grads, inner_grad, other_grad = call(
        "backward",
        backward_kernel,
        [shape(rows, own_len, 3 * WIDE), shape(rows, 2 * win, 2 * WIDE)] * groups + [shape(rows, win, width)] * 2,
        queries,
        keys,
        values,
        halo_keys,
        halo_values,
        mid_grad_attended,
        out_grad_attended,
        mid_probs,
        out_probs,
        angles,
        weight,
        flops=12e9,
        after=[chip_one[0]],
    )
    inner_grad, other_grad = to_neighbours(inner_grad, other_grad)
    (total_in,) = call(
        "weight_in",
        weight_in_kernel,
        [shape(*attention_in.shape)],
        normed,
        halo_normed,
        *grads,
        flops=4e9,
    )
    plane_one = add_up([chip_one[0], *from_plane], cut(chip_one[0], 4), after=[total_in])
    keep_two, send_two = call(
        "split",
        split_kernel,
        [shape(BLOCKS // 2, attention_in.shape[1] // BLOCKS, width)] * 2,
        total_in,
        flops=1e9,
        after=[plane_one[0]],
    )
    chip_two = add_up([keep_two, swap(send_two, core=1)], cut(keep_two, 4))
    from_plane_rs = swap_plane(chip_two)
    own_grad, done_own = call(
        "grad_own",
        grad_own_kernel,
        [shape(rows, own_len, width, kind=F32)],
        weight,
        *grads[::2],
        flops=2e9,
        after=[chip_two[0]],
        token=True,
    )
    (line_one0,) = add_up([plane_one[0], *swap_line(plane_one)], cut(plane_one[0], 1), after=[])
    line_one0 = swap_rest(line_one0)
    plane_two = add_up([chip_two[0], *from_plane_rs], cut(chip_two[0], 2), after=[inner_grad])
    line_one6 = join([line_one0, swap(line_one0, z=2)], after=[done_own])
    near_two = add_up([plane_two[0], swap(plane_two[1], z=1)], cut(plane_two[0], 2), after=[line_one6])
    line_one7 = join([line_one6, swap(line_one6, z=1)], after=[near_two[0]])
    from_plane = swap_plane([line_one7] * 4)
    (line_two0,) = add_up([near_two[0], swap(near_two[1], z=2)], cut(near_two[0], 1), after=[line_one6])
    line_two0 = swap_rest(line_two0)
    line_two8 = join([line_two0, swap(line_two0, z=2)], after=[])
    line_two9 = join([line_two8, swap(line_two8, z=1)], after=[other_grad])
    from_plane_two = swap_plane([line_two9] * 4)
    line_two = line_two9
    whole_one = join([line_one7, *from_plane], after=[line_two9])
    grad_tokens, done_finish = call(
        "finish",
        finish_kernel,
        [shape(rows, own_len, width, kind=F32)],
        tokens,
        own_grad,
        inner_grad,
        other_grad,
        mid_grad,
        out_grad,
        gain_one,
        flops=1e8,
        after=[whole_one],
        token=True,
    )

    def placed(parts, gain, *weights):
        outs = [shape(*w.shape, kind=F32) for w in weights] + [shape(1, width, kind=F32)]
        return call("place", place_kernel, outs, *parts, weights[0], gain, flops=1e6, token=True)

    grad_up, grad_out, grad_down, grad_gain_two, done_one = placed(
        (whole_one, swap(whole_one, core=1)), gain_two, feedforward_in, attention_out, feedforward_out
    )
    whole_two = join([line_two, *from_plane_two], after=[done_one, done_finish])
    grad_in, grad_gain_one, _ = placed((whole_two, swap(whole_two, core=1)), gain_one, attention_in)
    return activations, grad_tokens, grad_in, grad_out, grad_up, grad_down, grad_gain_one[0], grad_gain_two[0]


def solution(mesh):
    token, rest = P("dp", "seq", None), P()
    return jax.shard_map(
        shards,
        mesh=mesh,
        in_specs=(token, P("dp", None)) + (rest,) * 6 + (token,),
        out_specs=(token, token) + (rest,) * 6,
        check_vma=False,
    )
```

```python
import functools

import jax
import jax.numpy as jnp
import numpy as np
from jax import lax
from jax.experimental import pallas as pl
from jax.experimental.pallas import tpu as pltpu
from jax.sharding import PartitionSpec as P

HEADS = 8
HEAD_DIM = 64
HALF = HEAD_DIM // 2
HALF_WIN = 64
EPSILON = 1e-05
ROTARY_BASE = 10000.0
SCALE = HEAD_DIM**-0.5
BLOCKS = 32
GROUP = 4
WIDE = GROUP * HEAD_DIM
LANES = 128
MB = 1024 * 1024

F32 = jnp.float32
BF16 = jnp.bfloat16


def dot(a, b, contract):
    return lax.dot_general(a, b, ((contract[:1], contract[1:]), ((), ())), preferred_element_type=F32)


def nn(a, b):
    return dot(a, b, (1, 0))


def nt(a, b):
    return dot(a, b, (1, 1))


def tn(a, b):
    return dot(a, b, (0, 0))


def iota(shape, dim):
    return lax.broadcasted_iota(jnp.int32, shape, dim)


def flat(values):
    return values.reshape(-1, values.shape[-1])


def normalize(values):
    shifted = values - jnp.mean(values, axis=-1, keepdims=True)
    inverse = lax.rsqrt(jnp.mean(shifted * shifted, axis=-1, keepdims=True) + EPSILON)
    return shifted * inverse, inverse


def norm_back(scaled_grad, unit, inverse):
    return (
        scaled_grad
        - jnp.mean(scaled_grad, axis=-1, keepdims=True)
        - unit * jnp.mean(scaled_grad * unit, axis=-1, keepdims=True)
    ) * inverse


def halves_first():
    old, new = iota((WIDE, WIDE), 0), iota((WIDE, WIDE), 1)
    moved = (old % HEAD_DIM) // HALF * LANES + old // HEAD_DIM * HALF + old % HALF
    return (moved == new).astype(BF16)


def head_of(shape, halved):
    lane = iota(shape, 1)
    return lane % LANES // HALF if halved else lane // HEAD_DIM


def by_head(values, halved):
    head = head_of(values.shape, halved)
    zero = jnp.zeros_like(values)
    return jnp.concatenate([jnp.where(head == h, values, zero) for h in range(GROUP)], axis=0)


def pick_heads(stacked, halved):
    count = stacked.shape[0] // GROUP
    head = head_of((count, stacked.shape[1]), halved)
    out = stacked[:count]
    for h in range(1, GROUP):
        out = jnp.where(head == h, stacked[h * count : (h + 1) * count], out)
    return out


def turn(values, cosine, sines):
    first, second = values[:, :LANES], values[:, LANES:]
    return jnp.concatenate([first * cosine - second * sines, second * cosine + first * sines], axis=1)


def turn_back(values, cosine, sines):
    first, second = values[:, :LANES], values[:, LANES:]
    return jnp.concatenate([first * cosine + second * sines, second * cosine - first * sines], axis=1)


def load_kernel(tokens_ref, *refs):
    count = len(refs) // 2 - 1
    sources, (inner_ref, other_ref, *outs), sems = refs[:count], refs[count:-1], refs[-1]
    own_len, win = tokens_ref.shape[1], HALF_WIN
    odd = lax.axis_index("seq") % 2
    copies = []
    for k, (out, high) in enumerate(((inner_ref, odd == 0), (other_ref, odd == 1))):
        at = pl.multiple_of(jnp.where(high, own_len - win, 0), win)
        copies.append(pltpu.make_async_copy(tokens_ref.at[:, pl.ds(at, win)], out, sems.at[k]))
    for k, (source, out) in enumerate(zip(sources, outs, strict=True)):
        copies.append(pltpu.make_async_copy(source, out, sems.at[k + 2]))
    for copy in copies:
        copy.start()
    for copy in copies:
        copy.wait()


def by_side(inner, other):
    odd = lax.axis_index("seq") % 2 == 1
    return jnp.where(odd, inner, other), jnp.where(odd, other, inner)


def project_kernel(
    tokens_ref,
    starts_ref,
    in_ref,
    gain_ref,
    base_ref,
    table_ref,
    normed_ref,
    queries_ref,
    keys_ref,
    values_ref,
    weight_ref,
    angles_ref,
    bounds_ref,
):
    rows, own_len, width = tokens_ref.shape
    win = HALF_WIN
    place = lax.axis_index("seq")
    start = place * own_len
    row_len = own_len * lax.axis_size("seq")

    base_cos, base_sin = base_ref[place, 0:1], base_ref[place, 1:2]
    angles_ref[0] = base_cos * table_ref[0] - base_sin * table_ref[1]
    angles_ref[1] = base_sin * table_ref[0] + base_cos * table_ref[1]

    lane = iota((rows, own_len - 2 * win + 4 * win), 1)
    mid = own_len - 2 * win
    pos = start + jnp.where(
        lane < mid, lane + win, jnp.where(lane < mid + 2 * win, lane % win, own_len - win + lane % win)
    )
    first, last = jnp.maximum(pos - win, 0), jnp.minimum(pos + win, row_len - 1)
    for j in range(starts_ref.shape[1]):
        cut = starts_ref[:, j : j + 1]
        first = jnp.maximum(first, jnp.where(cut <= pos, cut, 0))
        last = jnp.minimum(last, jnp.where(cut > pos, cut - 1, row_len))
    for r in range(rows):
        bounds_ref[r, 0:1] = first[r : r + 1]
        bounds_ref[r, 1:2] = last[r : r + 1]

    order = halves_first()
    for c in range(0, 2 * width, WIDE):
        weight_ref[:, c : c + WIDE] = nn(in_ref[:, c : c + WIDE], order).astype(BF16)
    weight_ref[:, 2 * width :] = in_ref[:, 2 * width :]

    pair = 6
    cosine, sines = angles_ref[0, win : win + own_len], angles_ref[1, win : win + own_len]
    cosine, sines = jnp.concatenate([cosine] * pair), jnp.concatenate([sines] * pair)

    @pl.loop(0, rows // pair)
    def _(i):
        at = pl.ds(i * pair, pair)
        unit, _ = normalize(flat(tokens_ref[at]).astype(F32))
        normed = (unit * gain_ref[...]).astype(BF16)
        normed_ref[at] = normed.reshape(pair, own_len, width)
        queries, keys = nn(normed, weight_ref[:, :width]), nn(normed, weight_ref[:, width : 2 * width])
        for c in range(0, width, WIDE):
            part = turn(queries[:, c : c + WIDE], cosine * SCALE, sines * SCALE)
            queries_ref[at, :, c : c + WIDE] = part.astype(BF16).reshape(pair, own_len, WIDE)
            part = turn(keys[:, c : c + WIDE], cosine, sines)
            keys_ref[at, :, c : c + WIDE] = part.astype(BF16).reshape(pair, own_len, WIDE)
        values_ref[at] = nn(normed, weight_ref[:, 2 * width :]).astype(BF16).reshape(pair, own_len, width)


def halo_kernel(inner_ref, other_ref, weight_ref, gain_ref, angles_ref, normed_ref, keys_ref, values_ref):
    rows, win, width = inner_ref.shape
    pair = 6
    span = angles_ref.shape[1]
    cosine = jnp.concatenate([angles_ref[0, :win], angles_ref[0, span - win :]] * pair)
    sines = jnp.concatenate([angles_ref[1, :win], angles_ref[1, span - win :]] * pair)

    @pl.loop(0, rows // pair)
    def _(i):
        at = pl.ds(i * pair, pair)
        sides = by_side(inner_ref[at], other_ref[at])
        unit, _ = normalize(flat(jnp.concatenate(sides, axis=1)).astype(F32))
        normed = (unit * gain_ref[...]).astype(BF16)
        normed_ref[at] = normed.reshape(pair, 2 * win, width)
        keys = nn(normed, weight_ref[:, width : 2 * width])
        for c in range(0, width, WIDE):
            part = turn(keys[:, c : c + WIDE], cosine, sines)
            keys_ref[at, :, c : c + WIDE] = part.astype(BF16).reshape(pair, 2 * win, WIDE)
        values_ref[at] = nn(normed, weight_ref[:, 2 * width :]).astype(BF16).reshape(pair, 2 * win, width)


def bias_of(bounds_ref, row, lanes, first_key, keys):
    key = first_key + iota((keys, LANES), 0)
    first, last = bounds_ref[row, 0:1, lanes], bounds_ref[row, 1:2, lanes]
    return jnp.where((key >= first) & (key <= last), 0.0, -jnp.inf)


def probabilities(scores, bias):
    parts = []
    for c in range(0, scores.shape[1], LANES):
        part = scores[:, c : c + LANES] + bias
        part = jnp.exp(part - jnp.max(part, axis=0, keepdims=True))
        parts.append(part * (1.0 / jnp.sum(part, axis=0, keepdims=True)))
    return jnp.concatenate(parts, axis=1)


def attend_mid_kernel(queries_ref, keys_ref, values_ref, bounds_ref, attended_ref, probs_ref):
    rows, own_len, width = queries_ref.shape
    win = HALF_WIN
    mid = own_len - 2 * win
    start = lax.axis_index("seq") * own_len
    pair = 6

    @pl.loop(0, rows // pair)
    def _(i):
        for r in range(pair):
            row = i * pair + r
            bias = bias_of(bounds_ref, row, slice(0, mid), start, own_len)
            for g in range(width // WIDE):
                cols = slice(g * WIDE, (g + 1) * WIDE)
                probs = probabilities(
                    nt(keys_ref[row, :, cols], by_head(queries_ref[row, win : win + mid, cols], True)), bias
                )
                probs_ref[row, g] = probs
                out = tn(probs.astype(BF16), values_ref[row, :, cols])
                attended_ref[row, :, cols] = pick_heads(out, False).astype(BF16)


def wide_side(own, halo, side):
    win = HALF_WIN
    if side == 0:
        return jnp.concatenate([halo[:win], own[: 2 * win]], axis=0)
    return jnp.concatenate([own[own.shape[0] - 2 * win :], halo[win:]], axis=0)


def attend_out_kernel(
    queries_ref, keys_ref, values_ref, halo_keys_ref, halo_values_ref, bounds_ref, attended_ref, probs_ref
):
    rows, own_len, width = queries_ref.shape
    win = HALF_WIN
    mid = own_len - 2 * win
    start = lax.axis_index("seq") * own_len
    pair = 6

    @pl.loop(0, rows // pair)
    def _(i):
        for r in range(pair):
            row = i * pair + r
            for side in range(2):
                own = slice(0, win) if side == 0 else slice(own_len - win, own_len)
                lanes = slice(mid + side * LANES, mid + (side + 1) * LANES)
                bias = bias_of(bounds_ref, row, lanes, start + own.start - win, 3 * win)
                for g in range(width // WIDE):
                    cols = slice(g * WIDE, (g + 1) * WIDE)
                    keys = wide_side(keys_ref[row, :, cols], halo_keys_ref[row, :, cols], side)
                    values = wide_side(values_ref[row, :, cols], halo_values_ref[row, :, cols], side)
                    probs = probabilities(nt(keys, by_head(queries_ref[row, own, cols], True)), bias)
                    probs_ref[row, side, g] = probs
                    out = tn(probs.astype(BF16), values)
                    attended_ref[row, side * win : (side + 1) * win, cols] = pick_heads(out, False).astype(BF16)


def gelu_parts(gate):
    bell = jnp.exp(-0.5 * gate * gate)
    t = 1.0 / (1.0 + (0.3275911 * 0.7071067811865476) * jnp.abs(gate))
    tail = t * (
        0.5 * 0.254829592
        + t * (0.5 * -0.284496736 + t * (0.5 * 1.421413741 + t * (0.5 * -1.453152027 + t * (0.5 * 1.061405429))))
    )
    tail = tail * bell
    return jnp.where(gate < 0, tail, 1.0 - tail), gate * bell * 0.3989422804014327


def part_of(ref, at, outer):
    own_len, win = ref.shape[1], HALF_WIN
    if outer:
        return flat(jnp.concatenate([ref[at, :win], ref[at, own_len - win :]], axis=1))
    return flat(ref[at, win : own_len - win])


def dense_kernel(
    outer,
    tokens_ref,
    top_ref,
    attended_ref,
    out_ref,
    up_ref,
    down_ref,
    gain_ref,
    middle_ref,
    normed_ref,
    mixed_ref,
    grad_up_ref,
    grad_middle_ref,
    branch_ref,
    grad_attended_ref,
):
    rows, count, width = attended_ref.shape
    hidden = down_ref.shape[0]
    pair = 3

    @pl.loop(0, rows // pair)
    def _(i):
        at = pl.ds(i * pair, pair)

        def put(ref, values, cols=slice(None)):
            ref[at, :, cols] = values.reshape(pair, count, -1)

        top = part_of(top_ref, at, outer)
        middle = part_of(tokens_ref, at, outer).astype(F32) + nn(flat(attended_ref[at]), out_ref[...])
        put(middle_ref, middle)
        unit, inverse = normalize(middle)
        normed = (unit * gain_ref[...]).astype(BF16)
        put(normed_ref, normed)
        grad_hidden = [nt(top, down_ref[:512]), nt(top, down_ref[512:])]
        for c in range(0, hidden, 256):
            halves = [up_ref[:, c : c + 256], up_ref[:, hidden + c : hidden + c + 256]]
            both = nn(normed, jnp.concatenate(halves, axis=1))
            gate, lift = both[:, :256], both[:, 256:]
            grad_mixed = grad_hidden[c // 512][:, c % 512 : c % 512 + 256]
            phi, slope = gelu_parts(gate)
            active = gate * phi
            put(mixed_ref, (active * lift).astype(BF16), slice(c, c + 256))
            put(grad_up_ref, (grad_mixed * lift * (phi + slope)).astype(BF16), slice(c, c + 256))
            put(grad_up_ref, (grad_mixed * active).astype(BF16), slice(hidden + c, hidden + c + 256))
        grad_normed = nt(flat(grad_up_ref[at]), up_ref[...])
        grad_middle = top.astype(F32) + norm_back(grad_normed * gain_ref[...], unit, inverse)
        put(grad_middle_ref, grad_middle)
        branch = grad_middle.astype(BF16)
        put(branch_ref, branch)
        put(grad_attended_ref, nt(branch, out_ref[...]).astype(BF16))


def store_blocks(keep_ref, send_ref, store):
    seq, dp = lax.axis_index("seq"), lax.axis_index("dp")
    place = (dp % 2) * 16 + (dp // 2) * 8 + (seq % 2) * 4 + (seq // 2) % 2 * 2 + (seq // 4) % 2
    for ref, base in ((keep_ref, 0), (send_ref, BLOCKS // 2)):

        @pl.loop(0, BLOCKS // 2)
        def _(i):
            store(ref, i, place ^ (i + base))


def weights_kernel(
    outer,
    top_ref,
    normed_ref,
    grad_up_ref,
    mixed_ref,
    attended_ref,
    branch_ref,
    *refs,
):
    begun, (*sums,) = (refs[:3], refs[3:]) if outer else ((None,) * 3, refs)
    if outer:
        keep_ref, send_ref, *sums = sums
    up_sum, down_sum, out_sum = sums
    width = top_ref.shape[2]

    def add(part, ref, at):
        return part if ref is None else part + ref[at].astype(F32)

    normed = flat(normed_ref[...])
    for c in range(0, up_sum.shape[1], 512):
        at = (slice(None), slice(c, c + 512))
        up_sum[at] = add(tn(normed, flat(grad_up_ref[:, :, c : c + 512])), begun[0], at).astype(BF16)
    top = part_of(top_ref, slice(0, top_ref.shape[0]), outer)
    for c in range(0, down_sum.shape[0], 256):
        at = (slice(c, c + 256), slice(None))
        down_sum[at] = add(tn(flat(mixed_ref[:, :, c : c + 256]), top), begun[1], at).astype(down_sum.dtype)
    at = (slice(None), slice(None))
    out_sum[at] = add(tn(flat(attended_ref[...]), flat(branch_ref[...])), begun[2], at).astype(BF16)
    if not outer:
        return
    rows, down_rows = width // BLOCKS, down_sum.shape[0] // BLOCKS

    def store(ref, i, block):
        own = pl.ds(pl.multiple_of(block * rows, rows), rows)
        at = 0
        for c in range(0, up_sum.shape[1], width):
            ref[i, at : at + rows] = up_sum[own, c : c + width]
            at += rows
        ref[i, at : at + rows] = out_sum[own, :]
        at += rows
        ref[i, at:] = down_sum[pl.ds(pl.multiple_of(block * down_rows, down_rows), down_rows), :].astype(BF16)

    store_blocks(keep_ref, send_ref, store)


def attend_back_kernel(
    group,
    queries_ref,
    keys_ref,
    values_ref,
    halo_keys_ref,
    halo_values_ref,
    mid_grad_ref,
    out_grad_ref,
    mid_probs_ref,
    out_probs_ref,
    angles_ref,
    own_ref,
    halo_ref,
):
    rows, own_len, _ = queries_ref.shape
    win = HALF_WIN
    mid = own_len - 2 * win
    cols = slice(group * WIDE, (group + 1) * WIDE)
    cosine, sines = angles_ref[0], angles_ref[1]
    own_cos, own_sin = cosine[win : win + own_len], sines[win : win + own_len]
    halo_cos = jnp.concatenate([cosine[:win], cosine[win + own_len :]])
    halo_sin = jnp.concatenate([sines[:win], sines[win + own_len :]])
    pair = 2

    def unit(queries, keys, values, grads, probs):
        q4, g4 = by_head(queries, True), by_head(grads, False)
        grad_probs = nt(values, g4)
        lows, grad_scores = [], []
        for c in range(0, probs.shape[1], LANES):
            part, grad_part = probs[:, c : c + LANES], grad_probs[:, c : c + LANES]
            inner = jnp.sum(part * grad_part, axis=0, keepdims=True)
            lows.append(part.astype(BF16))
            grad_scores.append((part * (grad_part - inner)).astype(BF16))
        grad_scores = jnp.concatenate(grad_scores, axis=1)
        return (
            pick_heads(tn(grad_scores, keys), True),
            nn(grad_scores, q4),
            nn(jnp.concatenate(lows, axis=1), g4),
        )

    @pl.loop(0, rows // pair)
    def _(i):
        for r in range(pair):
            row = i * pair + r
            queries, keys, values = queries_ref[row, :, cols], keys_ref[row, :, cols], values_ref[row, :, cols]
            halo_keys, halo_values = halo_keys_ref[row, :, cols], halo_values_ref[row, :, cols]
            grads = out_grad_ref[row, :, cols]
            middle = unit(queries[win : win + mid], keys, values, mid_grad_ref[row, :, cols], mid_probs_ref[row, group])
            sides = [
                unit(
                    queries[:win] if side == 0 else queries[own_len - win :],
                    wide_side(keys, halo_keys, side),
                    wide_side(values, halo_values, side),
                    grads[side * win : (side + 1) * win],
                    out_probs_ref[row, side, group],
                )
                for side in range(2)
            ]
            low, high = sides
            own = [jnp.concatenate([low[0], middle[0], high[0]], axis=0) * SCALE]
            halo = []
            for k in (1, 2):
                own.append(middle[k] + jnp.concatenate([low[k][win:], high[k][: 2 * win]], axis=0))
                halo.append(jnp.concatenate([low[k][:win], high[k][2 * win :]], axis=0))
            own_ref[row, :, :WIDE] = turn_back(own[0], own_cos, own_sin).astype(BF16)
            own_ref[row, :, WIDE : 2 * WIDE] = turn_back(own[1], own_cos, own_sin).astype(BF16)
            own_ref[row, :, 2 * WIDE :] = own[2].astype(BF16)
            halo_ref[row, :, :WIDE] = turn_back(halo[0], halo_cos, halo_sin).astype(BF16)
            halo_ref[row, :, WIDE:] = halo[1].astype(BF16)


def weight_in_kernel(normed_ref, halo_normed_ref, *refs):
    *grads, total = refs
    width = normed_ref.shape[2]
    normed, halo_normed = flat(normed_ref[...]), flat(halo_normed_ref[...])
    order = halves_first()
    for k in range(3):
        part = tn(normed, jnp.concatenate([flat(own[:, :, k * WIDE : (k + 1) * WIDE]) for own in grads[::2]], axis=1))
        if k > 0:
            halo = [flat(halo[:, :, (k - 1) * WIDE : k * WIDE]) for halo in grads[1::2]]
            part = part + tn(halo_normed, jnp.concatenate(halo, axis=1))
        part = part.astype(BF16)
        if k < 2:
            part = [nt(part[:, c : c + WIDE], order).astype(BF16) for c in range(0, width, WIDE)]
            part = jnp.concatenate(part, axis=1)
        total[:, k * width : (k + 1) * width] = part


def split_kernel(total_ref, keep_ref, send_ref):
    rows, width = total_ref.shape[0] // BLOCKS, total_ref.shape[0]

    def store(ref, i, block):
        own = pl.ds(pl.multiple_of(block * rows, rows), rows)
        for k in range(3):
            ref[i, k * rows : (k + 1) * rows] = total_ref[own, k * width : (k + 1) * width]

    store_blocks(keep_ref, send_ref, store)


def grad_halo_kernel(weight_ref, *refs):
    *grads, inner_ref, other_ref = refs
    rows, win, width = inner_ref.shape
    total = None
    for g, ref in enumerate(grads):
        weight = jnp.concatenate(
            [weight_ref[:, k * width + g * WIDE : k * width + (g + 1) * WIDE] for k in (1, 2)], axis=1
        )
        part = nt(flat(ref[...]), weight)
        total = part if total is None else total + part
    total = total.astype(BF16).reshape(rows, 2 * win, width)
    inner_ref[...], other_ref[...] = by_side(total[:, :win], total[:, win:])


def backward_kernel(*refs):
    shared, (weight_ref, *grads, inner_ref, other_ref) = refs[:10], refs[10:]
    for group in range(len(grads) // 2):
        attend_back_kernel(group, *shared, *grads[2 * group : 2 * group + 2])
    grad_halo_kernel(weight_ref, *grads[1::2], inner_ref, other_ref)


def grad_own_kernel(weight_ref, *refs):
    *grads, out_ref = refs
    rows, own_len, width = out_ref.shape
    pair = 2
    groups = len(grads)

    @pl.loop(0, rows // pair)
    def _(i):
        at = pl.ds(i * pair, pair)
        grad = jnp.concatenate([flat(ref[at]) for ref in grads], axis=1)
        weight = jnp.concatenate(
            [
                weight_ref[:, k * width + g * WIDE : k * width + (g + 1) * WIDE]
                for g in range(groups)
                for k in range(3)
            ],
            axis=1,
        )
        out_ref[at] = nt(grad, weight).reshape(pair, own_len, width)


def result_kernel(mid_middle_ref, out_middle_ref, mid_mixed_ref, out_mixed_ref, down_ref, result_ref):
    own_len, win = result_ref.shape[1], HALF_WIN
    pair = 3

    @pl.loop(0, result_ref.shape[0] // pair)
    def _(i):
        at = pl.ds(i * pair, pair)

        def result(middle_ref, mixed_ref):
            total = flat(middle_ref[at]) + nn(flat(mixed_ref[at]), down_ref[...])
            return total.astype(BF16).reshape(middle_ref[at].shape)

        result_ref[at, win : own_len - win] = result(mid_middle_ref, mid_mixed_ref)
        outer = result(out_middle_ref, out_mixed_ref)
        result_ref[at, :win] = outer[:, :win]
        result_ref[at, own_len - win :] = outer[:, win:]


def finish_kernel(
    tokens_ref, own_ref, inner_ref, other_ref, mid_grad_ref, out_grad_ref, gain_ref, grad_ref
):
    own_len, win = tokens_ref.shape[1], HALF_WIN

    @pl.loop(0, tokens_ref.shape[0])
    def _(row):
        unit, inverse = normalize(tokens_ref[row].astype(F32))
        own = own_ref[row]
        low, high = by_side(inner_ref[row].astype(F32), other_ref[row].astype(F32))
        grads = jnp.concatenate(
            [own[:win] + low, own[win : own_len - win], own[own_len - win :] + high],
            axis=0,
        )
        outer = out_grad_ref[row]
        middle = jnp.concatenate([outer[:win], mid_grad_ref[row], outer[win:]], axis=0)
        grad_ref[row] = middle + norm_back(grads * gain_ref[...], unit, inverse)


def place_kernel(own_ref, other_ref, weight_ref, gain_ref, *out_refs):
    *out_refs, gain_grad_ref = out_refs

    def store(ref, i, block):
        at = 0
        for out in out_refs:
            rows = out.shape[0] // BLOCKS
            for c in range(0, out.shape[1], ref.shape[2]):
                out[pl.ds(pl.multiple_of(block * rows, rows), rows), c : c + ref.shape[2]] = ref[
                    i, at : at + rows
                ].astype(F32)
                at += rows

    store_blocks(own_ref, other_ref, store)
    total = None
    for c in range(0, weight_ref.shape[1], LANES):
        part = out_refs[0][:, c : c + LANES] * weight_ref[:, c : c + LANES].astype(F32)
        total = part if total is None else total + part
    gain_grad_ref[...] = jnp.sum(total.T, axis=0, keepdims=True) / gain_ref[...]


def add_kernel(count, *refs):
    parts, outs = refs[:count], refs[count:]
    size = parts[0].shape[0] // len(outs)
    for k, out in enumerate(outs):
        at = slice(k * size, (k + 1) * size)
        out[...] = sum(p[at].astype(F32) for p in parts).astype(BF16)


def join_kernel(*refs):
    *parts, out = refs
    size = parts[0].shape[0]
    for k, part in enumerate(parts):
        out[k * size : (k + 1) * size] = part[...]


def to_neighbours(inner, other):
    size = lax.axis_size("seq")
    pairs = [(i, i ^ 1) for i in range(size)]
    between = [p for i in range(1, size - 1, 2) for p in ((i, i + 1), (i + 1, i))]
    return lax.ppermute(inner, "seq", pairs), lax.ppermute(other, "seq", between)


def swap_route(core, x, y, z, rest):
    dp, seq = lax.axis_size("dp"), lax.axis_size("seq")

    def partner(i):
        d, s = divmod(i, seq)
        return (d ^ (core + 2 * x)) * seq + (s ^ (y + 2 * z + 8 * rest))

    return [(i, partner(i)) for i in range(dp * seq)]


def swap(values, core=0, x=0, y=0, z=0, rest=0):
    return lax.ppermute(values, ("dp", "seq"), swap_route(core, x, y, z, rest))


def shape(*dims, kind=BF16):
    return jax.ShapeDtypeStruct(dims, kind)


def call(name, kernel, outs, *args, after=(), token=False, grant=6, flops=1e9, scratch=()):
    outs = [*outs, shape(8, LANES, kind=F32)] if token else outs
    spec = pl.BlockSpec(memory_space=pltpu.VMEM)
    moved = sum(int(np.prod(a.shape)) * a.dtype.itemsize for a in (*args, *outs))

    def body(*refs):
        refs = refs[len(after) :]
        if token:
            at = len(args) + len(outs) - 1
            refs[at][...] = jnp.zeros_like(refs[at])
            refs = refs[:at] + refs[at + 1 :]
        return kernel(*refs)

    return pl.pallas_call(
        body,
        out_shape=outs,
        in_specs=[pl.BlockSpec(memory_space=pl.ANY)] * len(after) + [spec] * len(args),
        out_specs=[spec] * len(outs),
        scratch_shapes=scratch,
        compiler_params=pltpu.CompilerParams(vmem_limit_bytes=grant * MB),
        cost_estimate=pl.CostEstimate(flops=int(flops) // 100, bytes_accessed=moved // 100, transcendentals=0),
        name=name,
    )(*after, *args)


def add_up(parts, outs, after=()):
    return call("add", functools.partial(add_kernel, len(parts)), outs, *parts, after=after, grant=4, flops=1e6)


def join(parts, after=()):
    size = parts[0].shape
    out = shape(len(parts) * size[0], *size[1:])
    return call("join", join_kernel, [out], *parts, after=after, grant=4, flops=1e6)[0]


def swap_plane(parts):
    return [swap(parts[k], x=k >> 1, y=k & 1) for k in (1, 2, 3)]


def swap_line(parts):
    return [swap(parts[k], z=(k >> 1) + 2 * (k & 1)) for k in (1, 2, 3)]


def swap_rest(own):
    rest = 1
    while 8 * rest < lax.axis_size("seq"):
        (own,) = add_up([own, swap(own, rest=rest)], [shape(*own.shape)])
        rest *= 2
    return own


def angle_tables(own_len, pieces):
    inverse = ROTARY_BASE ** (-(np.arange(0, HEAD_DIM, 2) / HEAD_DIM))
    inverse = np.tile(inverse, LANES // HALF)
    base = np.arange(pieces)[:, None] * own_len * inverse
    local = (np.arange(own_len + 2 * HALF_WIN) - HALF_WIN)[:, None] * inverse
    return [jnp.asarray(np.stack([np.cos(a), np.sin(a)], axis=d), F32) for a, d in ((base, 1), (local, 0))]


def shards(
    tokens,
    document_starts,
    attention_in,
    attention_out,
    feedforward_in,
    feedforward_out,
    gain_first,
    gain_second,
    result_grad,
):
    rows, own_len, width = tokens.shape
    hidden = feedforward_out.shape[0]
    win = HALF_WIN
    mid = own_len - 2 * win
    seq = lax.axis_size("seq")
    groups = width // WIDE
    gain_one, gain_two = gain_first[None], gain_second[None]

    small = [document_starts, gain_one, attention_in, *angle_tables(own_len, seq)]
    outs = [pltpu.VMEM((rows, win, width), BF16)] * 2 + [pltpu.VMEM(a.shape, a.dtype) for a in small]
    inner_tokens, other_tokens, document_starts, gain_one, attention_in, *tables = pl.pallas_call(
        load_kernel,
        out_shape=outs,
        in_specs=[pl.BlockSpec(memory_space=pltpu.HBM)] * (1 + len(small)),
        out_specs=[pl.BlockSpec(memory_space=pltpu.VMEM)] * len(outs),
        scratch_shapes=[pltpu.SemaphoreType.DMA((len(outs),))],
        compiler_params=pltpu.CompilerParams(vmem_limit_bytes=MB),
        name="load",
    )(*[pltpu.with_memory_space_constraint(a, pltpu.HBM) for a in (tokens, *small)])
    inner_halo, other_halo = to_neighbours(inner_tokens, other_tokens)

    row_shape = shape(rows, own_len, width)
    normed, queries, keys, values, weight, angles, bounds = call(
        "project",
        project_kernel,
        [row_shape] * 4
        + [
            shape(*attention_in.shape),
            shape(2, own_len + 2 * win, LANES, kind=F32),
            shape(rows, 2, mid + 4 * win, kind=jnp.int32),
        ],
        tokens,
        document_starts,
        attention_in,
        gain_one,
        *tables,
        flops=3e9,
    )
    mid_attended, mid_probs = call(
        "attend_mid",
        attend_mid_kernel,
        [shape(rows, mid, width), shape(rows, groups, own_len, GROUP * mid, kind=F32)],
        queries,
        keys,
        values,
        bounds,
        flops=2e9,
    )

    def dense(name, outer, attended):
        count = attended.shape[1]
        return call(
            name,
            functools.partial(dense_kernel, outer),
            [
                shape(rows, count, width, kind=F32),
                shape(rows, count, width),
                shape(rows, count, hidden),
                shape(rows, count, 2 * hidden),
                shape(rows, count, width, kind=F32),
                shape(rows, count, width),
                shape(rows, count, width),
            ],
            tokens,
            result_grad,
            attended,
            attention_out,
            feedforward_in,
            feedforward_out,
            gain_two,
            flops=5e9,
            grant=14,
        )

    mid_middle, mid_normed, mid_mixed, mid_grad_up, mid_grad, mid_branch, mid_grad_attended = dense(
        "dense_mid", False, mid_attended
    )

    begun = call(
        "begin",
        functools.partial(weights_kernel, False),
        [shape(*w.shape) for w in (feedforward_in, feedforward_out, attention_out)],
        result_grad,
        mid_normed,
        mid_grad_up,
        mid_mixed,
        mid_attended,
        mid_branch,
        flops=3e9,
    )

    halo_normed, halo_keys, halo_values = call(
        "halo",
        halo_kernel,
        [shape(rows, 2 * win, width)] * 3,
        inner_halo,
        other_halo,
        weight,
        gain_one,
        angles,
        flops=1e9,
        after=[begun[2]],
    )
    out_attended, out_probs = call(
        "attend_out",
        attend_out_kernel,
        [shape(rows, 2 * win, width), shape(rows, 2, groups, 3 * win, GROUP * win, kind=F32)],
        queries,
        keys,
        values,
        halo_keys,
        halo_values,
        bounds,
        flops=2e9,
    )
    out_middle, out_normed, out_mixed, out_grad_up, out_grad, out_branch, out_grad_attended = dense(
        "dense_out", True, out_attended
    )

    piece = (feedforward_in.shape[1] // width * width + width + hidden) // BLOCKS
    keep_one, send_one = call(
        "weights",
        functools.partial(weights_kernel, True),
        [shape(BLOCKS // 2, piece, width)] * 2,
        result_grad,
        out_normed,
        out_grad_up,
        out_mixed,
        out_attended,
        out_branch,
        *begun,
        flops=5e9,
        scratch=[
            pltpu.VMEM(feedforward_in.shape, BF16),
            pltpu.VMEM(feedforward_out.shape, F32),
            pltpu.VMEM(attention_out.shape, BF16),
        ],
    )

    def cut(blocks, parts):
        return [shape(blocks.shape[0] // parts, *blocks.shape[1:])] * parts

    activations, done_result = call(
        "result",
        result_kernel,
        [row_shape],
        mid_middle,
        out_middle,
        mid_mixed,
        out_mixed,
        feedforward_out,
        flops=2e9,
        after=[keep_one],
        token=True,
    )
    chip_one = add_up([keep_one, swap(send_one, core=1)], cut(keep_one, 4), after=[done_result])
    from_plane = swap_plane(chip_one)
    grad_shapes = [shape(rows, own_len, 3 * WIDE), shape(rows, 2 * win, 2 * WIDE)] * groups
    *grads, inner_grad, other_grad = call(
        "backward",
        backward_kernel,
        [shape(rows, own_len, 3 * WIDE), shape(rows, 2 * win, 2 * WIDE)] * groups + [shape(rows, win, width)] * 2,
        queries,
        keys,
        values,
        halo_keys,
        halo_values,
        mid_grad_attended,
        out_grad_attended,
        mid_probs,
        out_probs,
        angles,
        weight,
        flops=12e9,
        after=[chip_one[0]],
    )
    inner_grad, other_grad = to_neighbours(inner_grad, other_grad)
    (total_in,) = call(
        "weight_in",
        weight_in_kernel,
        [shape(*attention_in.shape)],
        normed,
        halo_normed,
        *grads,
        flops=4e9,
    )
    plane_one = add_up([chip_one[0], *from_plane], cut(chip_one[0], 4), after=[total_in])
    keep_two, send_two = call(
        "split",
        split_kernel,
        [shape(BLOCKS // 2, attention_in.shape[1] // BLOCKS, width)] * 2,
        total_in,
        flops=1e9,
        after=[plane_one[0]],
    )
    chip_two = add_up([keep_two, swap(send_two, core=1)], cut(keep_two, 4))
    from_plane_rs = swap_plane(chip_two)
    own_grad, done_own = call(
        "grad_own",
        grad_own_kernel,
        [shape(rows, own_len, width, kind=F32)],
        weight,
        *grads[::2],
        flops=2e9,
        after=[chip_two[0]],
        token=True,
    )
    (line_one0,) = add_up([plane_one[0], *swap_line(plane_one)], cut(plane_one[0], 1), after=[])
    line_one0 = swap_rest(line_one0)
    plane_two = add_up([chip_two[0], *from_plane_rs], cut(chip_two[0], 2), after=[inner_grad])
    line_one6 = join([line_one0, swap(line_one0, z=2)], after=[done_own])
    near_two = add_up([plane_two[0], swap(plane_two[1], z=1)], cut(plane_two[0], 2), after=[])
    line_one7 = join([line_one6, swap(line_one6, z=1)], after=[near_two[0]])
    from_plane = swap_plane([line_one7] * 4)
    (line_two0,) = add_up([near_two[0], swap(near_two[1], z=2)], cut(near_two[0], 1), after=[line_one6])
    line_two0 = swap_rest(line_two0)
    line_two8 = join([line_two0, swap(line_two0, z=2)], after=[])
    line_two9 = join([line_two8, swap(line_two8, z=1)], after=[other_grad])
    from_plane_two = swap_plane([line_two9] * 4)
    line_two = line_two9
    whole_one = join([line_one7, *from_plane], after=[line_two9])
    grad_tokens, done_finish = call(
        "finish",
        finish_kernel,
        [shape(rows, own_len, width, kind=F32)],
        tokens,
        own_grad,
        inner_grad,
        other_grad,
        mid_grad,
        out_grad,
        gain_one,
        flops=1e8,
        after=[whole_one],
        token=True,
    )

    def placed(parts, gain, *weights):
        outs = [shape(*w.shape, kind=F32) for w in weights] + [shape(1, width, kind=F32)]
        return call("place", place_kernel, outs, *parts, weights[0], gain, flops=1e6, token=True)

    grad_up, grad_out, grad_down, grad_gain_two, done_one = placed(
        (whole_one, swap(whole_one, core=1)), gain_two, feedforward_in, attention_out, feedforward_out
    )
    whole_two = join([line_two, *from_plane_two], after=[done_one, done_finish])
    grad_in, grad_gain_one, _ = placed((whole_two, swap(whole_two, core=1)), gain_one, attention_in)
    return activations, grad_tokens, grad_in, grad_out, grad_up, grad_down, grad_gain_one[0], grad_gain_two[0]


def solution(mesh):
    token, rest = P("dp", "seq", None), P()
    return jax.shard_map(
        shards,
        mesh=mesh,
        in_specs=(token, P("dp", None)) + (rest,) * 6 + (token,),
        out_specs=(token, token) + (rest,) * 6,
        check_vma=False,
    )
```
